32 devices in a mesh: dp: 16 (over z, y, core), section: 2 (over x).
Axes of the slice: x: 2, y: 2, z: 4, core: 2. Of those that a mesh axis runs over, the one named last changes fastest.
Arguments:
- inputs: bfloat16 [32, 512, 1024], P('dp', None, 'section'), may hold values from -6 to 6
- cotangent: bfloat16 [32, 512, 1024], P('dp', None, 'section'), may hold values from -6 to 6
- memory: bfloat16 [2, 32, 512, 1024], P('section', 'dp'), may hold values from -6 to 6
- compressed: bfloat16 [2, 32, 512, 1024], P('section', 'dp'), may hold values from -6 to 6
- reset_flags: int32 [32], P('dp'), may hold values 0 or 1
- boundary: int32 [32], P('dp'), may hold values from 1 to 512
- gain_attn: bfloat16 [2, 1024], P('section'), may hold values from 0.5 to 1.5
- projection_weight: bfloat16 [2, 1024, 3072], P('section'), may hold values from -0.1875 to 0.1875
- w_output: bfloat16 [2, 1024, 1024], P('section'), may hold values from -1 to 1
- gain_ffn: bfloat16 [2, 1024], P('section'), may hold values from 0.5 to 1.5
- w_up: bfloat16 [2, 1024, 4096], P('section'), may hold values from -0.1875 to 0.1875
- b_up: bfloat16 [2, 4096], P('section'), may hold values from -3 to 3
- w_down: bfloat16 [2, 4096, 1024], P('section'), may hold values from -0.09375 to 0.09375
- b_down: bfloat16 [2, 1024], P('section'), may hold values from -2 to 2
- w_compress: bfloat16 [2, 2, 1024, 1024], P('section'), may hold values from -0.125 to 0.125
- b_compress: bfloat16 [2, 1024], P('section'), may hold values from -2 to 2
Outputs:
- outputs: bfloat16 [32, 512, 1024], P('dp', None, 'section')
- grad_inputs: bfloat16 [32, 512, 1024], P('dp', None, 'section')
- new_memory: bfloat16 [2, 32, 512, 1024], P('section', 'dp')
- new_compressed: bfloat16 [2, 32, 512, 1024], P('section', 'dp')
- grad_gain_attn: float32 [2, 1024], P('section', 'dp')
- grad_w_project: float32 [2, 1024, 3072], P('section', 'dp')
- grad_w_output: float32 [2, 1024, 1024], P('section', 'dp')
- grad_gain_ffn: float32 [2, 1024], P('section', 'dp')
- grad_w_up: float32 [2, 1024, 4096], P('section', 'dp')
- grad_b_up: float32 [2, 4096], P('section', 'dp')
- grad_w_down: float32 [2, 4096, 1024], P('section', 'dp')
- grad_b_down: float32 [2, 1024], P('section', 'dp')
The draws below stay inside these ranges and needn't reach their ends.
All inputs are finite; a program needn't handle non-finite values. No bound on the sum of `reset_flags` on one device may be relied on, other than what follows from the above.
Results may differ from the reference program's by a relative error of at most 0.024.
Values may be sent and summed in bfloat16 or wider, within the bound.
No kernel may reach another device: no remote copies, remote signals or barrier semaphores. Data moves between devices by JAX's collectives and lax.ppermute only.
A program may use at most 448 MiB of HBM per device.

```python
import jax
import jax.numpy as jnp
from jax import lax

MODEL_WIDTH = 1024
HEADS = 8
HEAD = 128
FF = 4096
SEG = 512
MEM = 512
CMEM = 512
RATE = 2
COMP = 256
SEQS = 32
LAYERS = 2


def touch_ends(result, rng, least, top_value):
    longest = result.shape.index(max(result.shape))
    spots = []
    for shift in (0, 1):
        where = [jax.random.randint(jax.random.fold_in(rng, axis), (), 0, length) for axis, length in enumerate(result.shape)]
        where[longest] = (where[longest] + shift) % result.shape[longest]
        spots.append(tuple(where))
    return result.at[spots[0]].set(least).at[spots[1]].set(top_value)


def shard_levels(stream_key, dims, shards, smallest, high):
    def one(position, parts):
        heights = jax.random.uniform(jax.random.fold_in(jax.random.fold_in(stream_key, 6), position), (parts,), jnp.float32, smallest / len(shards), high / len(shards))
        return jnp.repeat(jnp.exp(heights), dims[position] // parts).reshape((-1,) + (1,) * (len(dims) - position - 1))

    gain = one(*shards[0])
    for cut in shards[1:]:
        gain = gain * one(*cut)
    return gain


def noise(rng, extent, scale, most, shards=(), dtype=jnp.bfloat16):
    values = scale * jax.random.normal(rng, extent, jnp.float32)
    if shards:
        values = values * shard_levels(rng, extent, shards, -0.22, 0.18)
    return jnp.clip(values, -most, most).astype(dtype)


def setup_inputs(seed: int = 0) -> dict:
    seeds = jax.random.split(jax.random.key(seed), 17)
    inputs = noise(seeds[0], (SEQS, SEG, MODEL_WIDTH), 1.0, 6.0, ((0, 16), (2, 2)))
    cotangent = noise(seeds[1], (SEQS, SEG, MODEL_WIDTH), 1.0, 6.0, ((0, 16), (2, 2)))
    memory = noise(seeds[2], (LAYERS, SEQS, MEM, MODEL_WIDTH), 1.0, 6.0, ((0, 2), (1, 16)))
    compressed = noise(seeds[3], (LAYERS, SEQS, CMEM, MODEL_WIDTH), 1.0, 6.0, ((0, 2), (1, 16)))
    reset_flags = touch_ends((jax.random.randint(seeds[4], (SEQS,), 0, 4) < 1).astype(jnp.int32), jax.random.fold_in(seeds[4], 1), 0, 1)
    boundary = touch_ends(jax.random.randint(seeds[5], (SEQS,), 1, SEG + 1), jax.random.fold_in(seeds[5], 1), 1, SEG).astype(jnp.int32)
    gain_attn = jnp.clip(1.0 + 0.1 * jax.random.normal(seeds[6], (LAYERS, MODEL_WIDTH), jnp.float32), 0.5, 1.5).astype(jnp.bfloat16)
    projection_weight = noise(seeds[7], (LAYERS, MODEL_WIDTH, 3 * MODEL_WIDTH), MODEL_WIDTH ** -0.5, 0.1875, ((0, 2),))
    w_output = noise(seeds[8], (LAYERS, MODEL_WIDTH, MODEL_WIDTH), (MODEL_WIDTH // 32) ** -0.5, 1.0, ((0, 2),))
    gain_ffn = jnp.clip(1.0 + 0.1 * jax.random.normal(seeds[9], (LAYERS, MODEL_WIDTH), jnp.float32), 0.5, 1.5).astype(jnp.bfloat16)
    w_up = noise(seeds[10], (LAYERS, MODEL_WIDTH, FF), MODEL_WIDTH ** -0.5, 0.1875, ((0, 2),))
    b_up = noise(seeds[11], (LAYERS, FF), 0.5, 3.0, ((0, 2),))
    w_down = noise(seeds[12], (LAYERS, FF, MODEL_WIDTH), FF ** -0.5, 0.09375, ((0, 2),))
    b_down = noise(seeds[13], (LAYERS, MODEL_WIDTH), 0.3, 2.0, ((0, 2),))
    w_compress = noise(seeds[14], (LAYERS, RATE, MODEL_WIDTH, MODEL_WIDTH), (RATE * MODEL_WIDTH) ** -0.5, 0.125, ((0, 2),))
    b_compress = noise(seeds[15], (LAYERS, MODEL_WIDTH), 0.3, 2.0, ((0, 2),))
    return {"inputs": inputs, "cotangent": cotangent, "memory": memory, "compressed": compressed, "reset_flags": reset_flags, "boundary": boundary, "gain_attn": gain_attn, "projection_weight": projection_weight, "w_output": w_output, "gain_ffn": gain_ffn, "w_up": w_up, "b_up": b_up, "w_down": w_down, "b_down": b_down, "w_compress": w_compress, "b_compress": b_compress}


EPS = 1e-05
NEG = -1e+30
ROOT_TWO_PI = 0.7978845608028654

@jax.custom_vjp
def low(v):
    return lax.optimization_barrier(v.astype(jnp.bfloat16)).astype(jnp.float32)

@jax.custom_vjp
def low_back(v):
    return v

def low_keep(v):
    return (low(v), None)

def low_pass(kept, grad):
    return (grad,)

def back_keep(v):
    return (v, None)

def back_low(kept, grad):
    return (low(grad),)
low.defvjp(low_keep, low_pass)
low_back.defvjp(back_keep, back_low)

def layer_norm(values, scale_gain):
    centred = values - lax.optimization_barrier(jnp.mean(values, axis=-1, keepdims=True))
    spread = lax.optimization_barrier(jnp.mean(centred * centred, axis=-1, keepdims=True))
    return centred * lax.rsqrt(spread + EPS) * scale_gain

def gaussian_unit(values):
    return 0.5 * values * (1.0 + jnp.tanh(ROOT_TWO_PI * (values + 0.044715 * values * values * values)))

def exact_dot(factor, weights):
    return jnp.dot(factor, weights, precision=lax.Precision.HIGHEST)

def visible_keys(flag, bound):
    query_pos = lax.broadcasted_iota(jnp.int32, (SEG, 1), 0)
    key_pos = lax.broadcasted_iota(jnp.int32, (1, SEG), 1)
    after_bound = query_pos >= bound
    segment_keys = (key_pos <= query_pos) & ((key_pos >= bound) == after_bound)
    memory_keys = jnp.broadcast_to((flag == 0) & (query_pos < bound), (SEG, CMEM + MEM))
    return jnp.concatenate([memory_keys, segment_keys], axis=1)

def layer(inputs, memory_rows, condensed_rows, flag, bound, params):
    gain_attn, projection_weight, w_output, gain_ffn, w_up, b_up, w_down, b_down = params
    keep_rate = (1 - flag).astype(jnp.float32)
    context = jnp.concatenate([condensed_rows * keep_rate, memory_rows * keep_rate, inputs], axis=0)
    key_span = CMEM + MEM + SEG
    normalized_rows = low(layer_norm(context, gain_attn))
    queries = low(low_back(exact_dot(normalized_rows[CMEM + MEM:], projection_weight[:, :MODEL_WIDTH])))
    keyvals = low(low_back(exact_dot(normalized_rows, projection_weight[:, MODEL_WIDTH:])))
    head_queries = queries.reshape(SEG, HEADS, HEAD)
    key_rows = keyvals[:, :MODEL_WIDTH].reshape(key_span, HEADS, HEAD)
    value_rows = keyvals[:, MODEL_WIDTH:].reshape(key_span, HEADS, HEAD)
    attention_logits = low_back(jnp.einsum('qhd,khd->hqk', head_queries, key_rows, precision=lax.Precision.HIGHEST) * HEAD ** (-0.5))
    attention_logits = jnp.where(visible_keys(flag, bound)[None], attention_logits, NEG)
    exponent = jnp.exp(attention_logits - lax.optimization_barrier(jnp.max(attention_logits, axis=-1, keepdims=True)))
    attention = low(exponent / lax.optimization_barrier(jnp.sum(exponent, axis=-1, keepdims=True)))
    attended = jnp.einsum('hqk,khd->qhd', attention, value_rows, precision=lax.Precision.HIGHEST).reshape(SEG, MODEL_WIDTH)
    attended = low(low_back(attended))
    residual = inputs + low_back(exact_dot(attended, w_output))
    hidden_in = low_back(exact_dot(low(layer_norm(residual, gain_ffn)), w_up) + b_up)
    hidden = low(gaussian_unit(hidden_in))
    return residual + low_back(exact_dot(hidden, w_down) + b_down)

def reference(inputs, cotangent, memory, compressed, reset_flags, boundary, gain_attn, projection_weight, w_output, gain_ffn, w_up, b_up, w_down, b_down, w_compress, b_compress):
    params = tuple((member.astype(jnp.float32) for member in (gain_attn, projection_weight, w_output, gain_ffn, w_up, b_up, w_down, b_down)))
    memory_seqs = jnp.swapaxes(memory, 0, 1).astype(jnp.float32)
    compressed_seqs = jnp.swapaxes(compressed, 0, 1).astype(jnp.float32)
    memory_all = memory.astype(jnp.float32)
    conv_weights = w_compress.astype(jnp.float32)
    conv_bias = b_compress.astype(jnp.float32)
    keep_float = (1 - reset_flags).astype(jnp.float32)[:, None, None]

    def forward(seq_inputs, weights):

        def one_sequence(pieces):
            row_in, memory_rows, condensed_rows, flag, bound = pieces
            hidden_rows = row_in
            layer_inputs = []
            for layer_index in range(LAYERS):
                layer_inputs.append(hidden_rows)
                output = layer(hidden_rows, memory_rows[layer_index], condensed_rows[layer_index], flag, bound, tuple((member[layer_index] for member in weights)))
                if layer_index + 1 < LAYERS:
                    output = low(low_back(output))
                hidden_rows = output
            return (hidden_rows, jnp.stack(layer_inputs))
        final, retained_inputs = lax.map(jax.checkpoint(one_sequence), (seq_inputs, memory_seqs, compressed_seqs, reset_flags, boundary))
        squeezed_list = []
        for layer_index in range(LAYERS):
            evicted = memory_all[layer_index] * keep_float
            padded = jnp.pad(evicted, ((0, 0), (0, COMP * RATE - MEM), (0, 0)))
            grouped = padded.reshape(SEQS * COMP, RATE * MODEL_WIDTH)
            squeezed = exact_dot(grouped, conv_weights[layer_index].reshape(RATE * MODEL_WIDTH, MODEL_WIDTH)) + conv_bias[layer_index]
            squeezed_list.append(squeezed.reshape(SEQS, COMP, MODEL_WIDTH))
        return (final, (retained_inputs, jnp.stack(squeezed_list)))
    final_rows, pullback, extras = jax.vjp(forward, inputs.astype(jnp.float32), params, has_aux=True)
    layer_inputs, squeezed_all = extras
    grad_rows, grad_params = pullback(cotangent.astype(jnp.float32))
    new_memory = jnp.swapaxes(layer_inputs, 0, 1).astype(jnp.bfloat16)
    keep_all = (1 - reset_flags).astype(jnp.bfloat16)[:, None, None]
    joined_list = []
    for layer_index in range(LAYERS):
        joined = jnp.concatenate([compressed[layer_index] * keep_all, squeezed_all[layer_index].astype(jnp.bfloat16)], axis=1)
        joined_list.append(joined[:, COMP:])
    new_compressed = jnp.stack(joined_list)
    return (final_rows.astype(jnp.bfloat16), grad_rows.astype(jnp.bfloat16), new_memory, new_compressed, grad_params[0], grad_params[1], grad_params[2], grad_params[3], grad_params[4], grad_params[5], grad_params[6], grad_params[7])
```

```python
import math

import jax
import jax.numpy as jnp
from jax import lax
from jax.experimental import pallas as pl
from jax.experimental.pallas import tpu as pltpu
from jax.sharding import PartitionSpec as P

WIDTH = 1024
HEADS = 8
HEAD = 128
FF = 4096
SEG = 512
MEM = 512
CMEM = 512
RATE = 2
COMP = 256
CTX = MEM + CMEM
HALF = SEG // 2
HP = 4

EPS = 1e-05
NEG = -1e30
ROOT_TWO_PI = 0.7978845608028654
SCALE = HEAD**-0.5
LOG2E = math.log2(math.e)
LN2 = math.log(2.0)
BF = jnp.bfloat16
F32 = jnp.float32
PARAMS = pltpu.CompilerParams(vmem_limit_bytes=56 << 20)


def nn(a, b):
    return lax.dot_general(a, b, (((1,), (0,)), ((), ())), preferred_element_type=F32)


def nt(a, b):
    return lax.dot_general(a, b, (((1,), (1,)), ((), ())), preferred_element_type=F32)


def tn(a, b):
    return lax.dot_general(a, b, (((0,), (0,)), ((), ())), preferred_element_type=F32)


def shape(dims, dtype=BF):
    return jax.ShapeDtypeStruct(dims, dtype)


def whole(*dims):
    return pl.BlockSpec(dims, lambda *_: (0,) * len(dims))


def cost(flops, moved, trans=0):
    return pl.CostEstimate(flops=int(flops), bytes_accessed=int(moved), transcendentals=int(trans))


def normalise(values):
    centred = values - jnp.mean(values, axis=-1, keepdims=True)
    inverse = lax.rsqrt(jnp.mean(centred * centred, axis=-1, keepdims=True) + EPS)
    return centred * inverse, inverse


def norm_back(unit, inverse, gain, grad):
    scaled = grad * gain
    along = jnp.mean(scaled * unit, axis=-1, keepdims=True)
    return inverse * (scaled - jnp.mean(scaled, axis=-1, keepdims=True) - unit * along)


def memory_kernel(flags, comp, mem, gain, wk, wv, normed, kv):
    seq, source = pl.program_id(0), pl.program_id(1)
    keep = (1 - flags[seq]).astype(F32)
    rows = jnp.where(source == 0, comp[0].astype(F32), mem[0].astype(F32)) * keep
    unit, _ = normalise(rows)
    rounded = (unit * gain[...].astype(F32)).astype(BF)
    normed[0] = rounded
    kv[0, :, :WIDTH] = nn(rounded, wk[...]).astype(BF)
    kv[0, :, WIDTH:] = nn(rounded, wv[...]).astype(BF)


def memory_keyvals(flags, compressed, memory, gain, w_proj):
    seqs = memory.shape[0]
    rows = pl.BlockSpec((1, MEM, WIDTH), lambda s, j, *_: (s, 0, 0))
    return pl.pallas_call(
        memory_kernel,
        name="memory_keyvals",
        grid_spec=pltpu.PrefetchScalarGridSpec(
            num_scalar_prefetch=1,
            grid=(seqs, 2),
            in_specs=[
                rows,
                rows,
                whole(1, WIDTH),
                pl.BlockSpec((WIDTH, WIDTH), lambda *_: (0, 1)),
                pl.BlockSpec((WIDTH, WIDTH), lambda *_: (0, 2)),
            ],
            out_specs=[
                pl.BlockSpec((1, MEM, WIDTH), lambda s, j, *_: (s, j, 0)),
                pl.BlockSpec((1, MEM, 2 * WIDTH), lambda s, j, *_: (s, j, 0)),
            ],
        ),
        out_shape=[shape((seqs, CTX, WIDTH)), shape((seqs, CTX, 2 * WIDTH))],
        compiler_params=PARAMS,
        cost_estimate=cost(seqs * CTX * WIDTH * 2 * WIDTH * 2, 24 << 20),
    )(flags, compressed, memory, gain, w_proj, w_proj)


def project_kernel(x, gain, w, normed, qkv):
    tile = pl.program_id(0)

    @pl.when(tile == 0)
    def _():
        unit, _ = normalise(x[...].astype(F32))
        normed[...] = (unit * gain[...].astype(F32)).astype(BF)

    factor = jnp.where(tile == 0, SCALE * LOG2E, 1.0)
    qkv[...] = (nn(normed[...], w[...]) * factor).astype(BF)


def project(x, gain, w_proj):
    return pl.pallas_call(
        project_kernel,
        name="project",
        grid=(3,),
        in_specs=[whole(SEG, WIDTH), whole(1, WIDTH), pl.BlockSpec((WIDTH, WIDTH), lambda t: (0, t))],
        out_specs=[whole(SEG, WIDTH), pl.BlockSpec((SEG, WIDTH), lambda t: (0, t))],
        out_shape=[shape((SEG, WIDTH)), shape((SEG, 3 * WIDTH))],
        compiler_params=PARAMS,
        cost_estimate=cost(SEG * WIDTH * 3 * WIDTH * 2, 11 << 20),
    )(x, gain, w_proj)


def fill_masks(info, bias, unseen):
    key = lax.broadcasted_iota(jnp.int32, (SEG, SEG), 0)
    query = lax.broadcasted_iota(jnp.int32, (SEG, SEG), 1)
    least = jnp.where(query >= info[1], info[1], 0)
    bias[...] = jnp.where((key <= query) & (key >= least), 0.0, NEG)
    position = lax.broadcasted_iota(jnp.int32, (1, SEG), 1)
    limit = jnp.where(info[0] == 0, info[1], 0)
    unseen[...] = jnp.where(position < limit, 0.0, -NEG)


def attend_kernel(info, q, kx, vx, km, vm, attended, log_total, bias, unseen):
    @pl.when(pl.program_id(0) == 0)
    def _():
        fill_masks(info, bias, unseen)

    pieces = [
        (h, slice(h * HEAD, (h + 1) * HEAD), slice(part * HALF, (part + 1) * HALF), (part + 1) * HALF)
        for h in range(HP)
        for part in range(2)
    ]

    def scores(h, c, r, count):
        rows = q[r, c]
        return nt(km[:, c], rows), nt(kx[:count, c], rows) + bias[:count, r]

    def weights(h, c, r, count, on_memory, on_segment):
        hidden = unseen[:, r]
        top = jnp.maximum(
            jnp.max(on_memory, axis=0, keepdims=True) - hidden,
            jnp.max(on_segment, axis=0, keepdims=True),
        )
        p_memory = jnp.exp2(on_memory - (top + hidden))
        p_segment = jnp.exp2(on_segment - top)
        total = jnp.sum(p_memory, axis=0, keepdims=True) + jnp.sum(p_segment, axis=0, keepdims=True)
        log_total[h, :, r] = top + jnp.log2(total)
        return p_memory.astype(BF), p_segment.astype(BF), total

    def finish(h, c, r, count, p_memory, p_segment, total):
        turned = nn(vm[:, c].T, p_memory) + nn(vx[:count, c].T, p_segment)
        attended[r, c] = (turned * (1.0 / total)).T.astype(BF)

    held, ready = {}, {}
    for step in range(len(pieces) + 2):
        if step < len(pieces):
            held[step] = scores(*pieces[step])
        if 0 <= step - 1 < len(pieces):
            ready[step - 1] = weights(*pieces[step - 1], *held.pop(step - 1))
        if 0 <= step - 2 < len(pieces):
            finish(*pieces[step - 2], *ready.pop(step - 2))


def head_specs(seq):
    wide = HP * HEAD
    count = WIDTH // wide
    segment = [pl.BlockSpec((SEG, wide), lambda h, *_, o=o: (0, o * count + h)) for o in range(3)]
    memory = [
        pl.BlockSpec((None, CTX, wide), lambda h, *_, o=o: (seq, 0, o * count + h)) for o in range(2)
    ]
    stat = pl.BlockSpec((HP, 1, SEG), lambda h, *_: (h, 0, 0))
    scratch = [pltpu.VMEM((SEG, SEG), F32), pltpu.VMEM((1, SEG), F32)]
    return count, segment, memory, stat, scratch


def attend(info, qkv, kv_memory, seq):
    count, segment, memory, stat, scratch = head_specs(seq)
    return pl.pallas_call(
        attend_kernel,
        name="attend",
        grid_spec=pltpu.PrefetchScalarGridSpec(
            num_scalar_prefetch=1,
            grid=(count,),
            in_specs=segment + memory,
            out_specs=[segment[0], stat],
            scratch_shapes=scratch,
        ),
        out_shape=[shape((SEG, WIDTH)), shape((HEADS, 1, SEG), F32)],
        compiler_params=PARAMS,
        cost_estimate=cost(12e9, 10 << 20),
    )(info, qkv, qkv, qkv, kv_memory, kv_memory)


FT = 1024
FS = 512


def gelu_parts(v):
    square = v * v
    t = jnp.tanh(ROOT_TWO_PI * v * (1.0 + 0.044715 * square))
    half = 0.5 + 0.5 * t
    slope = ROOT_TWO_PI * (1.0 + 3 * 0.044715 * square)
    return v * half, half * (1.0 + v * (1.0 - t) * slope)


def feed_kernel(
    attended, x, w_out, gain, w_up, b_up, w_down, b_down, y, residual, ffn_in, hidden, gate, total
):
    step = pl.program_id(0)

    @pl.when(step == 0)
    def _():
        rows = x[...].astype(F32) + nn(attended[...], w_out[...])
        residual[...] = rows
        unit, _ = normalise(rows)
        ffn_in[...] = (unit * gain[...].astype(F32)).astype(BF)
        total[...] = rows + b_down[...].astype(F32)

    cuts = [slice(i * FS, (i + 1) * FS) for i in range(FT // FS)]
    ups = [nn(ffn_in[...], w_up[:, c]) + b_up[:, c].astype(F32) for c in cuts]
    added = None
    for c, up in zip(cuts, ups):
        value, slope = gelu_parts(up)
        value = value.astype(BF)
        hidden[:, c] = value
        gate[:, c] = slope.astype(BF)
        part = nn(value, w_down[c, :])
        added = part if added is None else added + part
    total[...] += added

    @pl.when(step == pl.num_programs(0) - 1)
    def _():
        y[...] = total[...].astype(BF)


def feed(attended, x, w_out, gain, w_up, b_up, w_down, b_down):
    steps = FF // FT
    wide = pl.BlockSpec((SEG, FT), lambda t: (0, t))
    return pl.pallas_call(
        feed_kernel,
        name="feed",
        grid=(steps,),
        in_specs=[
            whole(SEG, WIDTH),
            whole(SEG, WIDTH),
            whole(WIDTH, WIDTH),
            whole(1, WIDTH),
            pl.BlockSpec((WIDTH, FT), lambda t: (0, t)),
            pl.BlockSpec((1, FT), lambda t: (0, t)),
            pl.BlockSpec((FT, WIDTH), lambda t: (t, 0)),
            whole(1, WIDTH),
        ],
        out_specs=[whole(SEG, WIDTH), whole(SEG, WIDTH), whole(SEG, WIDTH), wide, wide],
        out_shape=[
            shape((SEG, WIDTH)),
            shape((SEG, WIDTH), F32),
            shape((SEG, WIDTH)),
            shape((SEG, FF)),
            shape((SEG, FF)),
        ],
        scratch_shapes=[pltpu.VMEM((SEG, WIDTH), F32)],
        compiler_params=PARAMS,
        cost_estimate=cost(SEG * WIDTH * (2 * FF + WIDTH) * 2, 32 << 20),
    )(attended, x, w_out, gain, w_up, b_up, w_down, b_down)


def feed_back_kernel(
    gy, w_down, gate, w_up, residual, gain, w_out, d_hidden, d_residual, low, d_attended, d_up, d_down, total
):
    step = pl.program_id(0)

    @pl.when(step == 0)
    def _():
        d_down[...] = jnp.sum(gy[...].astype(F32), axis=0, keepdims=True)

    cuts = [slice(i * FS, (i + 1) * FS) for i in range(FT // FS)]
    raws = [nt(gy[...], w_down[c, :]) for c in cuts]
    added = None
    for c, raw in zip(cuts, raws):
        value = (raw * gate[:, c].astype(F32)).astype(BF)
        d_hidden[:, c] = value
        d_up[:, c] = jnp.sum(value.astype(F32), axis=0, keepdims=True)
        part = nt(value, w_up[:, c])
        added = part if added is None else added + part

    @pl.when(step == 0)
    def _():
        total[...] = added

    @pl.when(step > 0)
    def _():
        total[...] += added

    @pl.when(step == pl.num_programs(0) - 1)
    def _():
        unit, inverse = normalise(residual[...])
        grad = gy[...].astype(F32) + norm_back(unit, inverse, gain[...].astype(F32), total[...])
        d_residual[...] = grad
        low[...] = grad.astype(BF)
        d_attended[...] = nt(low[...], w_out[...]).astype(BF)


def feed_back(gy, w_down, gate, w_up, residual, gain, w_out):
    steps = FF // FT
    wide = pl.BlockSpec((SEG, FT), lambda t: (0, t))
    return pl.pallas_call(
        feed_back_kernel,
        name="feed_back",
        grid=(steps,),
        in_specs=[
            whole(SEG, WIDTH),
            pl.BlockSpec((FT, WIDTH), lambda t: (t, 0)),
            wide,
            pl.BlockSpec((WIDTH, FT), lambda t: (0, t)),
            whole(SEG, WIDTH),
            whole(1, WIDTH),
            whole(WIDTH, WIDTH),
        ],
        out_specs=[
            wide,
            whole(SEG, WIDTH),
            whole(SEG, WIDTH),
            whole(SEG, WIDTH),
            pl.BlockSpec((1, FT), lambda t: (0, t)),
            whole(1, WIDTH),
        ],
        out_shape=[
            shape((SEG, FF)),
            shape((SEG, WIDTH), F32),
            shape((SEG, WIDTH)),
            shape((SEG, WIDTH)),
            shape((1, FF), F32),
            shape((1, WIDTH), F32),
        ],
        scratch_shapes=[pltpu.VMEM((SEG, WIDTH), F32)],
        compiler_params=PARAMS,
        cost_estimate=cost(SEG * WIDTH * (2 * FF + WIDTH) * 2, 32 << 20),
    )(gy, w_down, gate, w_up, residual, gain, w_out)


def attend_back_kernel(
    info, q, kx, vx, km, vm, d_out, out, log_total, dq, dkx, dvx, dkm, dvm, bias, unseen
):
    @pl.when(pl.program_id(0) == 0)
    def _():
        fill_masks(info, bias, unseen)

    every, low, high = slice(0, SEG), slice(0, HALF), slice(HALF, SEG)
    for h in range(d_out.shape[1] // HEAD):
        c = slice(h * HEAD, (h + 1) * HEAD)
        qh, gh = q[:, c], d_out[:, c]
        inner = jnp.sum((gh.astype(F32) * out[:, c].astype(F32)).T, axis=0, keepdims=True)
        level = log_total[h]

        def piece(k, v, r, mask):
            logits = nt(k, qh[r])
            if mask is None:
                p = jnp.exp2(logits - (level[:, r] + unseen[:, r]))
            else:
                p = jnp.exp2(logits + mask - level[:, r])
            ds = (p * (nt(v, gh[r]) - inner[:, r])).astype(BF)
            return p.astype(BF), ds

        p_memory, ds_memory = piece(km[:, c], vm[:, c], every, None)
        p_low, ds_low = piece(kx[low, c], vx[low, c], every, bias[low, :])
        p_high, ds_high = piece(kx[high, c], vx[high, c], high, bias[high, high])
        dvm[:, c] = nn(p_memory, gh).astype(BF)
        dkm[:, c] = (nn(ds_memory, qh) * LN2).astype(BF)
        dvx[low, c] = nn(p_low, gh).astype(BF)
        dkx[low, c] = (nn(ds_low, qh) * LN2).astype(BF)
        dvx[high, c] = nn(p_high, gh[high]).astype(BF)
        dkx[high, c] = (nn(ds_high, qh[high]) * LN2).astype(BF)
        turned = kx[:, c].T
        first = nn(km[:, c].T, ds_memory) + nn(turned[:, low], ds_low)
        dq[low, c] = (first[:, low] * SCALE).T.astype(BF)
        dq[high, c] = ((first[:, high] + nn(turned[:, high], ds_high)) * SCALE).T.astype(BF)


def attend_back(info, qkv, kv_memory, seq, d_out, out, log_total):
    count, segment, memory, stat, scratch = head_specs(seq)
    plain = segment[0]
    rows = pl.BlockSpec((CTX, HP * HEAD), lambda h, *_: (0, h))
    return pl.pallas_call(
        attend_back_kernel,
        name="attend_back",
        grid_spec=pltpu.PrefetchScalarGridSpec(
            num_scalar_prefetch=1,
            grid=(count,),
            in_specs=segment + memory + [plain, plain, stat],
            out_specs=[plain, plain, plain, rows, rows],
            scratch_shapes=scratch,
        ),
        out_shape=[shape((SEG, WIDTH))] * 3 + [shape((CTX, WIDTH))] * 2,
        compiler_params=PARAMS,
        cost_estimate=cost(18e9, 20 << 20),
    )(info, qkv, qkv, qkv, kv_memory, kv_memory, d_out, out, log_total)


def project_back_kernel(dq, dk, dv, w, x, gain, d_residual, dx, total):
    step = pl.program_id(0)

    @pl.when(step == 0)
    def _():
        total[...] = nt(dq[...], w[...])

    @pl.when(step == 1)
    def _():
        total[...] += nt(dk[...], w[...])

    @pl.when(step == 2)
    def _():
        grad = total[...] + nt(dv[...], w[...])
        unit, inverse = normalise(x[...].astype(F32))
        dx[...] = (d_residual[...] + norm_back(unit, inverse, gain[...].astype(F32), grad)).astype(BF)


def project_back(dq, dk, dv, w_proj, x, gain, d_residual):
    full = whole(SEG, WIDTH)
    return pl.pallas_call(
        project_back_kernel,
        name="project_back",
        grid=(3,),
        in_specs=[
            full,
            full,
            full,
            pl.BlockSpec((WIDTH, WIDTH), lambda t: (0, t)),
            full,
            whole(1, WIDTH),
            full,
        ],
        out_specs=full,
        out_shape=shape((SEG, WIDTH)),
        scratch_shapes=[pltpu.VMEM((SEG, WIDTH), F32)],
        compiler_params=PARAMS,
        cost_estimate=cost(SEG * WIDTH * 3 * WIDTH * 2, 14 << 20),
    )(dq, dk, dv, w_proj, x, gain, d_residual)


def compress_kernel(flags, grouped, w, bias, out):
    keep = (1 - flags[pl.program_id(0)]).astype(BF)
    out[0] = (nn(grouped[0] * keep, w[...]) + bias[...].astype(F32)).astype(BF)


def compress(flags, memory, w_compress, b_compress):
    seqs = memory.shape[0]
    wide = RATE * WIDTH
    grouped = memory.reshape(seqs, COMP, wide)
    return pl.pallas_call(
        compress_kernel,
        name="compress",
        grid_spec=pltpu.PrefetchScalarGridSpec(
            num_scalar_prefetch=1,
            grid=(seqs,),
            in_specs=[
                pl.BlockSpec((1, COMP, wide), lambda s, *_: (s, 0, 0)),
                whole(wide, WIDTH),
                whole(1, WIDTH),
            ],
            out_specs=pl.BlockSpec((1, COMP, WIDTH), lambda s, *_: (s, 0, 0)),
        ),
        out_shape=shape((seqs, COMP, WIDTH)),
        compiler_params=PARAMS,
        cost_estimate=cost(seqs * COMP * wide * WIDTH * 2, 8 << 20),
    )(flags, grouped, w_compress.reshape(wide, WIDTH), b_compress)


def turned_index(value, bits):
    return sum(((value >> b) & 1) << (bits - 1 - b) for b in range(bits))


def weight_kernel(count, rows, extra, mine, *refs):
    parts = (len(refs) - 2 - (1 if extra else 0)) // 2
    lefts, rights = refs[:parts], refs[parts : 2 * parts]
    send, keep = refs[-2:]
    value = None
    for left, right in zip(lefts, rights):
        term = tn(left[...], right[...])
        value = term if value is None else value + term
    value = value.astype(BF)
    even = mine[0] == 0
    bits = (count - 1).bit_length()
    for pair in range(count // 2):
        place = turned_index(pair, bits - 1)
        one = value[(2 * pair) * rows : (2 * pair + 1) * rows]
        two = value[(2 * pair + 1) * rows : (2 * pair + 2) * rows]
        send[place, 0, :rows] = jnp.where(even, two, one)
        keep[place, 0, :rows] = jnp.where(even, one, two)
    if extra:
        small = refs[2 * parts]
        for pair in range(count // 2):
            place = turned_index(pair, bits - 1)
            send[place, 0, rows:] = jnp.where(even, small[2 * pair + 1], small[2 * pair])
            keep[place, 0, rows:] = jnp.where(even, small[2 * pair], small[2 * pair + 1])


def weight_grad(mine, size, lefts, rights, columns, tile, small=None):
    height = lefts[0][0].shape[-1]
    tall = min(height, 1024)
    blocks = height // tall
    count = size // blocks
    rows = tall // count
    order = (blocks - 1).bit_length()

    def spec(array, lead, width, first, along):
        def place(i, j, *_):
            col = first + (i if along == 0 else j)
            return (0, col) if lead is None else (lead, 0, col)

        depth = array.shape[-2]
        return pl.BlockSpec((depth, width) if lead is None else (None, depth, width), place)

    def out_place(i, j, *_):
        return (0, sum(((i // (1 << b)) % 2) * (1 << (order - 1 - b)) for b in range(order)), 0, j)

    total = rows + (0 if small is None else small.shape[1])
    block = pl.BlockSpec((count // 2, 1, total, tile), out_place)
    out = shape((count // 2, blocks, total, columns))
    specs = [spec(a, lead, tall, 0, 0) for a, lead in lefts]
    specs += [spec(a, lead, tile, first, 1) for a, lead, first in rights]
    args = [a for a, _ in lefts] + [a for a, _, _ in rights]
    if small is not None:
        specs.append(pl.BlockSpec(small.shape[:2] + (tile,), lambda i, j, *_: (0, 0, j)))
        args.append(small)
    depth = sum(a.shape[-2] for a, _ in lefts)
    send, keep = pl.pallas_call(
        lambda *refs: weight_kernel(count, rows, small is not None, *refs),
        name="weight_grad",
        grid_spec=pltpu.PrefetchScalarGridSpec(
            num_scalar_prefetch=1,
            grid=(blocks, columns // tile),
            in_specs=specs,
            out_specs=[block, block],
        ),
        out_shape=[out, out],
        compiler_params=PARAMS,
        cost_estimate=cost(2 * depth * height * columns, 2 * (depth * (height + columns) + height * columns)),
    )(mine, *args)
    flat = (size // 2, total, columns)
    return send.reshape(flat), keep.reshape(flat)


def halve_kernel(bit, kept_a, got_a, kept_b, got_b, send, keep):
    send[...] = (kept_a[...].astype(F32) + got_a[...].astype(F32)).astype(BF)
    keep[...] = (kept_b[...].astype(F32) + got_b[...].astype(F32)).astype(BF)


def halve(bit, kept, got):
    count, rows, columns = kept.shape
    half = count // 2
    steps = 2 if columns % 256 == 0 and kept.size >= 1 << 19 else 1
    block = (half, rows, columns // steps)
    other = pl.BlockSpec(block, lambda j, b: (1 - b[0], 0, j))
    own = pl.BlockSpec(block, lambda j, b: (b[0], 0, j))
    plain = pl.BlockSpec(block, lambda j, b: (0, 0, j))
    out = shape((half, rows, columns))
    return pl.pallas_call(
        halve_kernel,
        name="halve",
        grid_spec=pltpu.PrefetchScalarGridSpec(
            num_scalar_prefetch=1,
            grid=(steps,),
            in_specs=[other, other, own, own],
            out_specs=[plain, plain],
        ),
        out_shape=[out, out],
        compiler_params=PARAMS,
        cost_estimate=cost(kept.size, kept.size * 6),
    )(bit, kept, got, kept, got)


def swap_bit(value, size, bit):
    return lax.ppermute(value, "dp", [(i, i ^ (1 << bit)) for i in range(size)])


def reduce_parts(send, keep, size, bits):
    for level in range(len(bits)):
        got = swap_bit(send, size, level)
        if level + 1 < len(bits):
            send, keep = halve(bits[level + 1], keep, got)
    return keep[0].astype(F32) + got[0].astype(F32)


def one_way(value, first, second):
    return lax.ppermute(value, "section", [(first, second)])


def nothing(shapes):
    def kernel(*refs):
        pass

    anywhere = pl.BlockSpec(memory_space=pl.ANY)
    return pl.pallas_call(
        kernel, name="nothing", out_shape=shapes, out_specs=[anywhere] * len(shapes), compiler_params=PARAMS
    )()


def branches(chosen, first, second):
    shapes = jax.eval_shape(first if first is not None else second)
    leaves, tree = jax.tree.flatten(shapes)
    empty = lambda: jax.tree.unflatten(tree, nothing([shape(leaf.shape, leaf.dtype) for leaf in leaves]))
    return lax.cond(chosen, first or empty, second or empty)


def after(value, *others):
    return lax.optimization_barrier((value,) + others)[0]


def body(
    inputs,
    cotangent,
    memory,
    compressed,
    reset_flags,
    boundary,
    gain_attn,
    projection_weight,
    w_output,
    gain_ffn,
    w_up,
    b_up,
    w_down,
    b_down,
    w_compress,
    b_compress,
):
    section = lax.axis_index("section")
    is_first = section == 0
    size = lax.axis_size("dp")
    mine = lax.axis_index("dp")
    levels = (size - 1).bit_length()
    bits = [((mine >> b) & 1).astype(jnp.int32).reshape(1) for b in range(levels)]
    seqs, _, width = inputs.shape
    memory, compressed = memory[0], compressed[0]
    w_proj, w_out, w_up, w_down = projection_weight[0], w_output[0], w_up[0], w_down[0]
    info = [jnp.stack([reset_flags[s], boundary[s]]).astype(jnp.int32) for s in range(seqs)]

    leaving = jnp.where(is_first, cotangent, inputs)
    arriving = [lax.ppermute(leaving[s], "section", [(0, 1), (1, 0)]) for s in range(seqs)]
    first_x = [jnp.concatenate([inputs[s], arriving[s]], axis=1) for s in range(seqs)]
    last_gy = [jnp.concatenate([arriving[s], cotangent[s]], axis=1) for s in range(seqs)]
    normed_memory, kv_memory = memory_keyvals(reset_flags, compressed, memory, gain_attn, w_proj)

    def forward(s, x):
        normed, qkv = project(x, gain_attn, w_proj)
        attended, log_total = attend(info[s], qkv, kv_memory, s)
        y, residual, ffn_in, hidden, gate = feed(
            attended, x, w_out, gain_ffn, w_up, b_up, w_down, b_down
        )
        return dict(
            y=y,
            normed=normed,
            qkv=qkv,
            attended=attended,
            log_total=log_total,
            residual=residual,
            ffn_in=ffn_in,
            hidden=hidden,
            gate=gate,
        )

    def back_ffn(saved, gy):
        names = ("d_hidden", "d_residual", "low", "d_attended", "d_up", "d_down")
        values = feed_back(gy, w_down, saved["gate"], w_up, saved["residual"], gain_ffn, w_out)
        return dict(zip(names, values))

    def back_attend(s, saved, part):
        names = ("dq", "dkx", "dvx", "dkm", "dvm")
        values = attend_back(
            info[s], saved["qkv"], kv_memory, s, part["d_attended"], saved["attended"], saved["log_total"]
        )
        return dict(zip(names, values))

    def back_project(x, part, grads):
        return project_back(
            grads["dq"], grads["dkx"], grads["dvx"], w_proj, x, gain_attn, part["d_residual"]
        )

    def backward(s, x, saved, gy):
        part = back_ffn(saved, gy)
        grads = back_attend(s, saved, part)
        return part, grads, back_project(x, part, grads)

    def squeeze():
        return compress(reset_flags, memory, w_compress[0], b_compress)

    run0 = is_first
    saved_a0, squeezed_second = lax.cond(
        run0,
        lambda: (forward(0, first_x[0]), nothing([shape((seqs, COMP, WIDTH))])[0]),
        lambda: (
            dict(zip(sorted(FORWARD), nothing([FORWARD[k] for k in sorted(FORWARD)]))),
            squeeze(),
        ),
    )
    hop_a = one_way(saved_a0["y"], 0, 1)
    run1 = after(is_first, saved_a0["log_total"])
    saved_b0 = branches(run1, lambda: forward(1, first_x[1]), None)
    hop_b = one_way(saved_b0["y"], 0, 1)
    run2 = after(is_first, saved_b0["log_total"])
    squeezed_first, saved_a1 = lax.cond(
        run2,
        lambda: (
            squeeze(),
            dict(zip(sorted(FORWARD), nothing([FORWARD[k] for k in sorted(FORWARD)]))),
        ),
        lambda: (nothing([shape((seqs, COMP, WIDTH))])[0], forward(0, hop_a)),
    )
    run3 = after(is_first, saved_a1["log_total"])
    saved_b1 = branches(run3, None, lambda: forward(1, hop_b))

    run4 = after(is_first, saved_b1["log_total"])
    part_a1, grads_a1, dx_a1 = branches(run4, None, lambda: backward(0, hop_a, saved_a1, last_gy[0]))
    back_a = one_way(dx_a1, 1, 0)
    run5 = after(is_first, part_a1["d_down"], dx_a1)
    part_b1, grads_b1, dx_b1 = branches(run5, None, lambda: backward(1, hop_b, saved_b1, last_gy[1]))
    back_b = one_way(dx_b1, 1, 0)
    run6 = after(is_first, part_b1["d_down"], dx_b1)
    part_a0, grads_a0, dx_a0 = branches(run6, lambda: backward(0, first_x[0], saved_a0, back_a), None)

    out_a = one_way(saved_a1["y"][:, :width], 1, 0)
    out_b = one_way(saved_b1["y"][:, :width], 1, 0)

    def chunk(token, make):
        pick = after(is_first, token)
        first = lambda: make(saved_a0, saved_b0, part_a0, part_b0, grads_a0, grads_b0, back_a, back_b)
        second = lambda: make(
            saved_a1, saved_b1, part_a1, part_b1, grads_a1, grads_b1, last_gy[0], last_gy[1]
        )
        return lax.cond(pick, first, second)

    part_b0 = grads_b0 = None
    sums = {}
    token = dx_a0
    halfw = WIDTH // 2
    for i in range(2):
        send, keep = chunk(
            token,
            lambda sa, sb, pa, pb, ga, gb, ya, yb, i=i: weight_grad(
                bits[0],
                size,
                [(sa["hidden"], None), (sb["hidden"], None)],
                [(ya, None, i), (yb, None, i)],
                halfw,
                halfw,
            ),
        )
        sums["down", i] = (send, keep)
        token = keep
    run7 = after(is_first, token)
    part_b0 = branches(run7, lambda: back_ffn(saved_b0, back_b), None)
    token = part_b0["d_down"]
    for i in range(2):
        send, keep = chunk(
            token,
            lambda sa, sb, pa, pb, ga, gb, ya, yb, i=i: weight_grad(
                bits[0],
                size,
                [(sa["ffn_in"], None), (sb["ffn_in"], None)],
                [(pa["d_hidden"], None, 2 * i), (pb["d_hidden"], None, 2 * i)],
                FF // 2,
                1024,
            ),
        )
        sums["up", i] = (send, keep)
        token = keep

    def biases(pa, pb):
        up = (pa["d_up"] + pb["d_up"]).reshape(size, FF // size)
        down = (pa["d_down"] + pb["d_down"]).reshape(size, WIDTH // size)
        row = jnp.concatenate([up, down], axis=1).astype(BF)
        return jnp.pad(row[:, None, :], ((0, 0), (0, 15), (0, WIDTH - row.shape[1])))

    send, keep = chunk(
        token,
        lambda sa, sb, pa, pb, ga, gb, ya, yb: weight_grad(
            bits[0],
            size,
            [(sa["attended"], None), (sb["attended"], None)],
            [(pa["low"], None, 0), (pb["low"], None, 0)],
            WIDTH,
            1024,
            biases(pa, pb),
        ),
    )
    sums["out"] = (send, keep)
    run8 = after(is_first, keep)
    grads_b0 = branches(run8, lambda: back_attend(1, saved_b0, part_b0), None)
    token = grads_b0["dq"]
    for name, key, mem_key in (("key", "dkx", "dkm"), ("value", "dvx", "dvm"), ("query", "dq", None)):

        def make(sa, sb, pa, pb, ga, gb, ya, yb, key=key, mem_key=mem_key):
            lefts = [(sa["normed"], None), (sb["normed"], None)]
            rights = [(ga[key], None, 0), (gb[key], None, 0)]
            if mem_key is not None:
                lefts += [(normed_memory, 0), (normed_memory, 1)]
                rights += [(ga[mem_key], None, 0), (gb[mem_key], None, 0)]
            return weight_grad(bits[0], size, lefts, rights, WIDTH, 512)

        sums[name] = chunk(token, make)
        token = sums[name][1]
    run9 = after(is_first, token)
    dx_b0 = branches(run9, lambda: back_project(first_x[1], part_b0, grads_b0), None)
    grad_a = one_way(dx_a0[:, width:], 0, 1)
    grad_b = one_way(dx_b0[:, width:], 0, 1)

    done = {name: reduce_parts(send, keep, size, bits) for name, (send, keep) in sums.items()}
    rows = WIDTH // size
    g_down = jnp.concatenate([done["down", 0], done["down", 1]], axis=1)
    g_up = jnp.concatenate([done["up", 0], done["up", 1]], axis=1)
    g_out = done["out"][:rows]
    g_b_up = done["out"][rows, : FF // size]
    g_b_down = done["out"][rows, FF // size : FF // size + WIDTH // size]
    g_proj = jnp.concatenate([done["query"], done["key"], done["value"]], axis=1)

    def gain_grad(grad, weight, gain):
        own = lax.dynamic_slice_in_dim(weight, mine * rows, rows, 0).astype(F32)
        scale = lax.dynamic_slice_in_dim(gain, mine * rows, rows, 0).astype(F32)
        return jnp.sum(grad * own, axis=1) / scale

    g_gain_attn = gain_grad(g_proj, w_proj, gain_attn[0])
    g_gain_ffn = gain_grad(g_up, w_up, gain_ffn[0])

    outputs = jnp.stack(
        [
            jnp.where(is_first, got, saved["y"][:, width:])
            for got, saved in ((out_a, saved_a1), (out_b, saved_b1))
        ]
    )
    grad_inputs = jnp.stack(
        [jnp.where(is_first, dx[:, :width], got) for got, dx in ((grad_a, dx_a0), (grad_b, dx_b0))]
    )
    new_memory = jnp.stack(
        [jnp.where(is_first, x, hop) for x, hop in ((first_x[0], hop_a), (first_x[1], hop_b))]
    )
    keep_all = (1 - reset_flags).astype(BF)[:, None, None]
    squeezed = jnp.where(is_first, squeezed_first, squeezed_second)
    new_compressed = jnp.concatenate([compressed[:, COMP:] * keep_all, squeezed], axis=1)
    return (
        outputs,
        grad_inputs,
        new_memory[None],
        new_compressed[None],
        g_gain_attn[None],
        g_proj[None],
        g_out[None],
        g_gain_ffn[None],
        g_up[None],
        g_b_up[None],
        g_down[None],
        g_b_down[None],
    )


FORWARD = dict(
    y=shape((SEG, WIDTH)),
    normed=shape((SEG, WIDTH)),
    qkv=shape((SEG, 3 * WIDTH)),
    attended=shape((SEG, WIDTH)),
    log_total=shape((HEADS, 1, SEG), F32),
    residual=shape((SEG, WIDTH), F32),
    ffn_in=shape((SEG, WIDTH)),
    hidden=shape((SEG, FF)),
    gate=shape((SEG, FF)),
)


def solution(mesh):
    return jax.shard_map(
        body,
        mesh=mesh,
        in_specs=(
            P("dp", None, "section"),
            P("dp", None, "section"),
            P("section", "dp", None, None),
            P("section", "dp", None, None),
            P("dp"),
            P("dp"),
            P("section", None),
            P("section", None, None),
            P("section", None, None),
            P("section", None),
            P("section", None, None),
            P("section", None),
            P("section", None, None),
            P("section", None),
            P("section", None, None, None),
            P("section", None),
        ),
        out_specs=(
            P("dp", None, "section"),
            P("dp", None, "section"),
            P("section", "dp", None, None),
            P("section", "dp", None, None),
            P("section", "dp"),
            P("section", "dp", None),
            P("section", "dp", None),
            P("section", "dp"),
            P("section", "dp", None),
            P("section", "dp"),
            P("section", "dp", None),
            P("section", "dp"),
        ),
        check_vma=False,
    )
```

```python
import math

import jax
import jax.numpy as jnp
from jax import lax
from jax.experimental import pallas as pl
from jax.experimental.pallas import tpu as pltpu
from jax.sharding import PartitionSpec as P

WIDTH = 1024
HEADS = 8
HEAD = 128
FF = 4096
SEG = 512
MEM = 512
CMEM = 512
RATE = 2
COMP = 256
CTX = MEM + CMEM
HALF = SEG // 2
HP = 4

EPS = 1e-05
NEG = -1e30
ROOT_TWO_PI = 0.7978845608028654
SCALE = HEAD**-0.5
LOG2E = math.log2(math.e)
LN2 = math.log(2.0)
BF = jnp.bfloat16
F32 = jnp.float32
PARAMS = pltpu.CompilerParams(vmem_limit_bytes=56 << 20)


def nn(a, b):
    return lax.dot_general(a, b, (((1,), (0,)), ((), ())), preferred_element_type=F32)


def nt(a, b):
    return lax.dot_general(a, b, (((1,), (1,)), ((), ())), preferred_element_type=F32)


def tn(a, b):
    return lax.dot_general(a, b, (((0,), (0,)), ((), ())), preferred_element_type=F32)


def shape(dims, dtype=BF):
    return jax.ShapeDtypeStruct(dims, dtype)


def whole(*dims):
    return pl.BlockSpec(dims, lambda *_: (0,) * len(dims))


def cost(flops, moved, trans=0):
    return pl.CostEstimate(flops=int(flops), bytes_accessed=int(moved), transcendentals=int(trans))


LONG = cost(1e11, 1)
SHORT = cost(1, 1)


def normalise(values):
    centred = values - jnp.mean(values, axis=-1, keepdims=True)
    inverse = lax.rsqrt(jnp.mean(centred * centred, axis=-1, keepdims=True) + EPS)
    return centred * inverse, inverse


def norm_back(unit, inverse, gain, grad):
    scaled = grad * gain
    along = jnp.mean(scaled * unit, axis=-1, keepdims=True)
    return inverse * (scaled - jnp.mean(scaled, axis=-1, keepdims=True) - unit * along)


ANY = pl.BlockSpec(memory_space=pl.ANY)


def call(kernel, name, scalars, ins, outs, scratch, tokens, aliases=None, estimate=LONG, specs=None):
    first = len(scalars) + len(ins)

    def run(*refs):
        kernel(*refs[:first], *refs[first + len(tokens) :])

    return pl.pallas_call(
        run,
        name=name,
        grid_spec=pltpu.PrefetchScalarGridSpec(
            num_scalar_prefetch=len(scalars),
            grid=(1,),
            in_specs=list(specs or [ANY] * len(ins)) + [ANY] * len(tokens),
            out_specs=[ANY] * len(outs),
            scratch_shapes=scratch,
        ),
        out_shape=list(outs),
        input_output_aliases=aliases or {},
        compiler_params=PARAMS,
        cost_estimate=estimate,
    )(*scalars, *ins, *tokens)


class Copies:
    def __init__(self, sems):
        self.sems, self.count, self.named = sems, 0, {}

    def start(self, source, target, name=None):
        copy = pltpu.make_async_copy(source, target, self.sems.at[self.count])
        copy.start()
        self.named[name if name is not None else self.count] = copy
        self.count += 1

    def wait(self, *names):
        for name in names:
            self.named.pop(name).wait()

    def wait_all(self):
        for name in list(self.named):
            self.wait(name)


def tiles(ref, axis, size=1024):
    if axis == 0:
        return [ref.at[pl.ds(i * size, size)] for i in range(ref.shape[0] // size)]
    return [ref.at[:, pl.ds(i * size, size)] for i in range(ref.shape[1] // size)]


def memory_kernel(flags, comp, mem, gain, w, normed, kv, rows, weights, unit_rows, out, sems):
    copies = Copies(sems)
    seqs = comp.shape[0]
    jobs = [(s, j) for s in range(seqs) for j in range(2)]
    for n, (s, j) in enumerate(jobs):
        copies.start((comp, mem)[j].at[s], rows.at[n], ("rows", n))
        if n == 0:
            for t in range(2):
                copies.start(w.at[:, pl.ds((1 + t) * WIDTH, WIDTH)], weights.at[t], ("w", t))

    def unit(n):
        copies.wait(("rows", n))
        keep = (1 - flags[jobs[n][0]]).astype(F32)
        value, _ = normalise(rows[n].astype(F32) * keep)
        unit_rows[n] = (value * gain[...].astype(F32)).astype(BF)

    unit(0)
    for n, (s, j) in enumerate(jobs):
        place = pl.ds(j * MEM, MEM)
        copies.start(unit_rows.at[n], normed.at[s, place])
        for t in range(2):
            if n == 0:
                copies.wait(("w", t))
            out[n, :, t * WIDTH : (t + 1) * WIDTH] = nn(unit_rows[n], weights[t]).astype(BF)
            if t == 0 and n + 1 < len(jobs):
                unit(n + 1)
        copies.start(out.at[n], kv.at[s, place])
    copies.wait_all()


def memory_keyvals(flags, compressed, memory, gain, w_proj, tokens):
    seqs = memory.shape[0]
    return call(
        memory_kernel,
        "memory_keyvals",
        [flags],
        [compressed, memory, gain, w_proj],
        [shape((seqs, CTX, WIDTH)), shape((seqs, CTX, 2 * WIDTH))],
        [
            pltpu.VMEM((2 * seqs, MEM, WIDTH), BF),
            pltpu.VMEM((2, WIDTH, WIDTH), BF),
            pltpu.VMEM((2 * seqs, MEM, WIDTH), BF),
            pltpu.VMEM((2 * seqs, MEM, 2 * WIDTH), BF),
            pltpu.SemaphoreType.DMA((6 * seqs + 2,)),
        ],
        tokens,
        specs=[ANY, ANY, whole(1, WIDTH), ANY],
    )


def fill_masks(flag, bound, bias, unseen):
    key = lax.broadcasted_iota(jnp.int32, (SEG, SEG), 0)
    query = lax.broadcasted_iota(jnp.int32, (SEG, SEG), 1)
    least = jnp.where(query >= bound, bound, 0)
    bias[...] = jnp.where((key <= query) & (key >= least), 0.0, NEG)
    position = lax.broadcasted_iota(jnp.int32, (1, SEG), 1)
    limit = jnp.where(flag == 0, bound, 0)
    unseen[...] = jnp.where(position < limit, 0.0, -NEG)


def gelu_parts(v):
    inner = v * (ROOT_TWO_PI + (0.044715 * ROOT_TWO_PI) * (v * v))
    t = jnp.tanh(inner)
    half = 0.5 + 0.5 * t
    slope = 3.0 * inner - (2.0 * ROOT_TWO_PI) * v
    return v * half, half + half * (1.0 - t) * slope


def attend_heads(first, qkv, kvm, attended, log_total, bias, unseen):
    def cols(base, h):
        return pl.ds(pl.multiple_of(base * WIDTH + (first + h) * HEAD, HEAD), HEAD)

    pieces = [(h, slice(part * HALF, (part + 1) * HALF), (part + 1) * HALF) for h in range(HP) for part in range(2)]

    def scores(h, r, count):
        rows = qkv[r, cols(0, h)]
        return nt(kvm[:, cols(0, h)], rows), nt(qkv[:count, cols(1, h)], rows) + bias[:count, r]

    def weights(h, r, count, on_memory, on_segment):
        hidden = unseen[:, r]
        top = jnp.maximum(
            jnp.max(on_memory, axis=0, keepdims=True) - hidden,
            jnp.max(on_segment, axis=0, keepdims=True),
        )
        p_memory = jnp.exp2(on_memory - (top + hidden))
        p_segment = jnp.exp2(on_segment - top)
        total = jnp.sum(p_memory, axis=0, keepdims=True) + jnp.sum(p_segment, axis=0, keepdims=True)
        log_total[first + h, :, r] = top + jnp.log2(total)
        return p_memory.astype(BF), p_segment.astype(BF), total

    values = {}

    def finish(h, r, count, p_memory, p_segment, total):
        if h not in values:
            values[h] = (kvm[:, cols(1, h)].T, qkv[:, cols(2, h)].T)
        turned = nn(values[h][0], p_memory) + nn(values[h][1][:, :count], p_segment)
        attended[r, cols(0, h)] = (turned * (1.0 / total)).T.astype(BF)

    held, ready = {}, {}
    for step in range(len(pieces) + 2):
        if step < len(pieces):
            held[step] = scores(*pieces[step])
        if 0 <= step - 1 < len(pieces):
            ready[step - 1] = weights(*pieces[step - 1], *held.pop(step - 1))
        if 0 <= step - 2 < len(pieces):
            finish(*pieces[step - 2], *ready.pop(step - 2))


SAVED = (
    ("x", (SEG, WIDTH), BF),
    ("normed", (SEG, WIDTH), BF),
    ("qkv", (SEG, 3 * WIDTH), BF),
    ("attended", (SEG, WIDTH), BF),
    ("log_total", (HEADS, 1, SEG), F32),
    ("residual", (SEG, WIDTH), F32),
    ("ffn_in", (SEG, WIDTH), BF),
    ("hidden", (SEG, FF), BF),
    ("gate", (SEG, FF), BF),
    ("y_low", (SEG, WIDTH // 2), BF),
    ("y_high", (SEG, WIDTH // 2), BF),
)
FS = 512


def forward_kernel(seq, parts, aliased, active, flags, bounds, *refs):
    xs, refs = refs[: len(parts)], refs[len(parts) :]
    (gain, w_proj, kv_memory, w_out, gain_ffn, w_up, b_up, w_down, b_down), refs = refs[:9], refs[9:]
    refs = refs[aliased:]
    y, refs = refs[0], refs[1:]
    out = dict(zip([name for name, _, _ in SAVED], refs))
    refs = refs[len(SAVED) :]
    held = dict(zip([name for name, _, _ in SAVED], refs))
    pool, kvm, wo, total, y_rows, bias, unseen, in_sems, out_sems, feed_sems = refs[len(SAVED) :]

    @pl.when(active[0] == 1)
    def _():
        loads, stores = Copies(in_sems), Copies(out_sems)

        def save(*names):
            for name in names:
                stores.start(held[name], out[name].at[seq])

        x = held["x"]
        for i, (part, lead) in enumerate(zip(xs, parts)):
            wide = WIDTH // len(parts)
            loads.start(part if lead is None else part.at[lead], x.at[:, pl.ds(i * wide, wide)], ("x", i))
        for t, tile in enumerate(tiles(w_proj, 1)):
            loads.start(tile, pool.at[t], ("proj", t))
        loads.start(kv_memory.at[seq], kvm, "kvm")
        loads.start(w_out, wo, "out")
        for t, tile in enumerate(tiles(w_up, 1)):
            loads.start(tile, pool.at[4 + t], ("up", t))
        fill_masks(flags[seq], bounds[seq], bias, unseen)
        loads.wait(*[("x", i) for i in range(len(parts))])
        unit, _ = normalise(x[...].astype(F32))
        held["normed"][...] = (unit * gain[...].astype(F32)).astype(BF)
        for t in range(3):
            loads.wait(("proj", t))
            factor = SCALE * LOG2E if t == 0 else 1.0
            held["qkv"][:, t * WIDTH : (t + 1) * WIDTH] = (nn(held["normed"][...], pool[t]) * factor).astype(BF)
        for t, tile in enumerate(tiles(w_down, 0)):
            loads.start(tile, pool.at[t], ("down", t))
        save("x", "normed", "qkv")
        loads.wait("kvm")

        def heads(g, _):
            attend_heads(g * HP, held["qkv"], kvm, held["attended"], held["log_total"], bias, unseen)
            return 0

        lax.fori_loop(0, HEADS // HP, heads, 0)
        save("attended", "log_total")
        loads.wait("out")
        rows = x[...].astype(F32) + nn(held["attended"][...], wo[...])
        held["residual"][...] = rows
        unit, _ = normalise(rows)
        held["ffn_in"][...] = (unit * gain_ffn[...].astype(F32)).astype(BF)
        save("residual", "ffn_in")
        total[...] = rows + b_down[...].astype(F32)
        loads.wait_all()

        def feed(t, _):
            cuts = [pl.ds(pl.multiple_of(t * 1024 + i * FS, FS), FS) for i in range(1024 // FS)]
            ups = [
                nn(held["ffn_in"][...], pool[4 + t, :, i * FS : (i + 1) * FS]) + b_up[:, c].astype(F32)
                for i, c in enumerate(cuts)
            ]
            added = None
            for i, (c, up) in enumerate(zip(cuts, ups)):
                value, slope = gelu_parts(up)
                value = value.astype(BF)
                held["hidden"][:, c] = value
                held["gate"][:, c] = slope.astype(BF)
                part = nn(value, pool[t, i * FS : (i + 1) * FS])
                added = part if added is None else added + part
            total[...] += added
            for name, sem in (("hidden", 0), ("gate", 1)):
                feed_copy(name, sem, t).start()
            return 0

        def feed_copy(name, sem, t):
            place = pl.ds(pl.multiple_of(t * 1024, 1024), 1024)
            return pltpu.make_async_copy(held[name].at[:, place], out[name].at[seq, :, place], feed_sems.at[sem, t])

        lax.fori_loop(0, FF // 1024, feed, 0)
        rows = total[...].astype(BF)
        y_rows[...] = rows
        held["y_low"][...] = rows[:, : WIDTH // 2]
        held["y_high"][...] = rows[:, WIDTH // 2 :]
        stores.start(y_rows, y)
        save("y_low", "y_high")
        for t in range(FF // 1024):
            feed_copy("hidden", 0, t).wait()
            feed_copy("gate", 1, t).wait()
        stores.wait_all()


def forward(seq, seqs, scalars, xs, kv_memory, params, saved, tokens):
    gain_attn, w_proj, w_out, gain_ffn, w_up, b_up, w_down, b_down = params
    args = [v for v, _ in xs] + [gain_attn, w_proj, kv_memory, w_out, gain_ffn, w_up, b_up, w_down, b_down]
    specs = [ANY] * len(xs) + [
        whole(1, WIDTH), ANY, ANY, ANY, whole(1, WIDTH), ANY, whole(1, FF), ANY, whole(1, WIDTH)
    ]
    aliases = {}
    if saved is not None:
        aliases = {len(scalars) + len(args) + i: 1 + i for i in range(len(SAVED))}
        args += [saved[name] for name, _, _ in SAVED]
        specs += [ANY] * len(SAVED)
    leads = [lead for _, lead in xs]
    results = call(
        lambda *refs: forward_kernel(seq, leads, len(aliases), *refs),
        "forward",
        scalars,
        args,
        [shape((SEG, WIDTH))] + [shape((seqs,) + dims, dtype) for _, dims, dtype in SAVED],
        [pltpu.VMEM(dims, dtype) for _, dims, dtype in SAVED]
        + [
            pltpu.VMEM((8, WIDTH, WIDTH), BF),
            pltpu.VMEM((CTX, 2 * WIDTH), BF),
            pltpu.VMEM((WIDTH, WIDTH), BF),
            pltpu.VMEM((SEG, WIDTH), F32),
            pltpu.VMEM((SEG, WIDTH), BF),
            pltpu.VMEM((SEG, SEG), F32),
            pltpu.VMEM((1, SEG), F32),
            pltpu.SemaphoreType.DMA((16,)),
            pltpu.SemaphoreType.DMA((14,)),
            pltpu.SemaphoreType.DMA((2, FF // 1024)),
        ],
        tokens,
        aliases,
        specs=specs,
    )
    return results[0], dict(zip([name for name, _, _ in SAVED], results[1:]))


FED = (
    ("d_hidden", (SEG, FF), BF),
    ("d_residual", (SEG, WIDTH), F32),
    ("low", (SEG, WIDTH), BF),
    ("d_attended", (SEG, WIDTH), BF),
    ("d_up", (1, FF), F32),
    ("d_down", (1, WIDTH), F32),
)


def feed_back_kernel(seq, leads, aliased, active, *refs):
    gys, refs = refs[: len(leads)], refs[len(leads) :]
    (w_down, gate, w_up, residual, gain, w_out), refs = refs[:6], refs[6:]
    refs = refs[aliased:]
    out = dict(zip([name for name, _, _ in FED], refs))
    refs = refs[len(FED) :]
    held = dict(zip([name for name, _, _ in FED], refs))
    gy_rows, pool, gates, rows, wo, total, in_sems, out_sems = refs[len(FED) :]

    @pl.when(active[0] == 1)
    def _():
        loads, stores = Copies(in_sems), Copies(out_sems)
        for i, (part, lead) in enumerate(zip(gys, leads)):
            wide = WIDTH // len(leads)
            loads.start(part if lead is None else part.at[lead], gy_rows.at[:, pl.ds(i * wide, wide)], ("gy", i))
        downs, ups = tiles(w_down, 0), tiles(w_up, 1)
        for t in range(FF // 1024):
            loads.start(downs[t], pool.at[t], ("down", t))
            loads.start(gate.at[seq, :, pl.ds(t * 1024, 1024)], gates.at[:, pl.ds(t * 1024, 1024)], ("gate", t))
            loads.start(ups[t], pool.at[4 + t], ("up", t))
        loads.start(residual.at[seq], rows, "rows")
        loads.start(w_out, wo, "out")
        loads.wait(*[("gy", i) for i in range(len(leads))])
        held["d_down"][...] = jnp.sum(gy_rows[...].astype(F32), axis=0, keepdims=True)
        for t in range(FF // 1024):
            loads.wait(("down", t), ("gate", t), ("up", t))
            raws = [nt(gy_rows[...], pool[t, i * FS : (i + 1) * FS]) for i in range(1024 // FS)]
            added = None
            for i, raw in enumerate(raws):
                c = slice(t * 1024 + i * FS, t * 1024 + (i + 1) * FS)
                value = (raw * gates[:, c].astype(F32)).astype(BF)
                held["d_hidden"][:, c] = value
                held["d_up"][:, c] = jnp.sum(value.astype(F32), axis=0, keepdims=True)
                part = nt(value, pool[4 + t, :, i * FS : (i + 1) * FS])
                added = part if added is None else added + part
            total[...] = added if t == 0 else total[...] + added
        for name in ("d_hidden", "d_up", "d_down"):
            stores.start(held[name], out[name].at[seq])
        loads.wait("rows", "out")
        unit, inverse = normalise(rows[...])
        grad = gy_rows[...].astype(F32) + norm_back(unit, inverse, gain[...].astype(F32), total[...])
        held["d_residual"][...] = grad
        held["low"][...] = grad.astype(BF)
        held["d_attended"][...] = nt(held["low"][...], wo[...]).astype(BF)
        for name in ("d_residual", "low", "d_attended"):
            stores.start(held[name], out[name].at[seq])
        stores.wait_all()


def feed_back(seq, scalars, gys, saved, params, fed, tokens):
    gain_attn, w_proj, w_out, gain_ffn, w_up, b_up, w_down, b_down = params
    seqs = saved["gate"].shape[0]
    args = [v for v, _ in gys] + [w_down, saved["gate"], w_up, saved["residual"], gain_ffn, w_out]
    specs = [ANY] * (len(gys) + 4) + [whole(1, WIDTH), ANY]
    aliases = {}
    if fed is not None:
        aliases = {len(scalars) + len(args) + i: i for i in range(len(FED))}
        args += [fed[name] for name, _, _ in FED]
        specs += [ANY] * len(FED)
    leads = [lead for _, lead in gys]
    results = call(
        lambda *refs: feed_back_kernel(seq, leads, len(aliases), *refs),
        "feed_back",
        scalars,
        args,
        [shape((seqs,) + dims, dtype) for _, dims, dtype in FED],
        [pltpu.VMEM(dims, dtype) for _, dims, dtype in FED]
        + [
            pltpu.VMEM((SEG, WIDTH), BF),
            pltpu.VMEM((8, WIDTH, WIDTH), BF),
            pltpu.VMEM((SEG, FF), BF),
            pltpu.VMEM((SEG, WIDTH), F32),
            pltpu.VMEM((WIDTH, WIDTH), BF),
            pltpu.VMEM((SEG, WIDTH), F32),
            pltpu.SemaphoreType.DMA((16,)),
            pltpu.SemaphoreType.DMA((8,)),
        ],
        tokens,
        aliases,
        specs=specs,
    )
    return dict(zip([name for name, _, _ in FED], results))


MADE = (
    ("dq", (SEG, WIDTH), BF),
    ("dkx", (SEG, WIDTH), BF),
    ("dvx", (SEG, WIDTH), BF),
    ("dkm", (CTX, WIDTH), BF),
    ("dvm", (CTX, WIDTH), BF),
    ("dx_low", (SEG, WIDTH // 2), BF),
    ("dx_high", (SEG, WIDTH // 2), BF),
)
GROUP = 2


def attend_back_heads(first, qkv, kvm, d_out, out, log_total, made, bias, unseen):
    every, low, high = slice(0, SEG), slice(0, HALF), slice(HALF, SEG)

    def cols(base, h):
        return pl.ds(pl.multiple_of(base * WIDTH + (first + h) * HEAD, HEAD), HEAD)

    for h in range(GROUP):
        c = cols(0, h)
        qh, gh = qkv[:, c], d_out[:, c]
        inner = jnp.sum((gh.astype(F32) * out[:, c].astype(F32)).T, axis=0, keepdims=True)
        level = log_total[first + h]

        def piece(k, v, r, mask):
            logits = nt(k, qh[r])
            if mask is None:
                p = jnp.exp2(logits - (level[:, r] + unseen[:, r]))
            else:
                p = jnp.exp2(logits + mask - level[:, r])
            ds = (p * (nt(v, gh[r]) - inner[:, r])).astype(BF)
            return p.astype(BF), ds

        km, vm, kx, vx = kvm[:, c], kvm[:, cols(1, h)], qkv[:, cols(1, h)], qkv[:, cols(2, h)]
        p_memory, ds_memory = piece(km, vm, every, None)
        p_low, ds_low = piece(kx[low], vx[low], every, bias[low, :])
        p_high, ds_high = piece(kx[high], vx[high], high, bias[high, high])
        made["dvm"][:, c] = nn(p_memory, gh).astype(BF)
        made["dkm"][:, c] = (nn(ds_memory, qh) * LN2).astype(BF)
        made["dvx"][low, c] = nn(p_low, gh).astype(BF)
        made["dkx"][low, c] = (nn(ds_low, qh) * LN2).astype(BF)
        made["dvx"][high, c] = nn(p_high, gh[high]).astype(BF)
        made["dkx"][high, c] = (nn(ds_high, qh[high]) * LN2).astype(BF)
        turned = kx.T
        both = nn(km.T, ds_memory) + nn(turned[:, low], ds_low)
        made["dq"][low, c] = (both[:, low] * SCALE).T.astype(BF)
        made["dq"][high, c] = ((both[:, high] + nn(turned[:, high], ds_high)) * SCALE).T.astype(BF)


def attend_back_kernel(seq, aliased, active, flags, bounds, *refs):
    (qkv_in, kv_memory, d_out_in, out_in, stat_in, w_proj, x_in, gain, d_residual), refs = refs[:9], refs[9:]
    refs = refs[aliased:]
    dx, refs = refs[0], refs[1:]
    result = dict(zip([name for name, _, _ in MADE], refs))
    refs = refs[len(MADE) :]
    made = dict(zip([name for name, _, _ in MADE], refs))
    refs = refs[len(MADE) :]
    qkv, kvm, d_out, out, log_total, pool, x, rows, dx_rows, bias, unseen, in_sems, head_sems, out_sems = refs

    @pl.when(active[0] == 1)
    def _():
        loads, stores = Copies(in_sems), Copies(out_sems)
        wide = GROUP * HEAD
        count = WIDTH // wide

        def head_copies(g):
            g = g * wide if isinstance(g, int) else pl.multiple_of(g * wide, wide)
            sems = head_sems.at[g // wide]
            pairs = [
                (ref.at[seq, :, pl.ds(base * WIDTH + g, wide)], target.at[:, pl.ds(base * WIDTH + g, wide)])
                for ref, target, bases in (
                    (qkv_in, qkv, 3),
                    (kv_memory, kvm, 2),
                    (d_out_in, d_out, 1),
                    (out_in, out, 1),
                )
                for base in range(bases)
            ]
            return [pltpu.make_async_copy(a, b, sems.at[i]) for i, (a, b) in enumerate(pairs)]

        loads.start(stat_in.at[seq], log_total, "stat")
        for g in range(count):
            for copy in head_copies(g):
                copy.start()
        for t, tile in enumerate(tiles(w_proj, 1)):
            loads.start(tile, pool.at[t])
        loads.start(x_in.at[seq], x)
        loads.start(d_residual.at[seq], rows)
        fill_masks(flags[seq], bounds[seq], bias, unseen)
        loads.wait("stat")

        def heads(g, _):
            for copy in head_copies(g):
                copy.wait()
            attend_back_heads(g * GROUP, qkv, kvm, d_out, out, log_total, made, bias, unseen)
            return 0

        lax.fori_loop(0, count, heads, 0)
        for name, _, _ in MADE[:5]:
            stores.start(made[name], result[name].at[seq])
        loads.wait_all()
        grad = nt(made["dq"][...], pool[0]) + nt(made["dkx"][...], pool[1]) + nt(made["dvx"][...], pool[2])
        unit, inverse = normalise(x[...].astype(F32))
        value = (rows[...] + norm_back(unit, inverse, gain[...].astype(F32), grad)).astype(BF)
        dx_rows[...] = value
        made["dx_low"][...] = value[:, : WIDTH // 2]
        made["dx_high"][...] = value[:, WIDTH // 2 :]
        stores.start(dx_rows, dx)
        for name, _, _ in MADE[5:]:
            stores.start(made[name], result[name].at[seq])
        stores.wait_all()


def attend_back(seq, scalars, saved, fed, kv_memory, params, made, tokens, estimate=LONG):
    gain_attn, w_proj, w_out, gain_ffn, w_up, b_up, w_down, b_down = params
    seqs = saved["qkv"].shape[0]
    args = [
        saved["qkv"],
        kv_memory,
        fed["d_attended"],
        saved["attended"],
        saved["log_total"],
        w_proj,
        saved["x"],
        gain_attn,
        fed["d_residual"],
    ]
    specs = [ANY] * 7 + [whole(1, WIDTH), ANY]
    aliases = {}
    if made is not None:
        aliases = {len(scalars) + len(args) + i: 1 + i for i in range(len(MADE))}
        args += [made[name] for name, _, _ in MADE]
        specs += [ANY] * len(MADE)
    results = call(
        lambda *refs: attend_back_kernel(seq, len(aliases), *refs),
        "attend_back",
        scalars,
        args,
        [shape((SEG, WIDTH))] + [shape((seqs,) + dims, dtype) for _, dims, dtype in MADE],
        [pltpu.VMEM(dims, dtype) for _, dims, dtype in MADE]
        + [
            pltpu.VMEM((SEG, 3 * WIDTH), BF),
            pltpu.VMEM((CTX, 2 * WIDTH), BF),
            pltpu.VMEM((SEG, WIDTH), BF),
            pltpu.VMEM((SEG, WIDTH), BF),
            pltpu.VMEM((HEADS, 1, SEG), F32),
            pltpu.VMEM((3, WIDTH, WIDTH), BF),
            pltpu.VMEM((SEG, WIDTH), BF),
            pltpu.VMEM((SEG, WIDTH), F32),
            pltpu.VMEM((SEG, WIDTH), BF),
            pltpu.VMEM((SEG, SEG), F32),
            pltpu.VMEM((1, SEG), F32),
            pltpu.SemaphoreType.DMA((8,)),
            pltpu.SemaphoreType.DMA((WIDTH // (GROUP * HEAD), 7)),
            pltpu.SemaphoreType.DMA((8,)),
        ],
        tokens,
        aliases,
        estimate,
        specs,
    )
    return results[0], dict(zip([name for name, _, _ in MADE], results[1:]))


def compress_kernel(flags, grouped, w, bias, out, rows, weights, result, sems):
    copies = Copies(sems)
    copies.start(grouped, rows, "rows")
    copies.start(w, weights, "w")
    copies.wait("rows", "w")
    for s in range(rows.shape[0]):
        keep = (1 - flags[s]).astype(BF)
        result[s] = (nn(rows[s] * keep, weights[...]) + bias[...].astype(F32)).astype(BF)
        copies.start(result.at[s], out.at[s])
    copies.wait_all()


def compress(flags, memory, w_compress, b_compress, tokens):
    seqs = memory.shape[0]
    wide = RATE * WIDTH
    grouped = memory.reshape(seqs, COMP, wide)
    return call(
        compress_kernel,
        "compress",
        [flags],
        [grouped, w_compress.reshape(wide, WIDTH), b_compress],
        [shape((seqs, COMP, WIDTH))],
        [
            pltpu.VMEM((seqs, COMP, wide), BF),
            pltpu.VMEM((wide, WIDTH), BF),
            pltpu.VMEM((seqs, COMP, WIDTH), BF),
            pltpu.SemaphoreType.DMA((2 + seqs,)),
        ],
        tokens,
        estimate=SHORT,
        specs=[ANY, ANY, whole(1, WIDTH)],
    )


WIDE = 512


def places_of(order, size):
    rest, place = order[1:], {}
    for index in range(size):
        place[index] = sum(((index >> b) & 1) << (len(rest) - 1 - n) for n, b in enumerate(rest))
    return place


class Either(list):
    def __init__(self, arrays, places):
        super().__init__(arrays)
        self.places = places


def either_copies(group, refs, target, sems, base):
    made = []
    for wanted, places in enumerate(group.places):
        copies = []
        for n, (k, lead, row, column) in enumerate(places):
            source = refs[k] if lead is None else refs[k].at[lead]
            rows, columns = source.shape
            to = target.at[pl.ds(row, rows), pl.ds(column, columns)]
            copies.append(pltpu.make_async_copy(source, to, sems.at[base + n]))
        made.append((wanted, copies))
    return made


def weight_kernel(size, groups, tasks, chunks, places, small_chunk, section, mine, *refs):
    total = sum(len(g) for g in groups)
    ins, refs = refs[:total], refs[total:]
    if small_chunk is not None:
        small, refs = refs[0], refs[1:]
    sends, refs = refs[: len(chunks)], refs[len(chunks) :]
    keeps, refs = refs[: len(chunks)], refs[len(chunks) :]
    held, refs = refs[: len(groups)], refs[len(groups) :]
    staged, small_rows, in_sems, out_sems = refs
    loads, stores = Copies(in_sems), Copies(out_sems)
    even = (mine[0] & 1) == 0
    parts, at = [], 0
    for g in groups:
        parts.append(ins[at : at + len(g)])
        at += len(g)

    either = {}
    for key in dict.fromkeys(k for t in tasks for k in (t["left"], t["right"])):
        g, tile = key
        place, row = pl.ds(tile * 1024, 1024), 0
        if isinstance(groups[g], Either):
            for wanted, copies in either_copies(groups[g], parts[g], held[g], in_sems, loads.count):
                pl.when(section[0] == wanted)(lambda copies=copies: [c.start() for c in copies] and None)
            either[g] = either_copies(groups[g], parts[g], held[g], in_sems, loads.count)
            loads.count += max(len(copies) for _, copies in either[g])
            continue
        for n, ref in enumerate(parts[g]):
            loads.start(ref.at[:, place], held[g].at[pl.ds(row, ref.shape[0]), place], key + (n,))
            row += ref.shape[0]
    ready = set()

    if small_chunk is not None:
        for pair in range(size // 2):
            place = places[small_chunk][2 * pair]
            one, two = small[2 * pair], small[2 * pair + 1]
            small_rows[0, place] = jnp.where(even, two, one)
            small_rows[1, place] = jnp.where(even, one, two)
        for i, target in enumerate((sends, keeps)):
            rows = target[small_chunk].shape[1] - 16
            stores.start(small_rows.at[i], target[small_chunk].at[:, pl.ds(rows, 16), pl.ds(0, WIDTH)], ("small", i))

    busy = {}
    for n, task in enumerate(tasks):
        slot = n % 2
        for key in (task["left"], task["right"]):
            if key not in ready:
                ready.add(key)
                if key[0] in either:
                    for wanted, copies in either[key[0]]:
                        pl.when(section[0] == wanted)(lambda copies=copies: [c.wait() for c in copies] and None)
                else:
                    loads.wait(*[key + (m,) for m in range(len(parts[key[0]]))])
        for name in busy.pop(slot, ()):
            stores.wait(name)
        count = size // task["blocks"]
        rows = 1024 // count
        (left, lt), (right, rt) = task["left"], task["right"]
        for cut in range(1024 // WIDE):
            c = slice(cut * WIDE, (cut + 1) * WIDE)
            value = tn(
                held[left][:, lt * 1024 : (lt + 1) * 1024],
                held[right][:, rt * 1024 + cut * WIDE : rt * 1024 + (cut + 1) * WIDE],
            ).astype(BF)
            for pair in range(count // 2):
                one = value[(2 * pair) * rows : (2 * pair + 1) * rows]
                two = value[(2 * pair + 1) * rows : (2 * pair + 2) * rows]
                staged[slot, 0, pair, :, c] = jnp.where(even, two, one)
                staged[slot, 1, pair, :, c] = jnp.where(even, one, two)
        names = []
        for k, first, width, base in task["outs"]:
            for i, target in enumerate((sends, keeps)):
                for pair in range(count // 2):
                    names.append((n, k, i, pair))
                    stores.start(
                        staged.at[slot, i, pair, :, pl.ds(first, width)],
                        target[k].at[places[k][task["block"] * count + 2 * pair], pl.ds(0, rows), pl.ds(base, width)],
                        names[-1],
                    )
        busy[slot] = names
    stores.wait_all()


def weight_grads(section, mine, size, groups, tasks, chunks, tokens, places, small=None, small_chunk=None):
    outs = []
    for k, (blocks, columns) in enumerate(chunks):
        rows = blocks * 1024 // size + (16 if k == small_chunk else 0)
        outs.append(shape((size // 2, rows, columns)))
    args = [v for g in groups for v in g] + ([small] if small is not None else [])
    specs = [ANY] * sum(len(g) for g in groups) + ([whole(*small.shape)] if small is not None else [])
    count = size // tasks[0]["blocks"]

    def buffer(g):
        if isinstance(g, Either):
            return pltpu.VMEM((2 * SEG, WIDTH), BF)
        return pltpu.VMEM((sum(v.shape[0] for v in g), g[0].shape[1]), BF)

    results = call(
        lambda *refs: weight_kernel(size, groups, tasks, chunks, places, small_chunk, *refs),
        "weight_grads",
        [section, mine],
        args,
        outs + outs,
        [buffer(g) for g in groups]
        + [
            pltpu.VMEM((2, 2, count // 2, 1024 // count, 1024), BF),
            pltpu.VMEM((2, size // 2, 16, WIDTH), BF),
            pltpu.SemaphoreType.DMA((sum(len(g) * max(1, g[0].shape[-1] // 1024) for g in groups),)),
            pltpu.SemaphoreType.DMA((2 + sum(count * len(t["outs"]) for t in tasks),)),
        ],
        tokens,
        specs=specs,
    )
    return list(zip(results[: len(chunks)], results[len(chunks) :]))


def halve_kernel(levels, mine, *refs):
    total = len(levels)
    kept, got, refs = refs[:total], refs[total : 2 * total], refs[2 * total :]
    outs = []
    for level in levels:
        outs.append(refs[: 1 if level is None else 2])
        refs = refs[len(outs[-1]) :]
    held, came, refs = refs[:total], refs[total : 2 * total], refs[2 * total :]
    wide, refs = refs[:-2], refs[-2:]
    loads, stores = Copies(refs[0]), Copies(refs[1])
    wide = list(wide)
    for n, level in enumerate(levels):
        if level is None:
            loads.start(kept[n], held[n], (n, 0, 0))
            loads.start(got[n], came[n], (n, 0, 1))
            continue
        half = kept[n].shape[0] // 2
        bit = (mine[0] >> level) & 1
        for j, which in enumerate((1 - bit, bit)):
            place = pl.ds(which * half, half)
            loads.start(kept[n].at[place], held[n].at[j], (n, j, 0))
            loads.start(got[n].at[place], came[n].at[j], (n, j, 1))
    for n, level in enumerate(levels):
        if level is None:
            total_rows = wide.pop(0)
            loads.wait((n, 0, 0), (n, 0, 1))
            total_rows[...] = held[n][0].astype(F32) + came[n][0].astype(F32)
            stores.start(total_rows, outs[n][0])
            continue
        for j, target in enumerate(outs[n]):
            loads.wait((n, j, 0), (n, j, 1))
            held[n][j] = held[n][j] + came[n][j]
            stores.start(held[n].at[j], target)
    stores.wait_all()


def halve(mine, levels, kept, got, tokens, estimate):
    total = len(kept)
    outs, held, wide = [], [], []
    for level, v in zip(levels, kept):
        if level is None:
            outs.append(shape(v.shape[1:], F32))
            wide.append(pltpu.VMEM(v.shape[1:], F32))
            held.append(pltpu.VMEM(v.shape, BF))
        else:
            half = (v.shape[0] // 2,) + v.shape[1:]
            outs += [shape(half)] * 2
            held.append(pltpu.VMEM((2,) + half, BF))
    results = call(
        lambda *refs: halve_kernel(levels, *refs),
        "halve",
        [mine],
        [*kept, *got],
        outs,
        held
        + held
        + wide
        + [pltpu.SemaphoreType.DMA((4 * total,)), pltpu.SemaphoreType.DMA((2 * total,))],
        tokens,
        estimate=estimate,
    )
    results, made = list(results), []
    for level in levels:
        made.append([results.pop(0) for _ in range(1 if level is None else 2)])
    return made


def gather_kernel(targets, ready, small, mine, *refs):
    total = len(targets)
    late = [n for n in range(total) if not ready[n]]
    kept, refs = refs[:total], refs[total:]
    got, refs = dict(zip(late, refs)), refs[len(late) :]
    (w_proj, w_up, gain_attn, gain_ffn), outs, refs = refs[:4], refs[4:12], refs[12:]
    held, refs = dict(zip(late, refs)), refs[len(late) :]
    came, refs = dict(zip(late, refs)), refs[len(late) :]
    sums, (small_rows, b_up, b_down, proj_rows, up_rows, gains), (in_sems, out_sems) = refs[:4], refs[4:10], refs[10:]
    loads, stores = Copies(in_sems), Copies(out_sems)
    rows = proj_rows.shape[0]
    for n, (k, first) in enumerate(targets):
        if ready[n]:
            place = sums[k].at[:, pl.ds(first, kept[n].shape[1])]
            if n == small:
                loads.start(kept[n].at[pl.ds(0, rows)], place, ("sum", n))
                loads.start(kept[n].at[pl.ds(rows, 16), pl.ds(0, WIDTH)], small_rows, "small")
            else:
                loads.start(kept[n], place, ("sum", n))
        else:
            loads.start(kept[n].at[0], held[n], ("kept", n))
            loads.start(got[n].at[0], came[n], ("got", n))
    own = pl.ds(pl.multiple_of(mine[0] * rows, rows), rows)
    loads.start(w_proj.at[own], proj_rows, "proj")
    loads.start(w_up.at[own], up_rows, "up")
    for n, (k, first) in enumerate(targets):
        if ready[n]:
            loads.wait(("sum", n))
            continue
        loads.wait(("kept", n), ("got", n))
        value = held[n][...].astype(F32) + came[n][...].astype(F32)
        sums[k][:, first : first + value.shape[1]] = value
    for k in range(4):
        stores.start(sums[k], outs[k])
    loads.wait("small")
    b_up[...] = small_rows[:1, : b_up.shape[1]]
    b_down[...] = small_rows[:1, b_up.shape[1] : b_up.shape[1] + rows]
    stores.start(b_up, outs[4])
    stores.start(b_down, outs[5])
    loads.wait("proj", "up")
    for n, (weight, grad, gain) in enumerate(((proj_rows, sums[3], gain_attn), (up_rows, sums[1], gain_ffn))):
        along = jnp.sum(weight[...].astype(F32) * grad[...], axis=1, keepdims=True)
        turned = jnp.broadcast_to(along, (rows, 128)).T
        gains[n] = turned[:1, :rows] / gain[...]
        stores.start(gains.at[n], outs[6 + n])
    stores.wait_all()


def gather_up(mine, targets, kept, got, small, w_proj, w_up, own_gain, size, tokens):
    rows = WIDTH // size
    widths = [(FF // size, WIDTH), (rows, FF), (rows, WIDTH), (rows, 3 * WIDTH)]
    outs = [shape(w, F32) for w in widths]
    outs += [shape((1, n), F32) for n in (FF // size, rows, rows, rows)]
    late = [v for v, g in zip(kept, got) if g is not None]
    pieces = [pltpu.VMEM(v.shape[1:], BF) for v in late]
    ready = [g is None for g in got]
    arrived = [g for g in got if g is not None]
    return call(
        lambda *refs: gather_kernel(targets, ready, small, *refs),
        "gather_up",
        [mine],
        [*kept, *arrived, w_proj, w_up, *own_gain],
        outs,
        pieces
        + pieces
        + [pltpu.VMEM(w, F32) for w in widths]
        + [
            pltpu.VMEM((16, WIDTH), F32),
            pltpu.VMEM((1, FF // size), F32),
            pltpu.VMEM((1, rows), F32),
            pltpu.VMEM((rows, 3 * WIDTH), BF),
            pltpu.VMEM((rows, FF), BF),
            pltpu.VMEM((2, 1, rows), F32),
            pltpu.SemaphoreType.DMA((2 * len(kept) + 3,)),
            pltpu.SemaphoreType.DMA((8,)),
        ],
        tokens,
        estimate=SHORT,
        specs=[ANY] * (len(kept) + len(late) + 2) + [whole(1, rows)] * 2,
    )


def pick_kernel(section, first, second, out, held, sems):
    for wanted, source in enumerate((first, second)):

        @pl.when(section[0] == wanted)
        def _(source=source):
            copies = Copies(sems)
            for s in range(held.shape[0]):
                copies.start(source.at[s], held.at[s], ("in", s))
            for s in range(held.shape[0]):
                copies.wait(("in", s))
                copies.start(held.at[s], out.at[s])
            copies.wait_all()


def pick(section, first, second, tokens):
    return call(
        pick_kernel,
        "pick",
        [section],
        [first, second],
        [shape(first.shape)],
        [pltpu.VMEM(first.shape, BF), pltpu.SemaphoreType.DMA((2 * first.shape[0],))],
        tokens,
        estimate=SHORT,
    )[0]


def swap_bit(value, size, bit):
    return lax.ppermute(value, "dp", [(i, i ^ (1 << bit)) for i in range(size)])


def one_way(value, first, second):
    return lax.ppermute(value, "section", [(first, second)])


def both_after(first, second):
    return lax.optimization_barrier((first, second))


def body(
    inputs,
    cotangent,
    memory,
    compressed,
    reset_flags,
    boundary,
    gain_attn,
    projection_weight,
    w_output,
    gain_ffn,
    w_up,
    b_up,
    w_down,
    b_down,
    w_compress,
    b_compress,
):
    section = lax.axis_index("section")
    is_first = section == 0
    size = lax.axis_size("dp")
    mine = lax.axis_index("dp")
    levels = (size - 1).bit_length()
    at_section, at_dp = section.astype(jnp.int32).reshape(1), mine.astype(jnp.int32).reshape(1)
    active = (1 - at_section, at_section)
    seqs, _, width = inputs.shape
    memory, compressed = memory[0], compressed[0]
    w_proj, w_out, w_up, w_down = projection_weight[0], w_output[0], w_up[0], w_down[0]
    params = (gain_attn, w_proj, w_out, gain_ffn, w_up, b_up, w_down, b_down)
    last = [[]]

    other_x = [one_way(inputs[0], 1, 0)]
    normed_memory, kv_memory = memory_keyvals(reset_flags, compressed, memory, gain_attn, w_proj, [])
    last[0] = [kv_memory]
    inputs_later, kv_memory = both_after(inputs, kv_memory)
    other_x.append(one_way(inputs_later[1], 1, 0))

    def ahead(layer, s, xs, saved):
        scalars = [active[layer], reset_flags, boundary]
        y, saved = forward(s, seqs, scalars, xs, kv_memory, params, saved, last[0])
        last[0] = [y]
        return y, saved

    y_a0, saved = ahead(0, 0, ((inputs, 0), (other_x[0], None)), None)
    hop_a = one_way(y_a0, 0, 1)
    y_b0, saved = ahead(0, 1, ((inputs, 1), (other_x[1], None)), saved)
    y_b0, cotangent_later = both_after(y_b0, cotangent)
    y_b0, memory_later = both_after(y_b0, memory)
    hop_b = one_way(y_b0, 0, 1)
    other_gy = one_way(cotangent_later, 0, 1)
    squeezed = compress(reset_flags, memory_later, w_compress[0], b_compress, last[0])[0]
    last[0] = [squeezed]
    y_a1, saved = ahead(1, 0, ((hop_a, None),), saved)
    y_b1, saved = ahead(1, 1, ((hop_b, None),), saved)
    other_y = one_way(saved["y_low"], 1, 0)

    def back(layer, s, gys, fed, made):
        fed = feed_back(s, [active[layer]], gys, saved, params, fed, last[0])
        scalars = [active[layer], reset_flags, boundary]
        dx, made = attend_back(s, scalars, saved, fed, kv_memory, params, made, [], SHORT)
        last[0] = [dx]
        return dx, fed, made

    dx_a1, fed, made = back(1, 0, ((other_gy, 0), (cotangent, 0)), None, None)
    back_a = one_way(dx_a1, 1, 0)
    dx_b1, fed, made = back(1, 1, ((other_gy, 1), (cotangent, 1)), fed, made)
    back_b = one_way(dx_b1, 1, 0)
    dx_a0, fed, made = back(0, 0, ((back_a, None),), fed, made)

    rows_of = lambda v: v.reshape((-1, v.shape[-1]))
    half = WIDTH // 2
    gy_all = Either(
        [back_a, back_b, other_gy, cotangent],
        (
            [(0, None, 0, 0), (1, None, SEG, 0)],
            [(2, 0, 0, 0), (3, 0, 0, half), (2, 1, SEG, 0), (3, 1, SEG, half)],
        ),
    )
    moving, done = {}, {}
    orders = {name: (0, *range(2, levels), 1) for name in ()}

    def send_on(name, send, keep, step):
        order = orders.get(name, tuple(range(levels)))
        moving[name] = (swap_bit(send, size, order[step]), keep, step)

    def halved(*names, estimate=SHORT):
        names = [name for name in names if name in moving]
        if not names:
            return
        which = []
        for name in names:
            step = moving[name][2] + 1
            which.append(None if step == levels else orders.get(name, tuple(range(levels)))[step])
        kept, got = [moving[name][1] for name in names], [moving[name][0] for name in names]
        made = halve(at_dp, which, kept, got, last[0], estimate)
        last[0] = [made[0][0]]
        for name, level, values in zip(names, which, made):
            if level is None:
                done[name] = values[0]
                moving.pop(name)
            else:
                send_on(name, *values, moving[name][2] + 1)

    def grads(names, groups, tasks, chunks, **more):
        places = [places_of(orders.get(name, tuple(range(levels))), size) for name in names]
        made = weight_grads(at_section, at_dp, size, groups, tasks, chunks, last[0], places, **more)
        last[0] = [made[0][0]]
        for name, (send, keep) in zip(names, made):
            send_on(name, send, keep, 0)

    eighth = WIDTH // 8
    grads(
        ("down0", "down1", "down2"),
        [[rows_of(saved["hidden"])], gy_all],
        [
            dict(
                left=(0, t),
                right=(1, 0),
                block=t,
                blocks=FF // WIDTH,
                outs=[(0, 0, 3 * eighth, 0), (1, 3 * eighth, 2 * eighth, 0), (2, 5 * eighth, 3 * eighth, 0)],
            )
            for t in range(FF // WIDTH)
        ],
        [(FF // WIDTH, 3 * eighth), (FF // WIDTH, 2 * eighth), (FF // WIDTH, 3 * eighth)],
    )
    halved("down0")
    halved("down1", "down2")
    fed = feed_back(1, [active[0]], ((back_b, None),), saved, params, fed, last[0])
    last[0] = [fed["d_down"]]
    halved("down0")

    up = jnp.sum(fed["d_up"], axis=(0, 1)).reshape(size, FF // size)
    down = jnp.sum(fed["d_down"], axis=(0, 1)).reshape(size, WIDTH // size)
    row = jnp.concatenate([up, down], axis=1).astype(BF)
    small = jnp.pad(row[:, None, :], ((0, 0), (0, 15), (0, WIDTH - row.shape[1])))
    ffn_in, d_hidden = [rows_of(saved["ffn_in"])], [rows_of(fed["d_hidden"])]
    grads(
        ("up0",),
        [ffn_in, d_hidden],
        [dict(left=(0, 0), right=(1, t), block=0, blocks=1, outs=[(0, 0, WIDTH, t * WIDTH)]) for t in range(2)],
        [(1, 2 * WIDTH)],
    )
    halved("down1", "down0")
    grads(
        ("up1", "out"),
        [ffn_in, d_hidden, [rows_of(saved["attended"])], [rows_of(fed["low"])]],
        [dict(left=(0, 0), right=(1, 2 + t), block=0, blocks=1, outs=[(0, 0, WIDTH, t * WIDTH)]) for t in range(2)]
        + [dict(left=(2, 0), right=(3, 0), block=0, blocks=1, outs=[(1, 0, WIDTH, 0)])],
        [(1, 2 * WIDTH), (1, WIDTH)],
        small=small,
        small_chunk=0,
    )
    halved("down2", "down1", "up0")
    dx_b0, made = attend_back(
        1, [active[0], reset_flags, boundary], saved, fed, kv_memory, params, made, last[0]
    )
    last[0] = [dx_b0]
    outputs = pick(at_section, other_y, saved["y_high"], last[0])
    last[0] = [outputs]
    halved("up0", "up1", "out", "down2", "down1", "down0")
    grads(
        ("key", "value", "query"),
        [
            [rows_of(saved["normed"]), rows_of(normed_memory)],
            [rows_of(made["dkx"]), rows_of(made["dkm"])],
            [rows_of(made["dvx"]), rows_of(made["dvm"])],
            [rows_of(saved["normed"])],
            [rows_of(made["dq"])],
        ],
        [
            dict(left=(0, 0), right=(1, 0), block=0, blocks=1, outs=[(0, 0, WIDTH, 0)]),
            dict(left=(0, 0), right=(2, 0), block=0, blocks=1, outs=[(1, 0, WIDTH, 0)]),
            dict(left=(3, 0), right=(4, 0), block=0, blocks=1, outs=[(2, 0, WIDTH, 0)]),
        ],
        [(1, WIDTH)] * 3,
    )
    halved("up1", estimate=LONG)
    halved("key", "value", "query")
    halved("out", "up0", "down2")
    grad_inputs = pick(at_section, made["dx_low"], one_way(made["dx_high"], 0, 1), last[0])
    last[0] = [grad_inputs]
    for names in (("key", "up1"), ("value", "key", "out", "up0"), ("query", "value", "up1", "out"), ("query", "key")):
        halved(*names)
    while any(step + 1 < levels for _, _, step in moving.values()):
        halved(*[name for name, (_, _, step) in moving.items() if step + 1 < levels])
    if "up1" in moving:
        halved("up1")
    rows = WIDTH // size
    own_gain = [
        lax.dynamic_slice_in_dim(gain, mine * rows, rows, 1).astype(F32) for gain in (gain_attn, gain_ffn)
    ]
    targets = dict(
        down0=(0, 0), down1=(0, 3 * eighth), down2=(0, 5 * eighth), up0=(1, 0), up1=(1, 2 * WIDTH), out=(2, 0),
        query=(3, 0), key=(3, WIDTH), value=(3, 2 * WIDTH),
    )
    names = list(targets)
    g_down, g_up, g_out, g_proj, g_b_up, g_b_down, g_gain_attn, g_gain_ffn = gather_up(
        at_dp,
        [targets[name] for name in names],
        [done[name] if name in done else moving[name][1] for name in names],
        [None if name in done else moving[name][0] for name in names],
        names.index("up1"),
        w_proj,
        w_up,
        own_gain,
        size,
        last[0],
    )
    keep_all = (1 - reset_flags).astype(BF)[:, None, None]
    new_compressed = jnp.concatenate([compressed[:, COMP:] * keep_all, squeezed], axis=1)
    return (
        outputs,
        grad_inputs,
        saved["x"][None],
        new_compressed[None],
        g_gain_attn,
        g_proj[None],
        g_out[None],
        g_gain_ffn,
        g_up[None],
        g_b_up,
        g_down[None],
        g_b_down,
    )


def solution(mesh):
    return jax.shard_map(
        body,
        mesh=mesh,
        in_specs=(
            P("dp", None, "section"),
            P("dp", None, "section"),
            P("section", "dp", None, None),
            P("section", "dp", None, None),
            P("dp"),
            P("dp"),
            P("section", None),
            P("section", None, None),
            P("section", None, None),
            P("section", None),
            P("section", None, None),
            P("section", None),
            P("section", None, None),
            P("section", None),
            P("section", None, None, None),
            P("section", None),
        ),
        out_specs=(
            P("dp", None, "section"),
            P("dp", None, "section"),
            P("section", "dp", None, None),
            P("section", "dp", None, None),
            P("section", "dp"),
            P("section", "dp", None),
            P("section", "dp", None),
            P("section", "dp"),
            P("section", "dp", None),
            P("section", "dp"),
            P("section", "dp", None),
            P("section", "dp"),
        ),
        check_vma=False,
    )
```

```python
import math

import jax
import jax.numpy as jnp
from jax import lax
from jax.experimental import pallas as pl
from jax.experimental.pallas import tpu as pltpu
from jax.sharding import PartitionSpec as P

WIDTH = 1024
HEADS = 8
HEAD = 128
FF = 4096
SEG = 512
MEM = 512
CMEM = 512
RATE = 2
COMP = 256
CTX = MEM + CMEM
HALF = SEG // 2
HP = 8

EPS = 1e-05
NEG = -1e30
ROOT_TWO_PI = 0.7978845608028654
SCALE = HEAD**-0.5
LOG2E = math.log2(math.e)
LN2 = math.log(2.0)
BF = jnp.bfloat16
F32 = jnp.float32
PARAMS = pltpu.CompilerParams(vmem_limit_bytes=56 << 20)


def nn(a, b):
    return lax.dot_general(a, b, (((1,), (0,)), ((), ())), preferred_element_type=F32)


def nt(a, b):
    return lax.dot_general(a, b, (((1,), (1,)), ((), ())), preferred_element_type=F32)


def tn(a, b):
    return lax.dot_general(a, b, (((0,), (0,)), ((), ())), preferred_element_type=F32)


def shape(dims, dtype=BF):
    return jax.ShapeDtypeStruct(dims, dtype)


def whole(*dims):
    return pl.BlockSpec(dims, lambda *_: (0,) * len(dims))


def cost(flops, moved, trans=0):
    return pl.CostEstimate(flops=int(flops), bytes_accessed=int(moved), transcendentals=int(trans))


LONG = cost(1e11, 1)
SHORT = cost(1, 1)


def normalise(values):
    centred = values - jnp.mean(values, axis=-1, keepdims=True)
    inverse = lax.rsqrt(jnp.mean(centred * centred, axis=-1, keepdims=True) + EPS)
    return centred * inverse, inverse


def norm_back(unit, inverse, gain, grad):
    scaled = grad * gain
    along = jnp.mean(scaled * unit, axis=-1, keepdims=True)
    return inverse * (scaled - jnp.mean(scaled, axis=-1, keepdims=True) - unit * along)


ANY = pl.BlockSpec(memory_space=pltpu.HBM)


def call(kernel, name, scalars, ins, outs, scratch, tokens, aliases=None, estimate=LONG, specs=None):
    first = len(scalars) + len(ins)

    def run(*refs):
        kernel(*refs[:first], *refs[first + len(tokens) :])

    return pl.pallas_call(
        run,
        name=name,
        grid_spec=pltpu.PrefetchScalarGridSpec(
            num_scalar_prefetch=len(scalars),
            grid=(1,),
            in_specs=list(specs or [ANY] * len(ins)) + [ANY] * len(tokens),
            out_specs=[ANY] * len(outs),
            scratch_shapes=scratch,
        ),
        out_shape=list(outs),
        input_output_aliases=aliases or {},
        compiler_params=PARAMS,
        cost_estimate=estimate,
    )(*scalars, *ins, *tokens)


class Copies:
    def __init__(self, sems):
        self.sems, self.count, self.named = sems, 0, {}

    def start(self, source, target, name=None):
        copy = pltpu.make_async_copy(source, target, self.sems.at[self.count])
        copy.start()
        self.named[name if name is not None else self.count] = copy
        self.count += 1

    def wait(self, *names):
        for name in names:
            self.named.pop(name).wait()

    def wait_all(self):
        for name in list(self.named):
            self.wait(name)


def tiles(ref, axis, size=1024):
    if axis == 0:
        return [ref.at[pl.ds(i * size, size)] for i in range(ref.shape[0] // size)]
    return [ref.at[:, pl.ds(i * size, size)] for i in range(ref.shape[1] // size)]


def memory_kernel(seq, flags, comp, mem, gain, w, normed, kv, rows, weights, unit_rows, out, sems):
    copies = Copies(sems)
    for n, source in enumerate((comp, mem)):
        copies.start(source.at[seq], rows.at[n], ("rows", n))
        copies.start(w.at[:, pl.ds((1 + n) * WIDTH, WIDTH)], weights.at[n], ("w", n))
    keep = (1 - flags[seq]).astype(F32)

    def unit(n):
        copies.wait(("rows", n))
        value, _ = normalise(rows[n].astype(F32) * keep)
        unit_rows[n] = (value * gain[...].astype(F32)).astype(BF)

    unit(0)
    for n in range(2):
        place = pl.ds(n * MEM, MEM)
        copies.start(unit_rows.at[n], normed.at[0, place])
        for t in range(2):
            if n == 0:
                copies.wait(("w", t))
            out[n, :, t * WIDTH : (t + 1) * WIDTH] = nn(unit_rows[n], weights[t]).astype(BF)
            if n == 0 and t == 0:
                unit(1)
        copies.start(out.at[n], kv.at[0, place])
    copies.wait_all()


def memory_keyvals(seq, flags, compressed, memory, gain, w_proj, tokens):
    return call(
        lambda *refs: memory_kernel(seq, *refs),
        "memory_keyvals",
        [flags],
        [compressed, memory, gain, w_proj],
        [shape((1, CTX, WIDTH)), shape((1, CTX, 2 * WIDTH))],
        [
            pltpu.VMEM((2, MEM, WIDTH), BF),
            pltpu.VMEM((2, WIDTH, WIDTH), BF),
            pltpu.VMEM((2, MEM, WIDTH), BF),
            pltpu.VMEM((2, MEM, 2 * WIDTH), BF),
            pltpu.SemaphoreType.DMA((8,)),
        ],
        tokens,
        specs=[ANY, ANY, whole(1, WIDTH), ANY],
    )


def fill_masks(flag, bound, bias, unseen):
    key = lax.broadcasted_iota(jnp.int32, (SEG, SEG), 0)
    query = lax.broadcasted_iota(jnp.int32, (SEG, SEG), 1)
    least = jnp.where(query >= bound, bound, 0)
    bias[...] = jnp.where((key <= query) & (key >= least), 0.0, NEG)
    position = lax.broadcasted_iota(jnp.int32, (1, SEG), 1)
    limit = jnp.where(flag == 0, bound, 0)
    unseen[...] = jnp.where(position < limit, 0.0, -NEG)


def gelu_parts(v):
    inner = v * (ROOT_TWO_PI + (0.044715 * ROOT_TWO_PI) * (v * v))
    t = jnp.tanh(inner)
    half = 0.5 + 0.5 * t
    slope = 3.0 * inner - (2.0 * ROOT_TWO_PI) * v
    return v * half, half + half * (1.0 - t) * slope


def attend_heads(first, qkv, kvm, attended, log_total, bias, unseen):
    def cols(base, h):
        return pl.ds(pl.multiple_of(base * WIDTH + (first + h) * HEAD, HEAD), HEAD)

    pieces = [(h, slice(part * HALF, (part + 1) * HALF), (part + 1) * HALF) for h in range(HP) for part in range(2)]

    def scores(h, r, count):
        rows = qkv[r, cols(0, h)]
        return nt(kvm[:, cols(0, h)], rows), nt(qkv[:count, cols(1, h)], rows) + bias[:count, r]

    def weights(h, r, count, on_memory, on_segment):
        hidden = unseen[:, r]
        top = jnp.maximum(
            jnp.max(on_memory, axis=0, keepdims=True) - hidden,
            jnp.max(on_segment, axis=0, keepdims=True),
        )
        p_memory = jnp.exp2(on_memory - (top + hidden))
        p_segment = jnp.exp2(on_segment - top)
        total = jnp.sum(p_memory, axis=0, keepdims=True) + jnp.sum(p_segment, axis=0, keepdims=True)
        log_total[first + h, :, r] = top + jnp.log2(total)
        return p_memory.astype(BF), p_segment.astype(BF), total

    values = {}

    def finish(h, r, count, p_memory, p_segment, total):
        if h not in values:
            values[h] = (kvm[:, cols(1, h)].T, qkv[:, cols(2, h)].T)
        turned = nn(values[h][0], p_memory) + nn(values[h][1][:, :count], p_segment)
        attended[r, cols(0, h)] = (turned * (1.0 / total)).T.astype(BF)

    held, ready = {}, {}
    for step in range(len(pieces) + 2):
        if step < len(pieces):
            held[step] = scores(*pieces[step])
        if 0 <= step - 1 < len(pieces):
            ready[step - 1] = weights(*pieces[step - 1], *held.pop(step - 1))
        if 0 <= step - 2 < len(pieces):
            finish(*pieces[step - 2], *ready.pop(step - 2))


SAVED = (
    ("x", (SEG, WIDTH), BF),
    ("normed", (SEG, WIDTH), BF),
    ("qkv", (SEG, 3 * WIDTH), BF),
    ("attended", (SEG, WIDTH), BF),
    ("log_total", (HEADS, 1, SEG), F32),
    ("residual", (SEG, WIDTH), F32),
    ("ffn_in", (SEG, WIDTH), BF),
    ("hidden", (SEG, FF), BF),
    ("gate", (SEG, FF), BF),
    ("y_low", (SEG, WIDTH // 2), BF),
    ("y_high", (SEG, WIDTH // 2), BF),
)
FS = 512


def forward_kernel(seq, parts, aliased, active, flags, bounds, *refs):
    xs, refs = refs[: len(parts)], refs[len(parts) :]
    (gain, w_proj, kv_memory, w_out, gain_ffn, w_up, b_up, w_down, b_down), refs = refs[:9], refs[9:]
    refs = refs[aliased:]
    y, refs = refs[0], refs[1:]
    out = dict(zip([name for name, _, _ in SAVED], refs))
    refs = refs[len(SAVED) :]
    held = dict(zip([name for name, _, _ in SAVED], refs))
    pool, kvm, wo, total, y_rows, bias, unseen, in_sems, out_sems, feed_sems = refs[len(SAVED) :]

    @pl.when(active[0] == 1)
    def _():
        loads, stores = Copies(in_sems), Copies(out_sems)

        def save(*names):
            for name in names:
                stores.start(held[name], out[name].at[seq])

        x = held["x"]
        for i, (part, lead) in enumerate(zip(xs, parts)):
            wide = WIDTH // len(parts)
            loads.start(part if lead is None else part.at[lead], x.at[:, pl.ds(i * wide, wide)], ("x", i))
        for t, tile in enumerate(tiles(w_proj, 1)):
            loads.start(tile, pool.at[t], ("proj", t))
        loads.start(kv_memory.at[0], kvm, "kvm")
        loads.start(w_out, wo, "out")
        for t, tile in enumerate(tiles(w_up, 1)):
            loads.start(tile, pool.at[4 + t], ("up", t))
        fill_masks(flags[seq], bounds[seq], bias, unseen)
        loads.wait(*[("x", i) for i in range(len(parts))])
        unit, _ = normalise(x[...].astype(F32))
        held["normed"][...] = (unit * gain[...].astype(F32)).astype(BF)
        for t in range(3):
            loads.wait(("proj", t))
            factor = SCALE * LOG2E if t == 0 else 1.0
            held["qkv"][:, t * WIDTH : (t + 1) * WIDTH] = (nn(held["normed"][...], pool[t]) * factor).astype(BF)
        for t, tile in enumerate(tiles(w_down, 0)):
            loads.start(tile, pool.at[t], ("down", t))
        save("x", "normed", "qkv")
        loads.wait("kvm")

        def heads(g, _):
            attend_heads(g * HP, held["qkv"], kvm, held["attended"], held["log_total"], bias, unseen)
            return 0

        lax.fori_loop(0, HEADS // HP, heads, 0)
        save("attended", "log_total")
        loads.wait("out")
        rows = x[...].astype(F32) + nn(held["attended"][...], wo[...])
        held["residual"][...] = rows
        unit, _ = normalise(rows)
        held["ffn_in"][...] = (unit * gain_ffn[...].astype(F32)).astype(BF)
        save("residual", "ffn_in")
        total[...] = rows + b_down[...].astype(F32)
        loads.wait_all()

        def feed(t, _):
            cuts = [pl.ds(t * 1024 + i * FS, FS) for i in range(1024 // FS)]
            ups = [
                nn(held["ffn_in"][...], pool[4 + t, :, i * FS : (i + 1) * FS]) + b_up[:, c].astype(F32)
                for i, c in enumerate(cuts)
            ]
            added = None
            for i, (c, up) in enumerate(zip(cuts, ups)):
                value, slope = gelu_parts(up)
                value = value.astype(BF)
                held["hidden"][:, c] = value
                held["gate"][:, c] = slope.astype(BF)
                part = nn(value, pool[t, i * FS : (i + 1) * FS])
                added = part if added is None else added + part
            total[...] += added
            for name, sem in (("hidden", 0), ("gate", 1)):
                feed_copy(name, sem, t).start()
            return 0

        def feed_copy(name, sem, t):
            place = pl.ds(t * 1024, 1024)
            return pltpu.make_async_copy(held[name].at[:, place], out[name].at[seq, :, place], feed_sems.at[sem, t])

        for t in range(FF // 1024):
            feed(t, 0)
        rows = total[...].astype(BF)
        y_rows[...] = rows
        held["y_low"][...] = rows[:, : WIDTH // 2]
        held["y_high"][...] = rows[:, WIDTH // 2 :]
        stores.start(y_rows, y)
        save("y_low", "y_high")
        for t in range(FF // 1024):
            feed_copy("hidden", 0, t).wait()
            feed_copy("gate", 1, t).wait()
        stores.wait_all()


def forward(seq, seqs, scalars, xs, kv_memory, params, saved, tokens, estimate):
    gain_attn, w_proj, w_out, gain_ffn, w_up, b_up, w_down, b_down = params
    args = [v for v, _ in xs] + [gain_attn, w_proj, kv_memory, w_out, gain_ffn, w_up, b_up, w_down, b_down]
    specs = [ANY] * len(xs) + [
        whole(1, WIDTH), ANY, ANY, ANY, whole(1, WIDTH), ANY, whole(1, FF), ANY, whole(1, WIDTH)
    ]
    aliases = {}
    if saved is not None:
        aliases = {len(scalars) + len(args) + i: 1 + i for i in range(len(SAVED))}
        args += [saved[name] for name, _, _ in SAVED]
        specs += [ANY] * len(SAVED)
    leads = [lead for _, lead in xs]
    results = call(
        lambda *refs: forward_kernel(seq, leads, len(aliases), *refs),
        "forward",
        scalars,
        args,
        [shape((SEG, WIDTH))] + [shape((seqs,) + dims, dtype) for _, dims, dtype in SAVED],
        [pltpu.VMEM(dims, dtype) for _, dims, dtype in SAVED]
        + [
            pltpu.VMEM((8, WIDTH, WIDTH), BF),
            pltpu.VMEM((CTX, 2 * WIDTH), BF),
            pltpu.VMEM((WIDTH, WIDTH), BF),
            pltpu.VMEM((SEG, WIDTH), F32),
            pltpu.VMEM((SEG, WIDTH), BF),
            pltpu.VMEM((SEG, SEG), F32),
            pltpu.VMEM((1, SEG), F32),
            pltpu.SemaphoreType.DMA((16,)),
            pltpu.SemaphoreType.DMA((14,)),
            pltpu.SemaphoreType.DMA((2, FF // 1024)),
        ],
        tokens,
        aliases,
        estimate,
        specs,
    )
    return results[0], dict(zip([name for name, _, _ in SAVED], results[1:]))


FED = (
    ("d_hidden", (SEG, FF), BF),
    ("d_residual", (SEG, WIDTH), F32),
    ("low", (SEG, WIDTH), BF),
    ("d_attended", (SEG, WIDTH), BF),
    ("d_up", (1, FF), F32),
    ("d_down", (1, WIDTH), F32),
)


def feed_back_kernel(seq, leads, aliased, active, *refs):
    gys, refs = refs[: len(leads)], refs[len(leads) :]
    (w_down, gate, w_up, residual, gain, w_out), refs = refs[:6], refs[6:]
    refs = refs[aliased:]
    out = dict(zip([name for name, _, _ in FED], refs))
    refs = refs[len(FED) :]
    held = dict(zip([name for name, _, _ in FED], refs))
    gy_rows, pool, gates, rows, wo, total, in_sems, out_sems = refs[len(FED) :]

    @pl.when(active[0] == 1)
    def _():
        loads, stores = Copies(in_sems), Copies(out_sems)
        for i, (part, (lead, row, column)) in enumerate(zip(gys, leads)):
            source = part if lead is None else part.at[lead]
            tall, wide = source.shape
            loads.start(source, gy_rows.at[pl.ds(row, tall), pl.ds(column, wide)], ("gy", i))
        downs, ups = tiles(w_down, 0), tiles(w_up, 1)
        for t in range(FF // 1024):
            loads.start(downs[t], pool.at[t], ("down", t))
            loads.start(gate.at[seq, :, pl.ds(t * 1024, 1024)], gates.at[:, pl.ds(t * 1024, 1024)], ("gate", t))
            loads.start(ups[t], pool.at[4 + t], ("up", t))
        loads.start(residual.at[seq], rows, "rows")
        loads.start(w_out, wo, "out")
        loads.wait(*[("gy", i) for i in range(len(leads))])
        held["d_down"][...] = jnp.sum(gy_rows[...].astype(F32), axis=0, keepdims=True)
        for t in range(FF // 1024):
            loads.wait(("down", t), ("gate", t), ("up", t))
            raws = [nt(gy_rows[...], pool[t, i * FS : (i + 1) * FS]) for i in range(1024 // FS)]
            added = None
            for i, raw in enumerate(raws):
                c = slice(t * 1024 + i * FS, t * 1024 + (i + 1) * FS)
                value = (raw * gates[:, c].astype(F32)).astype(BF)
                held["d_hidden"][:, c] = value
                held["d_up"][:, c] = jnp.sum(value.astype(F32), axis=0, keepdims=True)
                part = nt(value, pool[4 + t, :, i * FS : (i + 1) * FS])
                added = part if added is None else added + part
            total[...] = added if t == 0 else total[...] + added
        for name in ("d_hidden", "d_up", "d_down"):
            stores.start(held[name], out[name].at[seq])
        loads.wait("rows", "out")
        unit, inverse = normalise(rows[...])
        grad = gy_rows[...].astype(F32) + norm_back(unit, inverse, gain[...].astype(F32), total[...])
        held["d_residual"][...] = grad
        held["low"][...] = grad.astype(BF)
        held["d_attended"][...] = nt(held["low"][...], wo[...]).astype(BF)
        for name in ("d_residual", "low", "d_attended"):
            stores.start(held[name], out[name].at[seq])
        stores.wait_all()


def feed_back(seq, scalars, gys, saved, params, fed, tokens, estimate=LONG):
    gain_attn, w_proj, w_out, gain_ffn, w_up, b_up, w_down, b_down = params
    seqs = saved["gate"].shape[0]
    args = [v for v, *_ in gys] + [w_down, saved["gate"], w_up, saved["residual"], gain_ffn, w_out]
    specs = [ANY] * (len(gys) + 4) + [whole(1, WIDTH), ANY]
    aliases = {}
    if fed is not None:
        aliases = {len(scalars) + len(args) + i: i for i in range(len(FED))}
        args += [fed[name] for name, _, _ in FED]
        specs += [ANY] * len(FED)
    leads = [place for _, *place in gys]
    results = call(
        lambda *refs: feed_back_kernel(seq, leads, len(aliases), *refs),
        "feed_back",
        scalars,
        args,
        [shape((seqs,) + dims, dtype) for _, dims, dtype in FED],
        [pltpu.VMEM(dims, dtype) for _, dims, dtype in FED]
        + [
            pltpu.VMEM((SEG, WIDTH), BF),
            pltpu.VMEM((8, WIDTH, WIDTH), BF),
            pltpu.VMEM((SEG, FF), BF),
            pltpu.VMEM((SEG, WIDTH), F32),
            pltpu.VMEM((WIDTH, WIDTH), BF),
            pltpu.VMEM((SEG, WIDTH), F32),
            pltpu.SemaphoreType.DMA((16,)),
            pltpu.SemaphoreType.DMA((8,)),
        ],
        tokens,
        aliases,
        estimate,
        specs,
    )
    return dict(zip([name for name, _, _ in FED], results))


MADE = (
    ("dq", (SEG, WIDTH), BF),
    ("dkx", (SEG, WIDTH), BF),
    ("dvx", (SEG, WIDTH), BF),
    ("dkm", (CTX, WIDTH), BF),
    ("dvm", (CTX, WIDTH), BF),
    ("dx_low", (SEG, WIDTH // 2), BF),
    ("dx_high", (SEG, WIDTH // 2), BF),
)
GROUP = 2


def attend_back_heads(first, qkv, kvm, d_out, out, log_total, made, bias, unseen):
    every, low, high = slice(0, SEG), slice(0, HALF), slice(HALF, SEG)

    def cols(base, h):
        return pl.ds(pl.multiple_of(base * WIDTH + (first + h) * HEAD, HEAD), HEAD)

    for h in range(GROUP):
        c = cols(0, h)
        qh, gh = qkv[:, c], d_out[:, c]
        inner = jnp.sum((gh.astype(F32) * out[:, c].astype(F32)).T, axis=0, keepdims=True)
        level = log_total[first + h]

        def piece(k, v, r, mask):
            logits = nt(k, qh[r])
            if mask is None:
                p = jnp.exp2(logits - (level[:, r] + unseen[:, r]))
            else:
                p = jnp.exp2(logits + mask - level[:, r])
            ds = (p * (nt(v, gh[r]) - inner[:, r])).astype(BF)
            return p.astype(BF), ds

        km, vm, kx, vx = kvm[:, c], kvm[:, cols(1, h)], qkv[:, cols(1, h)], qkv[:, cols(2, h)]
        p_memory, ds_memory = piece(km, vm, every, None)
        p_low, ds_low = piece(kx[low], vx[low], every, bias[low, :])
        p_high, ds_high = piece(kx[high], vx[high], high, bias[high, high])
        made["dvm"][:, c] = nn(p_memory, gh).astype(BF)
        made["dkm"][:, c] = (nn(ds_memory, qh) * LN2).astype(BF)
        made["dvx"][low, c] = nn(p_low, gh).astype(BF)
        made["dkx"][low, c] = (nn(ds_low, qh) * LN2).astype(BF)
        made["dvx"][high, c] = nn(p_high, gh[high]).astype(BF)
        made["dkx"][high, c] = (nn(ds_high, qh[high]) * LN2).astype(BF)
        turned = kx.T
        both = nn(km.T, ds_memory) + nn(turned[:, low], ds_low)
        made["dq"][low, c] = (both[:, low] * SCALE).T.astype(BF)
        made["dq"][high, c] = ((both[:, high] + nn(turned[:, high], ds_high)) * SCALE).T.astype(BF)


def attend_back_kernel(seq, part, aliased, active, flags, bounds, *refs):
    (qkv_in, kv_memory, d_out_in, out_in, stat_in, w_proj, x_in, gain, d_residual), refs = refs[:9], refs[9:]
    refs = refs[aliased:]
    dx, refs = refs[0], refs[1:]
    result = dict(zip([name for name, _, _ in MADE], refs))
    refs = refs[len(MADE) :]
    made = dict(zip([name for name, _, _ in MADE], refs))
    refs = refs[len(MADE) :]
    qkv, kvm, d_out, out, log_total, pool, x, rows, dx_rows, bias, unseen, in_sems, head_sems, out_sems = refs

    @pl.when(active[0] == 1)
    def _():
        loads, stores = Copies(in_sems), Copies(out_sems)
        wide = GROUP * HEAD
        count = WIDTH // wide

        def head_copies(g):
            g = g * wide if isinstance(g, int) else pl.multiple_of(g * wide, wide)
            sems = head_sems.at[g // wide]
            pairs = [
                (ref.at[lead, :, pl.ds(base * WIDTH + g, wide)], target.at[:, pl.ds(base * WIDTH + g, wide)])
                for ref, lead, target, bases in (
                    (qkv_in, seq, qkv, 3),
                    (kv_memory, 0, kvm, 2),
                    (d_out_in, seq, d_out, 1),
                    (out_in, seq, out, 1),
                )
                for base in range(bases)
            ]
            return [pltpu.make_async_copy(a, b, sems.at[i]) for i, (a, b) in enumerate(pairs)]

        loads.start(stat_in.at[seq], log_total, "stat")
        for g in range(count):
            for copy in head_copies(g):
                copy.start()
        for t, tile in enumerate(tiles(w_proj, 1)):
            loads.start(tile, pool.at[t])
        loads.start(x_in.at[seq], x)
        loads.start(d_residual.at[seq], rows)
        fill_masks(flags[seq], bounds[seq], bias, unseen)
        loads.wait("stat")

        def heads(g, _):
            for copy in head_copies(g):
                copy.wait()
            attend_back_heads(g * GROUP, qkv, kvm, d_out, out, log_total, made, bias, unseen)
            return 0

        lax.fori_loop(0, count, heads, 0)
        for name, _, _ in MADE[:5]:
            stores.start(made[name], result[name].at[seq])
        loads.wait_all()
        top = slice(0, part)
        grad = nt(made["dq"][top], pool[0]) + nt(made["dkx"][top], pool[1]) + nt(made["dvx"][top], pool[2])
        unit, inverse = normalise(x[top].astype(F32))
        value = (rows[top] + norm_back(unit, inverse, gain[...].astype(F32), grad)).astype(BF)
        dx_rows[top] = value
        stores.start(dx_rows.at[pl.ds(0, part)], dx)
        if part == SEG:
            made["dx_low"][...] = value[:, : WIDTH // 2]
            made["dx_high"][...] = value[:, WIDTH // 2 :]
            for name, _, _ in MADE[5:]:
                stores.start(made[name], result[name].at[seq])
        stores.wait_all()


def attend_back(seq, scalars, saved, fed, kv_memory, params, made, tokens, estimate=LONG, part=SEG):
    gain_attn, w_proj, w_out, gain_ffn, w_up, b_up, w_down, b_down = params
    seqs = saved["qkv"].shape[0]
    args = [
        saved["qkv"],
        kv_memory,
        fed["d_attended"],
        saved["attended"],
        saved["log_total"],
        w_proj,
        saved["x"],
        gain_attn,
        fed["d_residual"],
    ]
    specs = [ANY] * 7 + [whole(1, WIDTH), ANY]
    aliases = {}
    if made is not None:
        aliases = {len(scalars) + len(args) + i: 1 + i for i in range(len(MADE))}
        args += [made[name] for name, _, _ in MADE]
        specs += [ANY] * len(MADE)
    results = call(
        lambda *refs: attend_back_kernel(seq, part, len(aliases), *refs),
        "attend_back",
        scalars,
        args,
        [shape((part, WIDTH))] + [shape((seqs,) + dims, dtype) for _, dims, dtype in MADE],
        [pltpu.VMEM(dims, dtype) for _, dims, dtype in MADE]
        + [
            pltpu.VMEM((SEG, 3 * WIDTH), BF),
            pltpu.VMEM((CTX, 2 * WIDTH), BF),
            pltpu.VMEM((SEG, WIDTH), BF),
            pltpu.VMEM((SEG, WIDTH), BF),
            pltpu.VMEM((HEADS, 1, SEG), F32),
            pltpu.VMEM((3, WIDTH, WIDTH), BF),
            pltpu.VMEM((SEG, WIDTH), BF),
            pltpu.VMEM((SEG, WIDTH), F32),
            pltpu.VMEM((SEG, WIDTH), BF),
            pltpu.VMEM((SEG, SEG), F32),
            pltpu.VMEM((1, SEG), F32),
            pltpu.SemaphoreType.DMA((8,)),
            pltpu.SemaphoreType.DMA((WIDTH // (GROUP * HEAD), 7)),
            pltpu.SemaphoreType.DMA((8,)),
        ],
        tokens,
        aliases,
        estimate,
        specs,
    )
    return results[0], dict(zip([name for name, _, _ in MADE], results[1:]))


def project_back_kernel(seq, active, dq, dkx, dvx, w_proj, x, gain, d_residual, dx, grads, pool, xs, rows, dx_rows, sems):
    @pl.when(active[0] == 1)
    def _():
        copies = Copies(sems)
        place = pl.ds(SEG - HALF, HALF)
        for n, (ref, tile) in enumerate(zip((dq, dkx, dvx), tiles(w_proj, 1))):
            copies.start(ref.at[seq, place], grads.at[n], ("grad", n))
            copies.start(tile, pool.at[n], ("w", n))
        copies.start(x.at[seq, place], xs, "x")
        copies.start(d_residual.at[seq, place], rows, "rows")
        grad = None
        for n in range(3):
            copies.wait(("grad", n), ("w", n))
            term = nt(grads[n], pool[n])
            grad = term if grad is None else grad + term
        copies.wait_all()
        unit, inverse = normalise(xs[...].astype(F32))
        dx_rows[...] = (rows[...] + norm_back(unit, inverse, gain[...].astype(F32), grad)).astype(BF)
        copies.start(dx_rows, dx)
        copies.wait_all()


def project_back(seq, scalars, saved, fed, params, made, tokens):
    gain_attn, w_proj = params[:2]
    return call(
        lambda *refs: project_back_kernel(seq, *refs),
        "project_back",
        scalars,
        [made["dq"], made["dkx"], made["dvx"], w_proj, saved["x"], gain_attn, fed["d_residual"]],
        [shape((HALF, WIDTH))],
        [
            pltpu.VMEM((3, HALF, WIDTH), BF),
            pltpu.VMEM((3, WIDTH, WIDTH), BF),
            pltpu.VMEM((HALF, WIDTH), BF),
            pltpu.VMEM((HALF, WIDTH), F32),
            pltpu.VMEM((HALF, WIDTH), BF),
            pltpu.SemaphoreType.DMA((9,)),
        ],
        tokens,
        estimate=LONG,
        specs=[ANY] * 5 + [whole(1, WIDTH), ANY],
    )[0]


def compress_kernel(flags, grouped, w, bias, out, rows, weights, result, sems):
    copies = Copies(sems)
    copies.start(grouped, rows, "rows")
    copies.start(w, weights, "w")
    copies.wait("rows", "w")
    for s in range(rows.shape[0]):
        keep = (1 - flags[s]).astype(BF)
        result[s] = (nn(rows[s] * keep, weights[...]) + bias[...].astype(F32)).astype(BF)
        copies.start(result.at[s], out.at[s])
    copies.wait_all()


def compress(flags, memory, w_compress, b_compress, tokens):
    seqs = memory.shape[0]
    wide = RATE * WIDTH
    grouped = memory.reshape(seqs, COMP, wide)
    return list(
        call(
            compress_kernel,
            "compress",
            [flags],
            [grouped, w_compress.reshape(wide, WIDTH), b_compress],
            [shape((seqs, COMP, WIDTH))],
            [
                pltpu.VMEM((seqs, COMP, wide), BF),
                pltpu.VMEM((wide, WIDTH), BF),
                pltpu.VMEM((seqs, COMP, WIDTH), BF),
                pltpu.SemaphoreType.DMA((2 + seqs,)),
            ],
            tokens,
            estimate=SHORT,
            specs=[ANY, ANY, whole(1, WIDTH)],
        )
    )


WIDE = 512


def places_of(order, size):
    rest, place = order[1:], {}
    for index in range(size):
        place[index] = sum(((index >> b) & 1) << (len(rest) - 1 - n) for n, b in enumerate(rest))
    return place


class Either(list):
    def __init__(self, arrays, places):
        super().__init__((v, None) for v in arrays)
        self.places = places


def either_copies(group, refs, target, sems, base):
    made = []
    for wanted, places in enumerate(group.places):
        copies = []
        for n, (k, lead, row, column) in enumerate(places):
            source = refs[k] if lead is None else refs[k].at[lead]
            rows, columns = source.shape
            to = target.at[pl.ds(row, rows), pl.ds(column, columns)]
            copies.append(pltpu.make_async_copy(source, to, sems.at[base + n]))
        made.append((wanted, copies))
    return made


class Sides:
    def __init__(self, groups, tasks, ins, held, section, loads):
        self.groups, self.held, self.section, self.loads = groups, held, section, loads
        self.parts, self.either, self.ready, at = [], {}, set(), 0
        for g in groups:
            self.parts.append(ins[at : at + len(g)])
            at += len(g)
        for key in dict.fromkeys(k for t in tasks for k in (t["left"], t["right"])):
            g, tile = key
            if isinstance(groups[g], Either):
                choices = either_copies(groups[g], self.parts[g], held[g], loads.sems, loads.count)
                for wanted, copies in choices:
                    pl.when(section[0] == wanted)(lambda copies=copies: [c.start() for c in copies] and None)
                self.either[g] = choices
                loads.count += max(len(copies) for _, copies in choices)
                continue
            place, row = pl.ds(tile * 1024, 1024), 0
            for n, (ref, (_, lead)) in enumerate(zip(self.parts[g], groups[g])):
                rows = ref.shape[-2]
                source = ref.at[:, place] if lead is None else ref.at[lead, :, place]
                loads.start(source, held[g].at[pl.ds(row, rows), place], key + (n,))
                row += rows

    def wait(self, task):
        for key in (task["left"], task["right"]):
            if key in self.ready:
                continue
            self.ready.add(key)
            if key[0] in self.either:
                for wanted, copies in self.either[key[0]]:
                    pl.when(self.section[0] == wanted)(lambda copies=copies: [c.wait() for c in copies] and None)
            else:
                self.loads.wait(*[key + (m,) for m in range(len(self.parts[key[0]]))])

    def product(self, task, first, width):
        (left, lt), (right, rt) = task["left"], task["right"]
        return tn(
            self.held[left][:, lt * 1024 : (lt + 1) * 1024],
            self.held[right][:, rt * 1024 + first : rt * 1024 + first + width],
        )


def side_buffers(groups):
    made = []
    for g in groups:
        if isinstance(g, Either):
            made.append(pltpu.VMEM((SEG, WIDTH), BF))
        else:
            made.append(pltpu.VMEM((sum(v.shape[-2] for v, _ in g), g[0][0].shape[-1]), BF))
    return made, sum(len(g) * max(1, g[0][0].shape[-1] // 1024) for g in groups)


def early_kernel(groups, jobs, outs, section, *refs):
    total = sum(len(g) for g in groups)
    ins, refs = refs[:total], refs[total:]
    outs, refs = refs[:outs], refs[outs:]
    held, (staged, side_sems, out_sems) = refs[: len(groups)], refs[len(groups) :]
    parts, at = [], 0
    for g in groups:
        parts.append(ins[at : at + len(g)])
        at += len(g)
    first, used = {}, 0
    for g, group in enumerate(groups):
        first[g] = used
        used += len(group) * max(1, held[g].shape[1] // 1024)

    def place(t):
        return pl.ds(t * 1024 if isinstance(t, int) else pl.multiple_of(t * 1024, 1024), 1024)

    def side(g, t, act):
        if isinstance(groups[g], Either):
            for wanted, copies in either_copies(groups[g], parts[g], held[g], side_sems, first[g]):
                pl.when(section[0] == wanted)(lambda copies=copies: [act(c) for c in copies] and None)
            return
        row, many = 0, held[g].shape[1] // 1024
        for n, (ref, (_, lead)) in enumerate(zip(parts[g], groups[g])):
            rows = ref.shape[-2]
            sem = side_sems.at[first[g] + n * many + t]
            target = held[g].at[pl.ds(row, rows), place(t)]
            act(pltpu.make_async_copy(ref.at[lead, :, place(t)], target, sem))
            row += rows

    begin, end = (lambda copy: copy.start()), (lambda copy: copy.wait())
    done = set()
    for job in jobs:
        for key, loops in ((job["left"], job["loop"] == "left"), (job["right"], job["loop"] == "right")):
            if key in done:
                continue
            done.add(key)
            for t in range(job["count"]) if loops else [0]:
                side(key, t, begin)

    n, done = 0, set()
    for job in jobs:
        left, right, loop = job["left"], job["right"], job["loop"]
        for key, loops in ((left, loop == "left"), (right, loop == "right")):
            if not loops and key not in done:
                done.add(key)
                side(key, 0, end)

        def store(t, slot, job=job):
            row, column = job["at"]
            if loop == "left":
                row += t * 1024
            elif loop == "right":
                column += t * 1024
            if not isinstance(t, int):
                row, column = pl.multiple_of(row, 1024), pl.multiple_of(column, 1024)
            target = outs[job["out"]].at[pl.ds(row, 1024), pl.ds(column, 1024)]
            return pltpu.make_async_copy(staged.at[slot], target, out_sems.at[slot])

        def step(t, _, job=job, base=n):
            slot = (base + t) % 2
            if loop is not None:
                side(left if loop == "left" else right, t, end)
            lt, rt = (t if loop == "left" else 0), (t if loop == "right" else 0)

            @pl.when(base + t >= 2)
            def _():
                store(t, slot).wait()

            product = tn(held[left][:, place(lt)], held[right][:, place(rt)])
            staged[slot] = product.astype(BF)
            store(t, slot).start()
            return 0

        if job["count"] == 1:
            step(0, 0)
        else:
            lax.fori_loop(0, job["count"], step, 0)
        n += job["count"]
    for slot in range(2):
        pltpu.make_async_copy(staged.at[slot], outs[0].at[pl.ds(0, 1024), pl.ds(0, 1024)], out_sems.at[slot]).wait()


def early_grads(section, groups, jobs, outs, tokens):
    buffers, loads = side_buffers(groups)
    return list(
        call(
            lambda *refs: early_kernel(groups, jobs, len(outs), *refs),
            "early_grads",
            [section],
            [v for g in groups for v, _ in g],
            [shape(dims) for dims in outs],
            buffers
            + [
                pltpu.VMEM((2, 1024, 1024), BF),
                pltpu.SemaphoreType.DMA((loads,)),
                pltpu.SemaphoreType.DMA((2,)),
            ],
            tokens,
            estimate=SHORT,
        )
    )


def unset(dims, tokens):
    def kernel(*refs):
        pass

    return list(call(kernel, "unset", [], [], [shape(d) for d in dims], [], tokens, estimate=SHORT))


def weight_kernel(size, groups, tasks, chunks, places, small_chunk, bases, section, mine, *refs):
    total = sum(len(g) for g in groups)
    ins, base, refs = refs[:total], refs[total : total + 2 * bases], refs[total + 2 * bases :]
    if small_chunk is not None:
        small, refs = refs[0], refs[1:]
    sends, refs = refs[: len(chunks)], refs[len(chunks) :]
    keeps, refs = refs[: len(chunks)], refs[len(chunks) :]
    held, refs = refs[: len(groups)], refs[len(groups) :]
    staged, small_rows, so_far, in_sems, out_sems, base_sems = refs
    loads, stores = Copies(in_sems), Copies(out_sems)
    even = (mine[0] & 1) == 0
    sides = Sides(groups, tasks, ins, held, section, loads)

    def base_copy(n, which=0):
        k, row, column = tasks[n]["base"]
        source = base[k + which * bases].at[pl.ds(row, 1024), pl.ds(column, 1024)]
        return pltpu.make_async_copy(source, so_far.at[n % 2], base_sems.at[n % 2])

    def begin_base(n):
        for which in range(2):
            pl.when(section[0] == which)(lambda which=which: base_copy(n, which).start())

    begin_base(0)
    if small_chunk is not None:
        for pair in range(size // 2):
            place = places[small_chunk][2 * pair]
            one, two = small[2 * pair], small[2 * pair + 1]
            small_rows[0, place] = jnp.where(even, two, one)
            small_rows[1, place] = jnp.where(even, one, two)
        for i, target in enumerate((sends, keeps)):
            rows = target[small_chunk].shape[1] - 16
            stores.start(
                small_rows.at[i], target[small_chunk].at[:, pl.ds(rows, 16), pl.ds(0, WIDTH)], ("small", i)
            )

    busy = {}
    for n, task in enumerate(tasks):
        slot = n % 2
        sides.wait(task)
        for name in busy.pop(slot, ()):
            stores.wait(name)
        base_copy(n).wait()
        if n + 1 < len(tasks):
            begin_base(n + 1)
        count = size // task["blocks"]
        rows = 1024 // count
        for cut in range(1024 // WIDE):
            c = slice(cut * WIDE, (cut + 1) * WIDE)
            value = (sides.product(task, cut * WIDE, WIDE) + so_far[slot, :, c].astype(F32)).astype(BF)
            for pair in range(count // 2):
                one = value[(2 * pair) * rows : (2 * pair + 1) * rows]
                two = value[(2 * pair + 1) * rows : (2 * pair + 2) * rows]
                staged[slot, 0, pair, :, c] = jnp.where(even, two, one)
                staged[slot, 1, pair, :, c] = jnp.where(even, one, two)
        names = []
        for k, first, width, start in task["outs"]:
            for i, target in enumerate((sends, keeps)):
                for pair in range(count // 2):
                    names.append((n, k, i, pair))
                    stores.start(
                        staged.at[slot, i, pair, :, pl.ds(first, width)],
                        target[k].at[places[k][task["block"] * count + 2 * pair], pl.ds(0, rows), pl.ds(start, width)],
                        names[-1],
                    )
        busy[slot] = names
    stores.wait_all()


def weight_grads(
    section, mine, size, groups, bases, tasks, chunks, tokens, places, small=None, small_chunk=None, estimate=LONG
):
    outs = []
    for k, (blocks, columns) in enumerate(chunks):
        rows = blocks * 1024 // size + (16 if k == small_chunk else 0)
        outs.append(shape((size // 2, rows, columns)))
    args = [v for g in groups for v, _ in g] + [v for side in zip(*bases) for v in side]
    args += [small] if small is not None else []
    specs = [ANY] * (sum(len(g) for g in groups) + 2 * len(bases)) + ([whole(*small.shape)] if small is not None else [])
    count = size // tasks[0]["blocks"]
    buffers, loads = side_buffers(groups)
    results = call(
        lambda *refs: weight_kernel(size, groups, tasks, chunks, places, small_chunk, len(bases), *refs),
        "weight_grads",
        [section, mine],
        args,
        outs + outs,
        buffers
        + [
            pltpu.VMEM((2, 2, count // 2, 1024 // count, 1024), BF),
            pltpu.VMEM((2, size // 2, 16, WIDTH), BF),
            pltpu.VMEM((2, 1024, 1024), BF),
            pltpu.SemaphoreType.DMA((loads,)),
            pltpu.SemaphoreType.DMA((2 + sum(count * len(t["outs"]) for t in tasks),)),
            pltpu.SemaphoreType.DMA((2,)),
        ],
        tokens,
        estimate=estimate,
        specs=specs,
    )
    return list(zip(results[: len(chunks)], results[len(chunks) :]))


def halve_kernel(levels, mine, *refs):
    total = len(levels)
    kept, got, refs = refs[:total], refs[total : 2 * total], refs[2 * total :]
    outs = []
    for level in levels:
        outs.append(refs[: 1 if level is None else 2])
        refs = refs[len(outs[-1]) :]
    held, came, refs = refs[:total], refs[total : 2 * total], refs[2 * total :]
    wide, refs = refs[:-2], refs[-2:]
    loads, stores = Copies(refs[0]), Copies(refs[1])
    wide = list(wide)
    for n, level in enumerate(levels):
        if level is None:
            loads.start(kept[n], held[n], (n, 0, 0))
            loads.start(got[n], came[n], (n, 0, 1))
            continue
        half = kept[n].shape[0] // 2
        bit = (mine[0] >> level) & 1
        for j, which in enumerate((1 - bit, bit)):
            place = pl.ds(which * half, half)
            loads.start(kept[n].at[place], held[n].at[j], (n, j, 0))
            loads.start(got[n].at[place], came[n].at[j], (n, j, 1))
    for n, level in enumerate(levels):
        if level is None:
            total_rows = wide.pop(0)
            loads.wait((n, 0, 0), (n, 0, 1))
            total_rows[...] = held[n][0].astype(F32) + came[n][0].astype(F32)
            stores.start(total_rows, outs[n][0])
            continue
        for j, target in enumerate(outs[n]):
            loads.wait((n, j, 0), (n, j, 1))
            held[n][j] = held[n][j] + came[n][j]
            stores.start(held[n].at[j], target)
    stores.wait_all()


def halve(mine, levels, kept, got, tokens, estimate):
    total = len(kept)
    outs, held, wide = [], [], []
    for level, v in zip(levels, kept):
        if level is None:
            outs.append(shape(v.shape[1:], F32))
            wide.append(pltpu.VMEM(v.shape[1:], F32))
            held.append(pltpu.VMEM(v.shape, BF))
        else:
            half = (v.shape[0] // 2,) + v.shape[1:]
            outs += [shape(half)] * 2
            held.append(pltpu.VMEM((2,) + half, BF))
    results = call(
        lambda *refs: halve_kernel(levels, *refs),
        "halve",
        [mine],
        [*kept, *got],
        outs,
        held
        + held
        + wide
        + [pltpu.SemaphoreType.DMA((4 * total,)), pltpu.SemaphoreType.DMA((2 * total,))],
        tokens,
        estimate=estimate,
    )
    results, made = list(results), []
    for level in levels:
        made.append([results.pop(0) for _ in range(1 if level is None else 2)])
    return made


def gather_kernel(targets, ready, small, mine, *refs):
    total = len(targets)
    late = [n for n in range(total) if not ready[n]]
    kept, refs = refs[:total], refs[total:]
    got, refs = dict(zip(late, refs)), refs[len(late) :]
    (w_proj, w_up, gain_attn, gain_ffn), outs, refs = refs[:4], refs[4:12], refs[12:]
    held, refs = dict(zip(late, refs)), refs[len(late) :]
    came, refs = dict(zip(late, refs)), refs[len(late) :]
    sums, (small_rows, b_up, b_down, proj_rows, up_rows, gains), (in_sems, out_sems) = refs[:4], refs[4:10], refs[10:]
    loads, stores = Copies(in_sems), Copies(out_sems)
    rows = proj_rows.shape[0]
    for n, (k, first) in enumerate(targets):
        if ready[n]:
            place = sums[k].at[:, pl.ds(first, kept[n].shape[1])]
            if n == small:
                loads.start(kept[n].at[pl.ds(0, rows)], place, ("sum", n))
                loads.start(kept[n].at[pl.ds(rows, 16), pl.ds(0, WIDTH)], small_rows, "small")
            else:
                loads.start(kept[n], place, ("sum", n))
        else:
            loads.start(kept[n].at[0], held[n], ("kept", n))
            loads.start(got[n].at[0], came[n], ("got", n))
    own = pl.ds(pl.multiple_of(mine[0] * rows, rows), rows)
    loads.start(w_proj.at[own], proj_rows, "proj")
    loads.start(w_up.at[own], up_rows, "up")
    for n, (k, first) in enumerate(targets):
        if ready[n]:
            loads.wait(("sum", n))
            continue
        loads.wait(("kept", n), ("got", n))
        value = held[n][...].astype(F32) + came[n][...].astype(F32)
        sums[k][:, first : first + value.shape[1]] = value
    for k in range(4):
        stores.start(sums[k], outs[k])
    loads.wait("small")
    b_up[...] = small_rows[:1, : b_up.shape[1]]
    b_down[...] = small_rows[:1, b_up.shape[1] : b_up.shape[1] + rows]
    stores.start(b_up, outs[4])
    stores.start(b_down, outs[5])
    loads.wait("proj", "up")
    for n, (weight, grad, gain) in enumerate(((proj_rows, sums[3], gain_attn), (up_rows, sums[1], gain_ffn))):
        along = jnp.sum(weight[...].astype(F32) * grad[...], axis=1, keepdims=True)
        turned = jnp.broadcast_to(along, (rows, 128)).T
        gains[n] = turned[:1, :rows] / gain[...]
        stores.start(gains.at[n], outs[6 + n])
    stores.wait_all()


def gather_up(mine, targets, kept, got, small, w_proj, w_up, own_gain, size, tokens):
    rows = WIDTH // size
    widths = [(FF // size, WIDTH), (rows, FF), (rows, WIDTH), (rows, 3 * WIDTH)]
    outs = [shape(w, F32) for w in widths]
    outs += [shape((1, n), F32) for n in (FF // size, rows, rows, rows)]
    late = [v for v, g in zip(kept, got) if g is not None]
    pieces = [pltpu.VMEM(v.shape[1:], BF) for v in late]
    ready = [g is None for g in got]
    arrived = [g for g in got if g is not None]
    return call(
        lambda *refs: gather_kernel(targets, ready, small, *refs),
        "gather_up",
        [mine],
        [*kept, *arrived, w_proj, w_up, *own_gain],
        outs,
        pieces
        + pieces
        + [pltpu.VMEM(w, F32) for w in widths]
        + [
            pltpu.VMEM((16, WIDTH), F32),
            pltpu.VMEM((1, FF // size), F32),
            pltpu.VMEM((1, rows), F32),
            pltpu.VMEM((rows, 3 * WIDTH), BF),
            pltpu.VMEM((rows, FF), BF),
            pltpu.VMEM((2, 1, rows), F32),
            pltpu.SemaphoreType.DMA((2 * len(kept) + 3,)),
            pltpu.SemaphoreType.DMA((8,)),
        ],
        tokens,
        estimate=SHORT,
        specs=[ANY] * (len(kept) + len(late) + 2) + [whole(1, rows)] * 2,
    )


def pick_kernel(section, first, second, out, held, sems):
    for wanted, source in enumerate((first, second)):

        @pl.when(section[0] == wanted)
        def _(source=source):
            copies = Copies(sems)
            for s in range(held.shape[0]):
                copies.start(source.at[s], held.at[s], ("in", s))
            for s in range(held.shape[0]):
                copies.wait(("in", s))
                copies.start(held.at[s], out.at[s])
            copies.wait_all()


def pick(section, first, second, tokens):
    return call(
        pick_kernel,
        "pick",
        [section],
        [first, second],
        [shape(first.shape)],
        [pltpu.VMEM(first.shape, BF), pltpu.SemaphoreType.DMA((2 * first.shape[0],))],
        tokens,
        estimate=SHORT,
    )[0]


def swap_bit(value, size, bit):
    return lax.ppermute(value, "dp", [(i, i ^ (1 << bit)) for i in range(size)])


def one_way(value, first, second):
    return lax.ppermute(value, "section", [(first, second)])


def both_after(first, second):
    return lax.optimization_barrier((first, second))


def body(
    inputs,
    cotangent,
    memory,
    compressed,
    reset_flags,
    boundary,
    gain_attn,
    projection_weight,
    w_output,
    gain_ffn,
    w_up,
    b_up,
    w_down,
    b_down,
    w_compress,
    b_compress,
):
    section = lax.axis_index("section")
    is_first = section == 0
    size = lax.axis_size("dp")
    mine = lax.axis_index("dp")
    levels = (size - 1).bit_length()
    at_section, at_dp = section.astype(jnp.int32).reshape(1), mine.astype(jnp.int32).reshape(1)
    active = (1 - at_section, at_section)
    seqs, _, width = inputs.shape
    memory, compressed = memory[0], compressed[0]
    w_proj, w_out, w_up, w_down = projection_weight[0], w_output[0], w_up[0], w_down[0]
    params = (gain_attn, w_proj, w_out, gain_ffn, w_up, b_up, w_down, b_down)
    last = [[]]

    other_x = [one_way(inputs[0], 1, 0)]
    normed_memory, kv_memory = [], []

    def keyvals(s):
        normed, kv = memory_keyvals(s, reset_flags, compressed, memory, gain_attn, w_proj, last[0])
        last[0] = [kv]
        normed_memory.append(normed)
        kv_memory.append(kv)

    keyvals(0)
    kv_memory[0], inputs_later = both_after(kv_memory[0], inputs)
    other_x.append(one_way(inputs_later[1], 1, 0))

    def ahead(layer, s, xs, saved, estimate):
        scalars = [active[layer], reset_flags, boundary]
        y, saved = forward(s, seqs, scalars, xs, kv_memory[s], params, saved, last[0], estimate)
        last[0] = [y]
        return y, saved

    y_a0, saved = ahead(0, 0, ((inputs, 0), (other_x[0], None)), None, LONG)
    hop_a = one_way(y_a0, 0, 1)
    keyvals(1)
    y_b0, saved = ahead(0, 1, ((inputs, 1), (other_x[1], None)), saved, SHORT)
    y_b0, cotangent_later = both_after(y_b0, cotangent)
    hop_b = one_way(y_b0, 0, 1)
    other_gy = [one_way(cotangent_later[s], 0, 1) for s in range(seqs)]

    def squeeze(layer):
        tokens = last[0]
        work = lambda: compress(reset_flags, memory, w_compress[0], b_compress, tokens)
        skip = lambda: unset([(seqs, COMP, WIDTH)], tokens)
        made = lax.cond(section == layer, work, skip)[0]
        last[0] = [made]
        return made

    squeezed_first = squeeze(0)

    def back(layer, s, gys, fed, made, estimate, part=SEG):
        fed = feed_back(s, [active[layer]], gys, saved, params, fed, last[0], estimate)
        scalars = [active[layer], reset_flags, boundary]
        dx, made = attend_back(s, scalars, saved, fed, kv_memory[s], params, made, [], SHORT, part)
        last[0] = [dx]
        return dx, fed, made

    y_a1, saved = ahead(1, 0, ((hop_a, None),), saved, SHORT)
    dx_a1, fed, made = back(1, 0, ((other_gy[0], None, 0, 0), (cotangent, 0, 0, width)), None, None, SHORT)
    back_a = one_way(dx_a1, 1, 0)
    y_b1, saved = ahead(1, 1, ((hop_b, None),), saved, SHORT)
    other_y = one_way(saved["y_low"], 1, 0)
    dx_b1, fed, made = back(1, 1, ((other_gy[1], None, 0, 0), (cotangent, 1, 0, width)), fed, made, SHORT, HALF)
    rest = project_back(1, [active[1]], saved, fed, params, made, [dx_b1, back_a])
    back_b = [one_way(dx_b1, 1, 0), one_way(rest, 1, 0)]
    last[0] = [rest]
    dx_a0, fed, made = back(0, 0, ((back_a, None, 0, 0),), fed, made, SHORT)

    def gy_of(s, arrived):
        count = len(arrived)
        first = [(n, None, n * (SEG // count), 0) for n in range(count)]
        second = [(count, None, 0, 0), (count + 1, s, 0, WIDTH // 2)]
        return Either([*arrived, other_gy[s], cotangent], (first, second))

    tall = FF // WIDTH
    kinds = lambda: dict(
        down=(
            [[(saved["hidden"], 0)], gy_of(0, [back_a])],
            [dict(left=0, right=1, loop="left", count=tall, out=0, at=(0, 0))],
            [(FF, WIDTH)],
        ),
        up=(
            [[(saved["ffn_in"], 0)], [(fed["d_hidden"], 0)], [(saved["attended"], 0)], [(fed["low"], 0)]],
            [
                dict(left=0, right=1, loop="right", count=tall, out=0, at=(0, 0)),
                dict(left=2, right=3, loop=None, count=1, out=1, at=(0, 0)),
            ],
            [(WIDTH, FF), (WIDTH, WIDTH)],
        ),
        proj=(
            [
                [(saved["normed"], 0), (normed_memory[0], 0)],
                [(made["dkx"], 0), (made["dkm"], 0)],
                [(made["dvx"], 0), (made["dvm"], 0)],
                [(saved["normed"], 0)],
                [(made["dq"], 0)],
            ],
            [
                dict(left=0, right=1, loop=None, count=1, out=0, at=(0, WIDTH)),
                dict(left=0, right=2, loop=None, count=1, out=0, at=(0, 2 * WIDTH)),
                dict(left=3, right=4, loop=None, count=1, out=0, at=(0, 0)),
            ],
            [(WIDTH, 3 * WIDTH)],
        ),
    )

    def early(tokens, *which):
        groups, jobs, outs = [], [], []
        for kind in which:
            more, jobs_more, outs_more = kinds()[kind]
            for job in jobs_more:
                jobs.append(
                    dict(
                        job,
                        left=job["left"] + len(groups),
                        right=job["right"] + len(groups),
                        out=job["out"] + len(outs),
                    )
                )
            groups, outs = groups + more, outs + outs_more
        return early_grads(at_section, groups, jobs, outs, tokens)

    sizes = {kind: value[2] for kind, value in kinds().items()}
    tokens = last[0]
    base_down, up_first, out_first, proj_first = lax.cond(
        is_first,
        lambda: early(tokens, "down", "up", "proj"),
        lambda: early(tokens, "down") + unset(sizes["up"] + sizes["proj"], tokens),
    )
    last[0] = [base_down]

    def early_second(kind):
        tokens = last[0]
        made_late = lax.cond(is_first, lambda: unset(sizes[kind], tokens), lambda: early(tokens, kind))
        last[0] = [made_late[0]]
        return made_late

    moving, done = {}, {}
    orders = {name: (0, *range(2, levels), 1) for name in ("up0",)}

    def send_on(name, send, keep, step):
        order = orders.get(name, tuple(range(levels)))
        moving[name] = (swap_bit(send, size, order[step]), keep, step)

    def halved(*names, estimate=SHORT):
        names = [name for name in names if name in moving]
        if not names:
            return
        which = []
        for name in names:
            step = moving[name][2] + 1
            which.append(None if step == levels else orders.get(name, tuple(range(levels)))[step])
        kept, got = [moving[name][1] for name in names], [moving[name][0] for name in names]
        made = halve(at_dp, which, kept, got, last[0], estimate)
        last[0] = [made[0][0]]
        for name, level, values in zip(names, which, made):
            if level is None:
                done[name] = values[0]
                moving.pop(name)
            else:
                send_on(name, *values, moving[name][2] + 1)

    def grads(names, groups, bases, tasks, chunks, **more):
        places = [places_of(orders.get(name, tuple(range(levels))), size) for name in names]
        made = weight_grads(at_section, at_dp, size, groups, bases, tasks, chunks, last[0], places, **more)
        last[0] = [made[0][0]]
        for name, (send, keep) in zip(names, made):
            send_on(name, send, keep, 0)

    eighth = WIDTH // 8
    grads(
        ("down0", "down1", "down2"),
        [[(saved["hidden"], 1)], gy_of(1, back_b)],
        [(base_down, base_down)],
        [
            dict(
                left=(0, t),
                right=(1, 0),
                base=(0, t * WIDTH, 0),
                block=t,
                blocks=FF // WIDTH,
                outs=[(0, 0, 3 * eighth, 0), (1, 3 * eighth, 2 * eighth, 0), (2, 5 * eighth, 3 * eighth, 0)],
            )
            for t in range(FF // WIDTH)
        ],
        [(FF // WIDTH, 3 * eighth), (FF // WIDTH, 2 * eighth), (FF // WIDTH, 3 * eighth)],
    )
    halved("down0")
    halved("down1", "down2")
    fed = feed_back(1, [active[0]], [(part, None, n * HALF, 0) for n, part in enumerate(back_b)], saved, params, fed, last[0])
    last[0] = [fed["d_down"]]
    up_second, out_second = early_second("up")
    halved("down0")

    up = jnp.sum(fed["d_up"], axis=(0, 1)).reshape(size, FF // size)
    down = jnp.sum(fed["d_down"], axis=(0, 1)).reshape(size, WIDTH // size)
    row = jnp.concatenate([up, down], axis=1).astype(BF)
    small = jnp.pad(row[:, None, :], ((0, 0), (0, 15), (0, WIDTH - row.shape[1])))
    grads(
        ("up0", "up1", "out"),
        [[(saved["ffn_in"], 1)], [(fed["d_hidden"], 1)], [(saved["attended"], 1)], [(fed["low"], 1)]],
        [(up_first, up_second), (out_first, out_second)],
        [
            dict(
                left=(0, 0),
                right=(1, t),
                base=(0, 0, t * WIDTH),
                block=0,
                blocks=1,
                outs=[(t // 2, 0, WIDTH, (t % 2) * WIDTH)],
            )
            for t in range(tall)
        ]
        + [dict(left=(2, 0), right=(3, 0), base=(1, 0, 0), block=0, blocks=1, outs=[(2, 0, WIDTH, 0)])],
        [(1, 2 * WIDTH), (1, 2 * WIDTH), (1, WIDTH)],
        small=small,
        small_chunk=1,
        estimate=SHORT,
    )
    halved("down1", "down2", "down0", estimate=LONG)
    halved("up1")
    halved("up0", "out")
    dx_b0, made = attend_back(
        1, [active[0], reset_flags, boundary], saved, fed, kv_memory[1], params, made, last[0]
    )
    last[0] = [dx_b0]
    (proj_second,) = early_second("proj")
    squeezed_second = squeeze(1)
    outputs = pick(at_section, other_y, saved["y_high"], last[0])
    last[0] = [outputs]
    halved("up1", "up0", "down1", "down2", "down0")
    grads(
        ("key", "value", "query"),
        [
            [(saved["normed"], 1), (normed_memory[1], 0)],
            [(made["dkx"], 1), (made["dkm"], 1)],
            [(made["dvx"], 1), (made["dvm"], 1)],
            [(saved["normed"], 1)],
            [(made["dq"], 1)],
        ],
        [(proj_first, proj_second)],
        [
            dict(left=(0, 0), right=(1, 0), base=(0, 0, WIDTH), block=0, blocks=1, outs=[(0, 0, WIDTH, 0)]),
            dict(left=(0, 0), right=(2, 0), base=(0, 0, 2 * WIDTH), block=0, blocks=1, outs=[(1, 0, WIDTH, 0)]),
            dict(left=(3, 0), right=(4, 0), base=(0, 0, 0), block=0, blocks=1, outs=[(2, 0, WIDTH, 0)]),
        ],
        [(1, WIDTH)] * 3,
        estimate=SHORT,
    )
    halved("out", "up1", "up0", "down1", "down2", estimate=LONG)
    halved("key", "value", "query")
    grad_inputs = pick(at_section, made["dx_low"], one_way(made["dx_high"], 0, 1), last[0])
    last[0] = [grad_inputs]
    halved("up0", estimate=LONG)
    for names in (("key", "up1", "out"), ("value", "key"), ("query", "value", "out"), ("query", "key")):
        halved(*names)
    while any(step + 1 < levels for _, _, step in moving.values()):
        halved(*[name for name, (_, _, step) in moving.items() if step + 1 < levels])
    if "up1" in moving:
        halved("up1")
    rows = WIDTH // size
    own_gain = [
        lax.dynamic_slice_in_dim(gain, mine * rows, rows, 1).astype(F32) for gain in (gain_attn, gain_ffn)
    ]
    targets = dict(
        down0=(0, 0), down1=(0, 3 * eighth), down2=(0, 5 * eighth), up0=(1, 0), up1=(1, 2 * WIDTH), out=(2, 0),
        query=(3, 0), key=(3, WIDTH), value=(3, 2 * WIDTH),
    )
    names = list(targets)
    g_down, g_up, g_out, g_proj, g_b_up, g_b_down, g_gain_attn, g_gain_ffn = gather_up(
        at_dp,
        [targets[name] for name in names],
        [done[name] if name in done else moving[name][1] for name in names],
        [None if name in done else moving[name][0] for name in names],
        names.index("up1"),
        w_proj,
        w_up,
        own_gain,
        size,
        last[0],
    )
    keep_all = (1 - reset_flags).astype(BF)[:, None, None]
    squeezed = jnp.where(is_first, squeezed_first, squeezed_second)
    new_compressed = jnp.concatenate([compressed[:, COMP:] * keep_all, squeezed], axis=1)
    return (
        outputs,
        grad_inputs,
        saved["x"][None],
        new_compressed[None],
        g_gain_attn,
        g_proj[None],
        g_out[None],
        g_gain_ffn,
        g_up[None],
        g_b_up,
        g_down[None],
        g_b_down,
    )


def solution(mesh):
    return jax.shard_map(
        body,
        mesh=mesh,
        in_specs=(
            P("dp", None, "section"),
            P("dp", None, "section"),
            P("section", "dp", None, None),
            P("section", "dp", None, None),
            P("dp"),
            P("dp"),
            P("section", None),
            P("section", None, None),
            P("section", None, None),
            P("section", None),
            P("section", None, None),
            P("section", None),
            P("section", None, None),
            P("section", None),
            P("section", None, None, None),
            P("section", None),
        ),
        out_specs=(
            P("dp", None, "section"),
            P("dp", None, "section"),
            P("section", "dp", None, None),
            P("section", "dp", None, None),
            P("section", "dp"),
            P("section", "dp", None),
            P("section", "dp", None),
            P("section", "dp"),
            P("section", "dp", None),
            P("section", "dp"),
            P("section", "dp", None),
            P("section", "dp"),
        ),
        check_vma=False,
    )
```

```python
import math

import jax
import jax.numpy as jnp
from jax import lax
from jax.experimental import pallas as pl
from jax.experimental.pallas import tpu as pltpu
from jax.sharding import PartitionSpec as P

WIDTH = 1024
HEADS = 8
HEAD = 128
FF = 4096
SEG = 512
MEM = 512
CMEM = 512
RATE = 2
COMP = 256
CTX = MEM + CMEM
HALF = SEG // 2
HP = 8

EPS = 1e-05
NEG = -1e30
ROOT_TWO_PI = 0.7978845608028654
SCALE = HEAD**-0.5
LOG2E = math.log2(math.e)
LN2 = math.log(2.0)
BF = jnp.bfloat16
F32 = jnp.float32
PARAMS = pltpu.CompilerParams(vmem_limit_bytes=56 << 20)


def nn(a, b):
    return lax.dot_general(a, b, (((1,), (0,)), ((), ())), preferred_element_type=F32)


def nt(a, b):
    return lax.dot_general(a, b, (((1,), (1,)), ((), ())), preferred_element_type=F32)


def tn(a, b):
    return lax.dot_general(a, b, (((0,), (0,)), ((), ())), preferred_element_type=F32)


def shape(dims, dtype=BF):
    return jax.ShapeDtypeStruct(dims, dtype)


def whole(*dims):
    return pl.BlockSpec(dims, lambda *_: (0,) * len(dims))


def cost(flops, moved, trans=0):
    return pl.CostEstimate(flops=int(flops), bytes_accessed=int(moved), transcendentals=int(trans))


LONG = cost(1e11, 1)
SHORT = cost(1, 1)


def normalise(values):
    centred = values - jnp.mean(values, axis=-1, keepdims=True)
    inverse = lax.rsqrt(jnp.mean(centred * centred, axis=-1, keepdims=True) + EPS)
    return centred * inverse, inverse


def norm_back(unit, inverse, gain, grad):
    scaled = grad * gain
    along = jnp.mean(scaled * unit, axis=-1, keepdims=True)
    return inverse * (scaled - jnp.mean(scaled, axis=-1, keepdims=True) - unit * along)


ANY = pl.BlockSpec(memory_space=pltpu.HBM)


def call(kernel, name, scalars, ins, outs, scratch, tokens, aliases=None, estimate=LONG, specs=None):
    first = len(scalars) + len(ins)

    def run(*refs):
        kernel(*refs[:first], *refs[first + len(tokens) :])

    return pl.pallas_call(
        run,
        name=name,
        grid_spec=pltpu.PrefetchScalarGridSpec(
            num_scalar_prefetch=len(scalars),
            grid=(1,),
            in_specs=list(specs or [ANY] * len(ins)) + [ANY] * len(tokens),
            out_specs=[ANY] * len(outs),
            scratch_shapes=scratch,
        ),
        out_shape=list(outs),
        input_output_aliases=aliases or {},
        compiler_params=PARAMS,
        cost_estimate=estimate,
    )(*scalars, *ins, *tokens)


class Copies:
    def __init__(self, sems):
        self.sems, self.count, self.named = sems, 0, {}

    def start(self, source, target, name=None):
        copy = pltpu.make_async_copy(source, target, self.sems.at[self.count])
        copy.start()
        self.named[name if name is not None else self.count] = copy
        self.count += 1

    def wait(self, *names):
        for name in names:
            self.named.pop(name).wait()

    def wait_all(self):
        for name in list(self.named):
            self.wait(name)


def tiles(ref, axis, size=1024):
    if axis == 0:
        return [ref.at[pl.ds(i * size, size)] for i in range(ref.shape[0] // size)]
    return [ref.at[:, pl.ds(i * size, size)] for i in range(ref.shape[1] // size)]


def memory_kernel(seq, flags, comp, mem, gain, w, normed, kv, rows, weights, unit_rows, out, sems):
    copies = Copies(sems)
    for n, source in enumerate((comp, mem)):
        copies.start(source.at[seq], rows.at[n], ("rows", n))
        copies.start(w.at[:, pl.ds((1 + n) * WIDTH, WIDTH)], weights.at[n], ("w", n))
    keep = (1 - flags[seq]).astype(F32)

    def unit(n):
        copies.wait(("rows", n))
        value, _ = normalise(rows[n].astype(F32) * keep)
        unit_rows[n] = (value * gain[...].astype(F32)).astype(BF)

    unit(0)
    for n in range(2):
        place = pl.ds(n * MEM, MEM)
        copies.start(unit_rows.at[n], normed.at[0, place])
        for t in range(2):
            if n == 0:
                copies.wait(("w", t))
            out[n, :, t * WIDTH : (t + 1) * WIDTH] = nn(unit_rows[n], weights[t]).astype(BF)
            if n == 0 and t == 0:
                unit(1)
        copies.start(out.at[n], kv.at[0, place])
    copies.wait_all()


def memory_keyvals(seq, flags, compressed, memory, gain, w_proj, tokens):
    return call(
        lambda *refs: memory_kernel(seq, *refs),
        "memory_keyvals",
        [flags],
        [compressed, memory, gain, w_proj],
        [shape((1, CTX, WIDTH)), shape((1, CTX, 2 * WIDTH))],
        [
            pltpu.VMEM((2, MEM, WIDTH), BF),
            pltpu.VMEM((2, WIDTH, WIDTH), BF),
            pltpu.VMEM((2, MEM, WIDTH), BF),
            pltpu.VMEM((2, MEM, 2 * WIDTH), BF),
            pltpu.SemaphoreType.DMA((8,)),
        ],
        tokens,
        specs=[ANY, ANY, whole(1, WIDTH), ANY],
    )


def fill_masks(flag, bound, bias, unseen):
    key = lax.broadcasted_iota(jnp.int32, (SEG, SEG), 0)
    query = lax.broadcasted_iota(jnp.int32, (SEG, SEG), 1)
    least = jnp.where(query >= bound, bound, 0)
    bias[...] = jnp.where((key <= query) & (key >= least), 0.0, NEG)
    position = lax.broadcasted_iota(jnp.int32, (1, SEG), 1)
    limit = jnp.where(flag == 0, bound, 0)
    unseen[...] = jnp.where(position < limit, 0.0, -NEG)


def gelu_parts(v):
    inner = v * (ROOT_TWO_PI + (0.044715 * ROOT_TWO_PI) * (v * v))
    t = jnp.tanh(inner)
    half = 0.5 + 0.5 * t
    slope = 3.0 * inner - (2.0 * ROOT_TWO_PI) * v
    return v * half, half + half * (1.0 - t) * slope


def attend_heads(first, qkv, kvm, attended, log_total, bias, unseen):
    def cols(base, h):
        return pl.ds(pl.multiple_of(base * WIDTH + (first + h) * HEAD, HEAD), HEAD)

    pieces = [(h, slice(part * HALF, (part + 1) * HALF), (part + 1) * HALF) for h in range(HP) for part in range(2)]

    def scores(h, r, count):
        rows = qkv[r, cols(0, h)]
        return nt(kvm[:, cols(0, h)], rows), nt(qkv[:count, cols(1, h)], rows) + bias[:count, r]

    def weights(h, r, count, on_memory, on_segment):
        hidden = unseen[:, r]
        top = jnp.maximum(
            jnp.max(on_memory, axis=0, keepdims=True) - hidden,
            jnp.max(on_segment, axis=0, keepdims=True),
        )
        p_memory = jnp.exp2(on_memory - (top + hidden))
        p_segment = jnp.exp2(on_segment - top)
        total = jnp.sum(p_memory, axis=0, keepdims=True) + jnp.sum(p_segment, axis=0, keepdims=True)
        log_total[first + h, :, r] = top + jnp.log2(total)
        return p_memory.astype(BF), p_segment.astype(BF), total

    values = {}

    def finish(h, r, count, p_memory, p_segment, total):
        if h not in values:
            values[h] = (kvm[:, cols(1, h)].T, qkv[:, cols(2, h)].T)
        turned = nn(values[h][0], p_memory) + nn(values[h][1][:, :count], p_segment)
        attended[r, cols(0, h)] = (turned * (1.0 / total)).T.astype(BF)

    held, ready = {}, {}
    for step in range(len(pieces) + 2):
        if step < len(pieces):
            held[step] = scores(*pieces[step])
        if 0 <= step - 1 < len(pieces):
            ready[step - 1] = weights(*pieces[step - 1], *held.pop(step - 1))
        if 0 <= step - 2 < len(pieces):
            finish(*pieces[step - 2], *ready.pop(step - 2))


SAVED = (
    ("x", (SEG, WIDTH), BF),
    ("normed", (SEG, WIDTH), BF),
    ("qkv", (SEG, 3 * WIDTH), BF),
    ("attended", (SEG, WIDTH), BF),
    ("log_total", (HEADS, 1, SEG), F32),
    ("residual", (SEG, WIDTH), F32),
    ("ffn_in", (SEG, WIDTH), BF),
    ("hidden", (SEG, FF), BF),
    ("gate", (SEG, FF), BF),
    ("y_low", (SEG, WIDTH // 2), BF),
    ("y_high", (SEG, WIDTH // 2), BF),
)
FS = 512


def forward_kernel(seq, parts, aliased, active, flags, bounds, *refs):
    xs, refs = refs[: len(parts)], refs[len(parts) :]
    (gain, w_proj, kv_memory, w_out, gain_ffn, w_up, b_up, w_down, b_down), refs = refs[:9], refs[9:]
    refs = refs[aliased:]
    y, refs = refs[0], refs[1:]
    out = dict(zip([name for name, _, _ in SAVED], refs))
    refs = refs[len(SAVED) :]
    held = dict(zip([name for name, _, _ in SAVED], refs))
    pool, kvm, wo, total, y_rows, bias, unseen, in_sems, out_sems, feed_sems = refs[len(SAVED) :]

    @pl.when(active[0] == 1)
    def _():
        loads, stores = Copies(in_sems), Copies(out_sems)

        def save(*names):
            for name in names:
                stores.start(held[name], out[name].at[seq])

        x = held["x"]
        for i, (part, lead) in enumerate(zip(xs, parts)):
            wide = WIDTH // len(parts)
            loads.start(part if lead is None else part.at[lead], x.at[:, pl.ds(i * wide, wide)], ("x", i))
        for t, tile in enumerate(tiles(w_proj, 1)):
            loads.start(tile, pool.at[t], ("proj", t))
        loads.start(kv_memory.at[0], kvm, "kvm")
        loads.start(w_out, wo, "out")
        for t, tile in enumerate(tiles(w_up, 1)):
            loads.start(tile, pool.at[4 + t], ("up", t))
        fill_masks(flags[seq], bounds[seq], bias, unseen)
        loads.wait(*[("x", i) for i in range(len(parts))])
        unit, _ = normalise(x[...].astype(F32))
        held["normed"][...] = (unit * gain[...].astype(F32)).astype(BF)
        for t in range(3):
            loads.wait(("proj", t))
            factor = SCALE * LOG2E if t == 0 else 1.0
            held["qkv"][:, t * WIDTH : (t + 1) * WIDTH] = (nn(held["normed"][...], pool[t]) * factor).astype(BF)
        for t, tile in enumerate(tiles(w_down, 0)):
            loads.start(tile, pool.at[t], ("down", t))
        save("x", "normed", "qkv")
        loads.wait("kvm")

        def heads(g, _):
            attend_heads(g * HP, held["qkv"], kvm, held["attended"], held["log_total"], bias, unseen)
            return 0

        lax.fori_loop(0, HEADS // HP, heads, 0)
        save("attended", "log_total")
        loads.wait("out")
        rows = x[...].astype(F32) + nn(held["attended"][...], wo[...])
        held["residual"][...] = rows
        unit, _ = normalise(rows)
        held["ffn_in"][...] = (unit * gain_ffn[...].astype(F32)).astype(BF)
        save("residual", "ffn_in")
        total[...] = rows + b_down[...].astype(F32)
        loads.wait_all()

        def feed(t, _):
            cuts = [pl.ds(t * 1024 + i * FS, FS) for i in range(1024 // FS)]
            ups = [
                nn(held["ffn_in"][...], pool[4 + t, :, i * FS : (i + 1) * FS]) + b_up[:, c].astype(F32)
                for i, c in enumerate(cuts)
            ]
            added = None
            for i, (c, up) in enumerate(zip(cuts, ups)):
                value, slope = gelu_parts(up)
                value = value.astype(BF)
                held["hidden"][:, c] = value
                held["gate"][:, c] = slope.astype(BF)
                part = nn(value, pool[t, i * FS : (i + 1) * FS])
                added = part if added is None else added + part
            total[...] += added
            for name, sem in (("hidden", 0), ("gate", 1)):
                feed_copy(name, sem, t).start()
            return 0

        def feed_copy(name, sem, t):
            place = pl.ds(t * 1024, 1024)
            return pltpu.make_async_copy(held[name].at[:, place], out[name].at[seq, :, place], feed_sems.at[sem, t])

        for t in range(FF // 1024):
            feed(t, 0)
        rows = total[...].astype(BF)
        y_rows[...] = rows
        held["y_low"][...] = rows[:, : WIDTH // 2]
        held["y_high"][...] = rows[:, WIDTH // 2 :]
        stores.start(y_rows, y)
        save("y_low", "y_high")
        for t in range(FF // 1024):
            feed_copy("hidden", 0, t).wait()
            feed_copy("gate", 1, t).wait()
        stores.wait_all()


def forward(seq, seqs, scalars, xs, kv_memory, params, saved, tokens, estimate):
    gain_attn, w_proj, w_out, gain_ffn, w_up, b_up, w_down, b_down = params
    args = [v for v, _ in xs] + [gain_attn, w_proj, kv_memory, w_out, gain_ffn, w_up, b_up, w_down, b_down]
    specs = [ANY] * len(xs) + [
        whole(1, WIDTH), ANY, ANY, ANY, whole(1, WIDTH), ANY, whole(1, FF), ANY, whole(1, WIDTH)
    ]
    aliases = {}
    if saved is not None:
        aliases = {len(scalars) + len(args) + i: 1 + i for i in range(len(SAVED))}
        args += [saved[name] for name, _, _ in SAVED]
        specs += [ANY] * len(SAVED)
    leads = [lead for _, lead in xs]
    results = call(
        lambda *refs: forward_kernel(seq, leads, len(aliases), *refs),
        "forward",
        scalars,
        args,
        [shape((SEG, WIDTH))] + [shape((seqs,) + dims, dtype) for _, dims, dtype in SAVED],
        [pltpu.VMEM(dims, dtype) for _, dims, dtype in SAVED]
        + [
            pltpu.VMEM((8, WIDTH, WIDTH), BF),
            pltpu.VMEM((CTX, 2 * WIDTH), BF),
            pltpu.VMEM((WIDTH, WIDTH), BF),
            pltpu.VMEM((SEG, WIDTH), F32),
            pltpu.VMEM((SEG, WIDTH), BF),
            pltpu.VMEM((SEG, SEG), F32),
            pltpu.VMEM((1, SEG), F32),
            pltpu.SemaphoreType.DMA((16,)),
            pltpu.SemaphoreType.DMA((14,)),
            pltpu.SemaphoreType.DMA((2, FF // 1024)),
        ],
        tokens,
        aliases,
        estimate,
        specs,
    )
    return results[0], dict(zip([name for name, _, _ in SAVED], results[1:]))


FED = (
    ("d_hidden", (SEG, FF), BF),
    ("d_residual", (SEG, WIDTH), F32),
    ("low", (SEG, WIDTH), BF),
    ("d_attended", (SEG, WIDTH), BF),
    ("d_up", (1, FF), F32),
    ("d_down", (1, WIDTH), F32),
)


def feed_back_kernel(seq, leads, aliased, active, *refs):
    gys, refs = refs[: len(leads)], refs[len(leads) :]
    (w_down, gate, w_up, residual, gain, w_out), refs = refs[:6], refs[6:]
    refs = refs[aliased:]
    out = dict(zip([name for name, _, _ in FED], refs))
    refs = refs[len(FED) :]
    held = dict(zip([name for name, _, _ in FED], refs))
    gy_rows, pool, gates, rows, wo, total, in_sems, out_sems = refs[len(FED) :]

    @pl.when(active[0] == 1)
    def _():
        loads, stores = Copies(in_sems), Copies(out_sems)
        for i, (part, (lead, row, column)) in enumerate(zip(gys, leads)):
            source = part if lead is None else part.at[lead]
            tall, wide = source.shape
            loads.start(source, gy_rows.at[pl.ds(row, tall), pl.ds(column, wide)], ("gy", i))
        downs, ups = tiles(w_down, 0), tiles(w_up, 1)
        for t in range(FF // 1024):
            loads.start(downs[t], pool.at[t], ("down", t))
            loads.start(gate.at[seq, :, pl.ds(t * 1024, 1024)], gates.at[:, pl.ds(t * 1024, 1024)], ("gate", t))
            loads.start(ups[t], pool.at[4 + t], ("up", t))
        loads.start(residual.at[seq], rows, "rows")
        loads.start(w_out, wo, "out")
        loads.wait(*[("gy", i) for i in range(len(leads))])
        held["d_down"][...] = jnp.sum(gy_rows[...].astype(F32), axis=0, keepdims=True)
        for t in range(FF // 1024):
            loads.wait(("down", t), ("gate", t), ("up", t))
            raws = [nt(gy_rows[...], pool[t, i * FS : (i + 1) * FS]) for i in range(1024 // FS)]
            added = None
            for i, raw in enumerate(raws):
                c = slice(t * 1024 + i * FS, t * 1024 + (i + 1) * FS)
                value = (raw * gates[:, c].astype(F32)).astype(BF)
                held["d_hidden"][:, c] = value
                held["d_up"][:, c] = jnp.sum(value.astype(F32), axis=0, keepdims=True)
                part = nt(value, pool[4 + t, :, i * FS : (i + 1) * FS])
                added = part if added is None else added + part
            total[...] = added if t == 0 else total[...] + added
        for name in ("d_hidden", "d_up", "d_down"):
            stores.start(held[name], out[name].at[seq])
        loads.wait("rows", "out")
        unit, inverse = normalise(rows[...])
        grad = gy_rows[...].astype(F32) + norm_back(unit, inverse, gain[...].astype(F32), total[...])
        held["d_residual"][...] = grad
        held["low"][...] = grad.astype(BF)
        held["d_attended"][...] = nt(held["low"][...], wo[...]).astype(BF)
        for name in ("d_residual", "low", "d_attended"):
            stores.start(held[name], out[name].at[seq])
        stores.wait_all()


def feed_back(seq, scalars, gys, saved, params, fed, tokens, estimate=LONG):
    gain_attn, w_proj, w_out, gain_ffn, w_up, b_up, w_down, b_down = params
    seqs = saved["gate"].shape[0]
    args = [v for v, *_ in gys] + [w_down, saved["gate"], w_up, saved["residual"], gain_ffn, w_out]
    specs = [ANY] * (len(gys) + 4) + [whole(1, WIDTH), ANY]
    aliases = {}
    if fed is not None:
        aliases = {len(scalars) + len(args) + i: i for i in range(len(FED))}
        args += [fed[name] for name, _, _ in FED]
        specs += [ANY] * len(FED)
    leads = [place for _, *place in gys]
    results = call(
        lambda *refs: feed_back_kernel(seq, leads, len(aliases), *refs),
        "feed_back",
        scalars,
        args,
        [shape((seqs,) + dims, dtype) for _, dims, dtype in FED],
        [pltpu.VMEM(dims, dtype) for _, dims, dtype in FED]
        + [
            pltpu.VMEM((SEG, WIDTH), BF),
            pltpu.VMEM((8, WIDTH, WIDTH), BF),
            pltpu.VMEM((SEG, FF), BF),
            pltpu.VMEM((SEG, WIDTH), F32),
            pltpu.VMEM((WIDTH, WIDTH), BF),
            pltpu.VMEM((SEG, WIDTH), F32),
            pltpu.SemaphoreType.DMA((16,)),
            pltpu.SemaphoreType.DMA((8,)),
        ],
        tokens,
        aliases,
        estimate,
        specs,
    )
    return dict(zip([name for name, _, _ in FED], results))


MADE = (
    ("dq", (SEG, WIDTH), BF),
    ("dkx", (SEG, WIDTH), BF),
    ("dvx", (SEG, WIDTH), BF),
    ("dkm", (CTX, WIDTH), BF),
    ("dvm", (CTX, WIDTH), BF),
    ("dx_low", (SEG, WIDTH // 2), BF),
    ("dx_high", (SEG, WIDTH // 2), BF),
)
GROUP = 2


def attend_back_heads(first, qkv, kvm, d_out, out, log_total, made, bias, unseen):
    every, low, high = slice(0, SEG), slice(0, HALF), slice(HALF, SEG)

    def cols(base, h):
        return pl.ds(pl.multiple_of(base * WIDTH + (first + h) * HEAD, HEAD), HEAD)

    for h in range(GROUP):
        c = cols(0, h)
        qh, gh = qkv[:, c], d_out[:, c]
        inner = jnp.sum((gh.astype(F32) * out[:, c].astype(F32)).T, axis=0, keepdims=True)
        level = log_total[first + h]

        def piece(k, v, r, mask):
            logits = nt(k, qh[r])
            if mask is None:
                p = jnp.exp2(logits - (level[:, r] + unseen[:, r]))
            else:
                p = jnp.exp2(logits + mask - level[:, r])
            ds = (p * (nt(v, gh[r]) - inner[:, r])).astype(BF)
            return p.astype(BF), ds

        km, vm, kx, vx = kvm[:, c], kvm[:, cols(1, h)], qkv[:, cols(1, h)], qkv[:, cols(2, h)]
        p_memory, ds_memory = piece(km, vm, every, None)
        p_low, ds_low = piece(kx[low], vx[low], every, bias[low, :])
        p_high, ds_high = piece(kx[high], vx[high], high, bias[high, high])
        made["dvm"][:, c] = nn(p_memory, gh).astype(BF)
        made["dkm"][:, c] = (nn(ds_memory, qh) * LN2).astype(BF)
        made["dvx"][low, c] = nn(p_low, gh).astype(BF)
        made["dkx"][low, c] = (nn(ds_low, qh) * LN2).astype(BF)
        made["dvx"][high, c] = nn(p_high, gh[high]).astype(BF)
        made["dkx"][high, c] = (nn(ds_high, qh[high]) * LN2).astype(BF)
        turned = kx.T
        both = nn(km.T, ds_memory) + nn(turned[:, low], ds_low)
        made["dq"][low, c] = (both[:, low] * SCALE).T.astype(BF)
        made["dq"][high, c] = ((both[:, high] + nn(turned[:, high], ds_high)) * SCALE).T.astype(BF)


def attend_back_kernel(seq, part, aliased, active, flags, bounds, *refs):
    (qkv_in, kv_memory, d_out_in, out_in, stat_in, w_proj, x_in, gain, d_residual), refs = refs[:9], refs[9:]
    refs = refs[aliased:]
    dx, refs = refs[0], refs[1:]
    result = dict(zip([name for name, _, _ in MADE], refs))
    refs = refs[len(MADE) :]
    made = dict(zip([name for name, _, _ in MADE], refs))
    refs = refs[len(MADE) :]
    qkv, kvm, d_out, out, log_total, pool, x, rows, dx_rows, bias, unseen, in_sems, head_sems, out_sems = refs

    @pl.when(active[0] == 1)
    def _():
        loads, stores = Copies(in_sems), Copies(out_sems)
        wide = GROUP * HEAD
        count = WIDTH // wide

        def head_copies(g):
            g = g * wide if isinstance(g, int) else pl.multiple_of(g * wide, wide)
            sems = head_sems.at[g // wide]
            pairs = [
                (ref.at[lead, :, pl.ds(base * WIDTH + g, wide)], target.at[:, pl.ds(base * WIDTH + g, wide)])
                for ref, lead, target, bases in (
                    (qkv_in, seq, qkv, 3),
                    (kv_memory, 0, kvm, 2),
                    (d_out_in, seq, d_out, 1),
                    (out_in, seq, out, 1),
                )
                for base in range(bases)
            ]
            return [pltpu.make_async_copy(a, b, sems.at[i]) for i, (a, b) in enumerate(pairs)]

        loads.start(stat_in.at[seq], log_total, "stat")
        for g in range(count):
            for copy in head_copies(g):
                copy.start()
        for t, tile in enumerate(tiles(w_proj, 1)):
            loads.start(tile, pool.at[t])
        loads.start(x_in.at[seq], x)
        loads.start(d_residual.at[seq], rows)
        fill_masks(flags[seq], bounds[seq], bias, unseen)
        loads.wait("stat")

        def heads(g, _):
            for copy in head_copies(g):
                copy.wait()
            attend_back_heads(g * GROUP, qkv, kvm, d_out, out, log_total, made, bias, unseen)
            return 0

        lax.fori_loop(0, count, heads, 0)
        for name, _, _ in MADE[:5]:
            stores.start(made[name], result[name].at[seq])
        loads.wait_all()
        top = slice(0, part)
        grad = nt(made["dq"][top], pool[0]) + nt(made["dkx"][top], pool[1]) + nt(made["dvx"][top], pool[2])
        unit, inverse = normalise(x[top].astype(F32))
        value = (rows[top] + norm_back(unit, inverse, gain[...].astype(F32), grad)).astype(BF)
        dx_rows[top] = value
        stores.start(dx_rows.at[pl.ds(0, part)], dx)
        if part == SEG:
            made["dx_low"][...] = value[:, : WIDTH // 2]
            made["dx_high"][...] = value[:, WIDTH // 2 :]
            for name, _, _ in MADE[5:]:
                stores.start(made[name], result[name].at[seq])
        stores.wait_all()


def attend_back(seq, scalars, saved, fed, kv_memory, params, made, tokens, estimate=LONG, part=SEG):
    gain_attn, w_proj, w_out, gain_ffn, w_up, b_up, w_down, b_down = params
    seqs = saved["qkv"].shape[0]
    args = [
        saved["qkv"],
        kv_memory,
        fed["d_attended"],
        saved["attended"],
        saved["log_total"],
        w_proj,
        saved["x"],
        gain_attn,
        fed["d_residual"],
    ]
    specs = [ANY] * 7 + [whole(1, WIDTH), ANY]
    aliases = {}
    if made is not None:
        aliases = {len(scalars) + len(args) + i: 1 + i for i in range(len(MADE))}
        args += [made[name] for name, _, _ in MADE]
        specs += [ANY] * len(MADE)
    results = call(
        lambda *refs: attend_back_kernel(seq, part, len(aliases), *refs),
        "attend_back",
        scalars,
        args,
        [shape((part, WIDTH))] + [shape((seqs,) + dims, dtype) for _, dims, dtype in MADE],
        [pltpu.VMEM(dims, dtype) for _, dims, dtype in MADE]
        + [
            pltpu.VMEM((SEG, 3 * WIDTH), BF),
            pltpu.VMEM((CTX, 2 * WIDTH), BF),
            pltpu.VMEM((SEG, WIDTH), BF),
            pltpu.VMEM((SEG, WIDTH), BF),
            pltpu.VMEM((HEADS, 1, SEG), F32),
            pltpu.VMEM((3, WIDTH, WIDTH), BF),
            pltpu.VMEM((SEG, WIDTH), BF),
            pltpu.VMEM((SEG, WIDTH), F32),
            pltpu.VMEM((SEG, WIDTH), BF),
            pltpu.VMEM((SEG, SEG), F32),
            pltpu.VMEM((1, SEG), F32),
            pltpu.SemaphoreType.DMA((8,)),
            pltpu.SemaphoreType.DMA((WIDTH // (GROUP * HEAD), 7)),
            pltpu.SemaphoreType.DMA((8,)),
        ],
        tokens,
        aliases,
        estimate,
        specs,
    )
    return results[0], dict(zip([name for name, _, _ in MADE], results[1:]))


def project_back_kernel(seq, active, dq, dkx, dvx, w_proj, x, gain, d_residual, dx, grads, pool, xs, rows, dx_rows, sems):
    @pl.when(active[0] == 1)
    def _():
        copies = Copies(sems)
        place = pl.ds(SEG - HALF, HALF)
        for n, (ref, tile) in enumerate(zip((dq, dkx, dvx), tiles(w_proj, 1))):
            copies.start(ref.at[seq, place], grads.at[n], ("grad", n))
            copies.start(tile, pool.at[n], ("w", n))
        copies.start(x.at[seq, place], xs, "x")
        copies.start(d_residual.at[seq, place], rows, "rows")
        grad = None
        for n in range(3):
            copies.wait(("grad", n), ("w", n))
            term = nt(grads[n], pool[n])
            grad = term if grad is None else grad + term
        copies.wait_all()
        unit, inverse = normalise(xs[...].astype(F32))
        dx_rows[...] = (rows[...] + norm_back(unit, inverse, gain[...].astype(F32), grad)).astype(BF)
        copies.start(dx_rows, dx)
        copies.wait_all()


def project_back(seq, scalars, saved, fed, params, made, tokens):
    gain_attn, w_proj = params[:2]
    return call(
        lambda *refs: project_back_kernel(seq, *refs),
        "project_back",
        scalars,
        [made["dq"], made["dkx"], made["dvx"], w_proj, saved["x"], gain_attn, fed["d_residual"]],
        [shape((HALF, WIDTH))],
        [
            pltpu.VMEM((3, HALF, WIDTH), BF),
            pltpu.VMEM((3, WIDTH, WIDTH), BF),
            pltpu.VMEM((HALF, WIDTH), BF),
            pltpu.VMEM((HALF, WIDTH), F32),
            pltpu.VMEM((HALF, WIDTH), BF),
            pltpu.SemaphoreType.DMA((9,)),
        ],
        tokens,
        estimate=LONG,
        specs=[ANY] * 5 + [whole(1, WIDTH), ANY],
    )[0]


def compress_kernel(flags, grouped, w, bias, out, rows, weights, result, sems):
    copies = Copies(sems)
    copies.start(grouped, rows, "rows")
    copies.start(w, weights, "w")
    copies.wait("rows", "w")
    for s in range(rows.shape[0]):
        keep = (1 - flags[s]).astype(BF)
        result[s] = (nn(rows[s] * keep, weights[...]) + bias[...].astype(F32)).astype(BF)
        copies.start(result.at[s], out.at[s])
    copies.wait_all()


def compress(flags, memory, w_compress, b_compress, tokens):
    seqs = memory.shape[0]
    wide = RATE * WIDTH
    grouped = memory.reshape(seqs, COMP, wide)
    return list(
        call(
            compress_kernel,
            "compress",
            [flags],
            [grouped, w_compress.reshape(wide, WIDTH), b_compress],
            [shape((seqs, COMP, WIDTH))],
            [
                pltpu.VMEM((seqs, COMP, wide), BF),
                pltpu.VMEM((wide, WIDTH), BF),
                pltpu.VMEM((seqs, COMP, WIDTH), BF),
                pltpu.SemaphoreType.DMA((2 + seqs,)),
            ],
            tokens,
            estimate=SHORT,
            specs=[ANY, ANY, whole(1, WIDTH)],
        )
    )


WIDE = 512


def places_of(order, size):
    rest, place = order[1:], {}
    for index in range(size):
        place[index] = sum(((index >> b) & 1) << (len(rest) - 1 - n) for n, b in enumerate(rest))
    return place


class Either(list):
    def __init__(self, arrays, places):
        super().__init__((v, None) for v in arrays)
        self.places = places


def either_copies(group, refs, target, sems, base):
    made = []
    for wanted, places in enumerate(group.places):
        copies = []
        for n, (k, lead, row, column) in enumerate(places):
            source = refs[k] if lead is None else refs[k].at[lead]
            rows, columns = source.shape
            to = target.at[pl.ds(row, rows), pl.ds(column, columns)]
            copies.append(pltpu.make_async_copy(source, to, sems.at[base + n]))
        made.append((wanted, copies))
    return made


class Sides:
    def __init__(self, groups, tasks, ins, held, section, loads):
        self.groups, self.held, self.section, self.loads = groups, held, section, loads
        self.parts, self.either, self.ready, at = [], {}, set(), 0
        for g in groups:
            self.parts.append(ins[at : at + len(g)])
            at += len(g)
        for key in dict.fromkeys(k for t in tasks for k in (t["left"], t["right"])):
            g, tile = key
            if isinstance(groups[g], Either):
                choices = either_copies(groups[g], self.parts[g], held[g], loads.sems, loads.count)
                for wanted, copies in choices:
                    pl.when(section[0] == wanted)(lambda copies=copies: [c.start() for c in copies] and None)
                self.either[g] = choices
                loads.count += max(len(copies) for _, copies in choices)
                continue
            place, row = pl.ds(tile * 1024, 1024), 0
            for n, (ref, (_, lead)) in enumerate(zip(self.parts[g], groups[g])):
                rows = ref.shape[-2]
                source = ref.at[:, place] if lead is None else ref.at[lead, :, place]
                loads.start(source, held[g].at[pl.ds(row, rows), place], key + (n,))
                row += rows

    def wait(self, task):
        for key in (task["left"], task["right"]):
            if key in self.ready:
                continue
            self.ready.add(key)
            if key[0] in self.either:
                for wanted, copies in self.either[key[0]]:
                    pl.when(self.section[0] == wanted)(lambda copies=copies: [c.wait() for c in copies] and None)
            else:
                self.loads.wait(*[key + (m,) for m in range(len(self.parts[key[0]]))])

    def product(self, task, first, width):
        (left, lt), (right, rt) = task["left"], task["right"]
        return tn(
            self.held[left][:, lt * 1024 : (lt + 1) * 1024],
            self.held[right][:, rt * 1024 + first : rt * 1024 + first + width],
        )


def side_buffers(groups):
    made = []
    for g in groups:
        if isinstance(g, Either):
            made.append(pltpu.VMEM((SEG, WIDTH), BF))
        else:
            made.append(pltpu.VMEM((sum(v.shape[-2] for v, _ in g), g[0][0].shape[-1]), BF))
    return made, sum(len(g) * max(1, g[0][0].shape[-1] // 1024) for g in groups)


def early_kernel(groups, jobs, outs, section, *refs):
    total = sum(len(g) for g in groups)
    ins, refs = refs[:total], refs[total:]
    outs, refs = refs[:outs], refs[outs:]
    held, (staged, side_sems, out_sems) = refs[: len(groups)], refs[len(groups) :]
    parts, at = [], 0
    for g in groups:
        parts.append(ins[at : at + len(g)])
        at += len(g)
    first, used = {}, 0
    for g, group in enumerate(groups):
        first[g] = used
        used += len(group) * max(1, held[g].shape[1] // 1024)

    def place(t):
        return pl.ds(t * 1024 if isinstance(t, int) else pl.multiple_of(t * 1024, 1024), 1024)

    def side(g, t, act):
        if isinstance(groups[g], Either):
            for wanted, copies in either_copies(groups[g], parts[g], held[g], side_sems, first[g]):
                pl.when(section[0] == wanted)(lambda copies=copies: [act(c) for c in copies] and None)
            return
        row, many = 0, held[g].shape[1] // 1024
        for n, (ref, (_, lead)) in enumerate(zip(parts[g], groups[g])):
            rows = ref.shape[-2]
            sem = side_sems.at[first[g] + n * many + t]
            target = held[g].at[pl.ds(row, rows), place(t)]
            act(pltpu.make_async_copy(ref.at[lead, :, place(t)], target, sem))
            row += rows

    begin, end = (lambda copy: copy.start()), (lambda copy: copy.wait())
    done = set()
    for job in jobs:
        for key, loops in ((job["left"], job["loop"] == "left"), (job["right"], job["loop"] == "right")):
            if key in done:
                continue
            done.add(key)
            for t in range(job["count"]) if loops else [0]:
                side(key, t, begin)

    n, done = 0, set()
    for job in jobs:
        left, right, loop = job["left"], job["right"], job["loop"]
        for key, loops in ((left, loop == "left"), (right, loop == "right")):
            if not loops and key not in done:
                done.add(key)
                side(key, 0, end)

        def store(t, slot, job=job):
            row, column = job["at"]
            if loop == "left":
                row += t * 1024
            elif loop == "right":
                column += t * 1024
            if not isinstance(t, int):
                row, column = pl.multiple_of(row, 1024), pl.multiple_of(column, 1024)
            target = outs[job["out"]].at[pl.ds(row, 1024), pl.ds(column, 1024)]
            return pltpu.make_async_copy(staged.at[slot], target, out_sems.at[slot])

        def step(t, _, job=job, base=n):
            slot = (base + t) % 2
            if loop is not None:
                side(left if loop == "left" else right, t, end)
            lt, rt = (t if loop == "left" else 0), (t if loop == "right" else 0)

            @pl.when(base + t >= 2)
            def _():
                store(t, slot).wait()

            product = tn(held[left][:, place(lt)], held[right][:, place(rt)])
            staged[slot] = product.astype(BF)
            store(t, slot).start()
            return 0

        if job["count"] == 1:
            step(0, 0)
        else:
            lax.fori_loop(0, job["count"], step, 0)
        n += job["count"]
    for slot in range(2):
        pltpu.make_async_copy(staged.at[slot], outs[0].at[pl.ds(0, 1024), pl.ds(0, 1024)], out_sems.at[slot]).wait()


def early_grads(section, groups, jobs, outs, tokens):
    buffers, loads = side_buffers(groups)
    return list(
        call(
            lambda *refs: early_kernel(groups, jobs, len(outs), *refs),
            "early_grads",
            [section],
            [v for g in groups for v, _ in g],
            [shape(dims) for dims in outs],
            buffers
            + [
                pltpu.VMEM((2, 1024, 1024), BF),
                pltpu.SemaphoreType.DMA((loads,)),
                pltpu.SemaphoreType.DMA((2,)),
            ],
            tokens,
            estimate=SHORT,
        )
    )


def unset(dims, tokens):
    def kernel(*refs):
        pass

    return list(call(kernel, "unset", [], [], [shape(d) for d in dims], [], tokens, estimate=SHORT))


def weight_kernel(size, groups, tasks, chunks, places, small_chunk, bases, section, mine, *refs):
    total = sum(len(g) for g in groups)
    ins, base, refs = refs[:total], refs[total : total + 2 * bases], refs[total + 2 * bases :]
    if small_chunk is not None:
        small, refs = refs[0], refs[1:]
    sends, refs = refs[: len(chunks)], refs[len(chunks) :]
    keeps, refs = refs[: len(chunks)], refs[len(chunks) :]
    held, refs = refs[: len(groups)], refs[len(groups) :]
    staged, small_rows, so_far, in_sems, out_sems, base_sems = refs
    loads, stores = Copies(in_sems), Copies(out_sems)
    even = (mine[0] & 1) == 0
    sides = Sides(groups, tasks, ins, held, section, loads)

    def base_copy(n, which=0):
        k, row, column = tasks[n]["base"]
        source = base[k + which * bases].at[pl.ds(row, 1024), pl.ds(column, 1024)]
        return pltpu.make_async_copy(source, so_far.at[n % 2], base_sems.at[n % 2])

    def begin_base(n):
        for which in range(2):
            pl.when(section[0] == which)(lambda which=which: base_copy(n, which).start())

    begin_base(0)
    if small_chunk is not None:
        for pair in range(size // 2):
            place = places[small_chunk][2 * pair]
            one, two = small[2 * pair], small[2 * pair + 1]
            small_rows[0, place] = jnp.where(even, two, one)
            small_rows[1, place] = jnp.where(even, one, two)
        for i, target in enumerate((sends, keeps)):
            rows = target[small_chunk].shape[1] - 16
            stores.start(
                small_rows.at[i], target[small_chunk].at[:, pl.ds(rows, 16), pl.ds(0, WIDTH)], ("small", i)
            )

    busy = {}
    for n, task in enumerate(tasks):
        slot = n % 2
        sides.wait(task)
        for name in busy.pop(slot, ()):
            stores.wait(name)
        base_copy(n).wait()
        if n + 1 < len(tasks):
            begin_base(n + 1)
        count = size // task["blocks"]
        rows = 1024 // count
        for cut in range(1024 // WIDE):
            c = slice(cut * WIDE, (cut + 1) * WIDE)
            value = (sides.product(task, cut * WIDE, WIDE) + so_far[slot, :, c].astype(F32)).astype(BF)
            for pair in range(count // 2):
                one = value[(2 * pair) * rows : (2 * pair + 1) * rows]
                two = value[(2 * pair + 1) * rows : (2 * pair + 2) * rows]
                staged[slot, 0, pair, :, c] = jnp.where(even, two, one)
                staged[slot, 1, pair, :, c] = jnp.where(even, one, two)
        names = []
        for k, first, width, start in task["outs"]:
            for i, target in enumerate((sends, keeps)):
                for pair in range(count // 2):
                    names.append((n, k, i, pair))
                    stores.start(
                        staged.at[slot, i, pair, :, pl.ds(first, width)],
                        target[k].at[places[k][task["block"] * count + 2 * pair], pl.ds(0, rows), pl.ds(start, width)],
                        names[-1],
                    )
        busy[slot] = names
    stores.wait_all()


def weight_grads(
    section, mine, size, groups, bases, tasks, chunks, tokens, places, small=None, small_chunk=None, estimate=LONG
):
    outs = []
    for k, (blocks, columns) in enumerate(chunks):
        rows = blocks * 1024 // size + (16 if k == small_chunk else 0)
        outs.append(shape((size // 2, rows, columns)))
    args = [v for g in groups for v, _ in g] + [v for side in zip(*bases) for v in side]
    args += [small] if small is not None else []
    specs = [ANY] * (sum(len(g) for g in groups) + 2 * len(bases)) + ([whole(*small.shape)] if small is not None else [])
    count = size // tasks[0]["blocks"]
    buffers, loads = side_buffers(groups)
    results = call(
        lambda *refs: weight_kernel(size, groups, tasks, chunks, places, small_chunk, len(bases), *refs),
        "weight_grads",
        [section, mine],
        args,
        outs + outs,
        buffers
        + [
            pltpu.VMEM((2, 2, count // 2, 1024 // count, 1024), BF),
            pltpu.VMEM((2, size // 2, 16, WIDTH), BF),
            pltpu.VMEM((2, 1024, 1024), BF),
            pltpu.SemaphoreType.DMA((loads,)),
            pltpu.SemaphoreType.DMA((2 + sum(count * len(t["outs"]) for t in tasks),)),
            pltpu.SemaphoreType.DMA((2,)),
        ],
        tokens,
        estimate=estimate,
        specs=specs,
    )
    return list(zip(results[: len(chunks)], results[len(chunks) :]))


def halve_kernel(levels, mine, *refs):
    total = len(levels)
    kept, got, refs = refs[:total], refs[total : 2 * total], refs[2 * total :]
    outs = []
    for level in levels:
        outs.append(refs[: 1 if level is None else 2])
        refs = refs[len(outs[-1]) :]
    held, came, refs = refs[:total], refs[total : 2 * total], refs[2 * total :]
    wide, refs = refs[:-2], refs[-2:]
    loads, stores = Copies(refs[0]), Copies(refs[1])
    wide = list(wide)
    for n, level in enumerate(levels):
        if level is None:
            loads.start(kept[n], held[n], (n, 0, 0))
            loads.start(got[n], came[n], (n, 0, 1))
            continue
        half = kept[n].shape[0] // 2
        bit = (mine[0] >> level) & 1
        for j, which in enumerate((1 - bit, bit)):
            place = pl.ds(which * half, half)
            loads.start(kept[n].at[place], held[n].at[j], (n, j, 0))
            loads.start(got[n].at[place], came[n].at[j], (n, j, 1))
    for n, level in enumerate(levels):
        if level is None:
            total_rows = wide.pop(0)
            loads.wait((n, 0, 0), (n, 0, 1))
            total_rows[...] = held[n][0].astype(F32) + came[n][0].astype(F32)
            stores.start(total_rows, outs[n][0])
            continue
        for j, target in enumerate(outs[n]):
            loads.wait((n, j, 0), (n, j, 1))
            held[n][j] = held[n][j] + came[n][j]
            stores.start(held[n].at[j], target)
    stores.wait_all()


def halve(mine, levels, kept, got, tokens, estimate):
    total = len(kept)
    outs, held, wide = [], [], []
    for level, v in zip(levels, kept):
        if level is None:
            outs.append(shape(v.shape[1:], F32))
            wide.append(pltpu.VMEM(v.shape[1:], F32))
            held.append(pltpu.VMEM(v.shape, BF))
        else:
            half = (v.shape[0] // 2,) + v.shape[1:]
            outs += [shape(half)] * 2
            held.append(pltpu.VMEM((2,) + half, BF))
    results = call(
        lambda *refs: halve_kernel(levels, *refs),
        "halve",
        [mine],
        [*kept, *got],
        outs,
        held
        + held
        + wide
        + [pltpu.SemaphoreType.DMA((4 * total,)), pltpu.SemaphoreType.DMA((2 * total,))],
        tokens,
        estimate=estimate,
    )
    results, made = list(results), []
    for level in levels:
        made.append([results.pop(0) for _ in range(1 if level is None else 2)])
    return made


def gather_kernel(targets, ready, small, mine, *refs):
    total = len(targets)
    late = [n for n in range(total) if not ready[n]]
    kept, refs = refs[:total], refs[total:]
    got, refs = dict(zip(late, refs)), refs[len(late) :]
    (w_proj, w_up, gain_attn, gain_ffn), outs, refs = refs[:4], refs[4:12], refs[12:]
    held, refs = dict(zip(late, refs)), refs[len(late) :]
    came, refs = dict(zip(late, refs)), refs[len(late) :]
    sums, (small_rows, b_up, b_down, proj_rows, up_rows, gains), (in_sems, out_sems) = refs[:4], refs[4:10], refs[10:]
    loads, stores = Copies(in_sems), Copies(out_sems)
    rows = proj_rows.shape[0]
    for n, (k, first) in enumerate(targets):
        if ready[n]:
            place = sums[k].at[:, pl.ds(first, kept[n].shape[1])]
            if n == small:
                loads.start(kept[n].at[pl.ds(0, rows)], place, ("sum", n))
                loads.start(kept[n].at[pl.ds(rows, 16), pl.ds(0, WIDTH)], small_rows, "small")
            else:
                loads.start(kept[n], place, ("sum", n))
        else:
            loads.start(kept[n].at[0], held[n], ("kept", n))
            loads.start(got[n].at[0], came[n], ("got", n))
    own = pl.ds(pl.multiple_of(mine[0] * rows, rows), rows)
    loads.start(w_proj.at[own], proj_rows, "proj")
    loads.start(w_up.at[own], up_rows, "up")
    for n, (k, first) in enumerate(targets):
        if ready[n]:
            loads.wait(("sum", n))
            continue
        loads.wait(("kept", n), ("got", n))
        value = held[n][...].astype(F32) + came[n][...].astype(F32)
        sums[k][:, first : first + value.shape[1]] = value
    for k in range(4):
        stores.start(sums[k], outs[k])
    loads.wait("small")
    b_up[...] = small_rows[:1, : b_up.shape[1]]
    b_down[...] = small_rows[:1, b_up.shape[1] : b_up.shape[1] + rows]
    stores.start(b_up, outs[4])
    stores.start(b_down, outs[5])
    loads.wait("proj", "up")
    for n, (weight, grad, gain) in enumerate(((proj_rows, sums[3], gain_attn), (up_rows, sums[1], gain_ffn))):
        along = jnp.sum(weight[...].astype(F32) * grad[...], axis=1, keepdims=True)
        turned = jnp.broadcast_to(along, (rows, 128)).T
        gains[n] = turned[:1, :rows] / gain[...]
        stores.start(gains.at[n], outs[6 + n])
    stores.wait_all()


def gather_up(mine, targets, kept, got, small, w_proj, w_up, own_gain, size, tokens):
    rows = WIDTH // size
    widths = [(FF // size, WIDTH), (rows, FF), (rows, WIDTH), (rows, 3 * WIDTH)]
    outs = [shape(w, F32) for w in widths]
    outs += [shape((1, n), F32) for n in (FF // size, rows, rows, rows)]
    late = [v for v, g in zip(kept, got) if g is not None]
    pieces = [pltpu.VMEM(v.shape[1:], BF) for v in late]
    ready = [g is None for g in got]
    arrived = [g for g in got if g is not None]
    return call(
        lambda *refs: gather_kernel(targets, ready, small, *refs),
        "gather_up",
        [mine],
        [*kept, *arrived, w_proj, w_up, *own_gain],
        outs,
        pieces
        + pieces
        + [pltpu.VMEM(w, F32) for w in widths]
        + [
            pltpu.VMEM((16, WIDTH), F32),
            pltpu.VMEM((1, FF // size), F32),
            pltpu.VMEM((1, rows), F32),
            pltpu.VMEM((rows, 3 * WIDTH), BF),
            pltpu.VMEM((rows, FF), BF),
            pltpu.VMEM((2, 1, rows), F32),
            pltpu.SemaphoreType.DMA((2 * len(kept) + 3,)),
            pltpu.SemaphoreType.DMA((8,)),
        ],
        tokens,
        estimate=SHORT,
        specs=[ANY] * (len(kept) + len(late) + 2) + [whole(1, rows)] * 2,
    )


def pick_kernel(section, first, second, out, held, sems):
    for wanted, source in enumerate((first, second)):

        @pl.when(section[0] == wanted)
        def _(source=source):
            copies = Copies(sems)
            for s in range(held.shape[0]):
                copies.start(source.at[s], held.at[s], ("in", s))
            for s in range(held.shape[0]):
                copies.wait(("in", s))
                copies.start(held.at[s], out.at[s])
            copies.wait_all()


def pick(section, first, second, tokens):
    return call(
        pick_kernel,
        "pick",
        [section],
        [first, second],
        [shape(first.shape)],
        [pltpu.VMEM(first.shape, BF), pltpu.SemaphoreType.DMA((2 * first.shape[0],))],
        tokens,
        estimate=SHORT,
    )[0]


def swap_bit(value, size, bit):
    return lax.ppermute(value, "dp", [(i, i ^ (1 << bit)) for i in range(size)])


def one_way(value, first, second):
    return lax.ppermute(value, "section", [(first, second)])


def both_after(first, second):
    return lax.optimization_barrier((first, second))


def body(
    inputs,
    cotangent,
    memory,
    compressed,
    reset_flags,
    boundary,
    gain_attn,
    projection_weight,
    w_output,
    gain_ffn,
    w_up,
    b_up,
    w_down,
    b_down,
    w_compress,
    b_compress,
):
    section = lax.axis_index("section")
    is_first = section == 0
    size = lax.axis_size("dp")
    mine = lax.axis_index("dp")
    levels = (size - 1).bit_length()
    at_section, at_dp = section.astype(jnp.int32).reshape(1), mine.astype(jnp.int32).reshape(1)
    active = (1 - at_section, at_section)
    seqs, _, width = inputs.shape
    memory, compressed = memory[0], compressed[0]
    w_proj, w_out, w_up, w_down = projection_weight[0], w_output[0], w_up[0], w_down[0]
    params = (gain_attn, w_proj, w_out, gain_ffn, w_up, b_up, w_down, b_down)
    last = [[]]

    other_x = [one_way(inputs[0], 1, 0)]
    normed_memory, kv_memory = [], []

    def keyvals(s):
        normed, kv = memory_keyvals(s, reset_flags, compressed, memory, gain_attn, w_proj, last[0])
        last[0] = [kv]
        normed_memory.append(normed)
        kv_memory.append(kv)

    keyvals(0)
    kv_memory[0], inputs_later = both_after(kv_memory[0], inputs)
    other_x.append(one_way(inputs_later[1], 1, 0))

    def ahead(layer, s, xs, saved, estimate):
        scalars = [active[layer], reset_flags, boundary]
        y, saved = forward(s, seqs, scalars, xs, kv_memory[s], params, saved, last[0], estimate)
        last[0] = [y]
        return y, saved

    y_a0, saved = ahead(0, 0, ((inputs, 0), (other_x[0], None)), None, LONG)
    hop_a = one_way(y_a0, 0, 1)
    keyvals(1)
    y_b0, saved = ahead(0, 1, ((inputs, 1), (other_x[1], None)), saved, SHORT)
    y_b0, cotangent_later = both_after(y_b0, cotangent)
    hop_b = one_way(y_b0, 0, 1)
    other_gy = [one_way(cotangent_later[s], 0, 1) for s in range(seqs)]

    def squeeze_now(tokens):
        return compress(reset_flags, memory, w_compress[0], b_compress, tokens)

    tokens = last[0]
    (squeezed_first,) = lax.cond(
        is_first, lambda: squeeze_now(tokens), lambda: unset([(seqs, COMP, WIDTH)], tokens)
    )
    last[0] = [squeezed_first]

    def back(layer, s, gys, fed, made, estimate, part=SEG):
        fed = feed_back(s, [active[layer]], gys, saved, params, fed, last[0], estimate)
        scalars = [active[layer], reset_flags, boundary]
        dx, made = attend_back(s, scalars, saved, fed, kv_memory[s], params, made, [], SHORT, part)
        last[0] = [dx]
        return dx, fed, made

    y_a1, saved = ahead(1, 0, ((hop_a, None),), saved, SHORT)
    dx_a1, fed, made = back(1, 0, ((other_gy[0], None, 0, 0), (cotangent, 0, 0, width)), None, None, SHORT)
    back_a = one_way(dx_a1, 1, 0)
    y_b1, saved = ahead(1, 1, ((hop_b, None),), saved, SHORT)
    other_y = one_way(saved["y_low"], 1, 0)
    dx_b1, fed, made = back(1, 1, ((other_gy[1], None, 0, 0), (cotangent, 1, 0, width)), fed, made, SHORT, HALF)
    rest = project_back(1, [active[1]], saved, fed, params, made, [dx_b1, back_a])
    back_b = [one_way(dx_b1, 1, 0), one_way(rest, 1, 0)]
    last[0] = [rest]
    dx_a0, fed, made = back(0, 0, ((back_a, None, 0, 0),), fed, made, SHORT)

    def gy_of(s, arrived):
        count = len(arrived)
        first = [(n, None, n * (SEG // count), 0) for n in range(count)]
        second = [(count, None, 0, 0), (count + 1, s, 0, WIDTH // 2)]
        return Either([*arrived, other_gy[s], cotangent], (first, second))

    tall = FF // WIDTH
    kinds = lambda: dict(
        down=(
            [[(saved["hidden"], 0)], gy_of(0, [back_a])],
            [dict(left=0, right=1, loop="left", count=tall, out=0, at=(0, 0))],
            [(FF, WIDTH)],
        ),
        up=(
            [[(saved["ffn_in"], 0)], [(fed["d_hidden"], 0)], [(saved["attended"], 0)], [(fed["low"], 0)]],
            [
                dict(left=0, right=1, loop="right", count=tall, out=0, at=(0, 0)),
                dict(left=2, right=3, loop=None, count=1, out=1, at=(0, 0)),
            ],
            [(WIDTH, FF), (WIDTH, WIDTH)],
        ),
        proj=(
            [
                [(saved["normed"], 0), (normed_memory[0], 0)],
                [(made["dkx"], 0), (made["dkm"], 0)],
                [(made["dvx"], 0), (made["dvm"], 0)],
                [(saved["normed"], 0)],
                [(made["dq"], 0)],
            ],
            [
                dict(left=0, right=1, loop=None, count=1, out=0, at=(0, WIDTH)),
                dict(left=0, right=2, loop=None, count=1, out=0, at=(0, 2 * WIDTH)),
                dict(left=3, right=4, loop=None, count=1, out=0, at=(0, 0)),
            ],
            [(WIDTH, 3 * WIDTH)],
        ),
    )

    def early(tokens, *which):
        groups, jobs, outs = [], [], []
        for kind in which:
            more, jobs_more, outs_more = kinds()[kind]
            for job in jobs_more:
                jobs.append(
                    dict(
                        job,
                        left=job["left"] + len(groups),
                        right=job["right"] + len(groups),
                        out=job["out"] + len(outs),
                    )
                )
            groups, outs = groups + more, outs + outs_more
        return early_grads(at_section, groups, jobs, outs, tokens)

    sizes = {kind: value[2] for kind, value in kinds().items()}
    tokens = last[0]
    base_down, up_first, out_first, proj_first = lax.cond(
        is_first,
        lambda: early(tokens, "down", "up", "proj"),
        lambda: early(tokens, "down") + unset(sizes["up"] + sizes["proj"], tokens),
    )
    last[0] = [base_down]

    def early_second(kind, more=None, dims=()):
        tokens = last[0]
        made_late = lax.cond(
            is_first,
            lambda: unset(sizes[kind] + list(dims), tokens),
            lambda: early(tokens, kind) + (more(tokens) if more else []),
        )
        last[0] = [made_late[0]]
        return made_late

    moving, done = {}, {}
    orders = {name: (0, *range(2, levels), 1) for name in ("up0",)}

    def send_on(name, send, keep, step):
        order = orders.get(name, tuple(range(levels)))
        moving[name] = (swap_bit(send, size, order[step]), keep, step)

    def halved(*names, estimate=SHORT):
        names = [name for name in names if name in moving]
        if not names:
            return
        which = []
        for name in names:
            step = moving[name][2] + 1
            which.append(None if step == levels else orders.get(name, tuple(range(levels)))[step])
        kept, got = [moving[name][1] for name in names], [moving[name][0] for name in names]
        made = halve(at_dp, which, kept, got, last[0], estimate)
        last[0] = [made[0][0]]
        for name, level, values in zip(names, which, made):
            if level is None:
                done[name] = values[0]
                moving.pop(name)
            else:
                send_on(name, *values, moving[name][2] + 1)

    def grads(names, groups, bases, tasks, chunks, **more):
        places = [places_of(orders.get(name, tuple(range(levels))), size) for name in names]
        made = weight_grads(at_section, at_dp, size, groups, bases, tasks, chunks, last[0], places, **more)
        last[0] = [made[0][0]]
        for name, (send, keep) in zip(names, made):
            send_on(name, send, keep, 0)

    eighth = WIDTH // 8
    grads(
        ("down0", "down1", "down2"),
        [[(saved["hidden"], 1)], gy_of(1, back_b)],
        [(base_down, base_down)],
        [
            dict(
                left=(0, t),
                right=(1, 0),
                base=(0, t * WIDTH, 0),
                block=t,
                blocks=FF // WIDTH,
                outs=[(0, 0, 3 * eighth, 0), (1, 3 * eighth, 2 * eighth, 0), (2, 5 * eighth, 3 * eighth, 0)],
            )
            for t in range(FF // WIDTH)
        ],
        [(FF // WIDTH, 3 * eighth), (FF // WIDTH, 2 * eighth), (FF // WIDTH, 3 * eighth)],
    )
    halved("down0")
    halved("down1", "down2")
    fed = feed_back(1, [active[0]], [(part, None, n * HALF, 0) for n, part in enumerate(back_b)], saved, params, fed, last[0])
    last[0] = [fed["d_down"]]
    up_second, out_second = early_second("up")
    halved("down0")

    up = jnp.sum(fed["d_up"], axis=(0, 1)).reshape(size, FF // size)
    down = jnp.sum(fed["d_down"], axis=(0, 1)).reshape(size, WIDTH // size)
    row = jnp.concatenate([up, down], axis=1).astype(BF)
    small = jnp.pad(row[:, None, :], ((0, 0), (0, 15), (0, WIDTH - row.shape[1])))
    grads(
        ("up0", "up1", "out"),
        [[(saved["ffn_in"], 1)], [(fed["d_hidden"], 1)], [(saved["attended"], 1)], [(fed["low"], 1)]],
        [(up_first, up_second), (out_first, out_second)],
        [
            dict(
                left=(0, 0),
                right=(1, t),
                base=(0, 0, t * WIDTH),
                block=0,
                blocks=1,
                outs=[(t // 2, 0, WIDTH, (t % 2) * WIDTH)],
            )
            for t in range(tall)
        ]
        + [dict(left=(2, 0), right=(3, 0), base=(1, 0, 0), block=0, blocks=1, outs=[(2, 0, WIDTH, 0)])],
        [(1, 2 * WIDTH), (1, 2 * WIDTH), (1, WIDTH)],
        small=small,
        small_chunk=1,
        estimate=SHORT,
    )
    halved("down1", "down2", "down0", estimate=LONG)
    halved("up1")
    halved("up0", "out")
    dx_b0, made = attend_back(
        1, [active[0], reset_flags, boundary], saved, fed, kv_memory[1], params, made, last[0]
    )
    last[0] = [dx_b0]
    proj_second, squeezed_second = early_second("proj", squeeze_now, [(seqs, COMP, WIDTH)])
    outputs = pick(at_section, other_y, saved["y_high"], last[0])
    last[0] = [outputs]
    halved("up1", "up0", "down1", "down2", "down0")
    grads(
        ("key", "value", "query"),
        [
            [(saved["normed"], 1), (normed_memory[1], 0)],
            [(made["dkx"], 1), (made["dkm"], 1)],
            [(made["dvx"], 1), (made["dvm"], 1)],
            [(saved["normed"], 1)],
            [(made["dq"], 1)],
        ],
        [(proj_first, proj_second)],
        [
            dict(left=(0, 0), right=(1, 0), base=(0, 0, WIDTH), block=0, blocks=1, outs=[(0, 0, WIDTH, 0)]),
            dict(left=(0, 0), right=(2, 0), base=(0, 0, 2 * WIDTH), block=0, blocks=1, outs=[(1, 0, WIDTH, 0)]),
            dict(left=(3, 0), right=(4, 0), base=(0, 0, 0), block=0, blocks=1, outs=[(2, 0, WIDTH, 0)]),
        ],
        [(1, WIDTH)] * 3,
        estimate=SHORT,
    )
    halved("out", "up1", "up0", estimate=LONG)
    halved("key", "value", "query")
    leaving, token = both_after(made["dx_high"], last[0][0])
    last[0] = [token]
    halved("up0", "down1", "down2", estimate=LONG)
    halved("key", "up1", "out")
    halved("value", "key")
    grad_inputs = pick(at_section, made["dx_low"], one_way(leaving, 0, 1), last[0])
    last[0] = [grad_inputs]
    halved("query", "value", "out")
    halved("query", "key")
    while any(step + 1 < levels for _, _, step in moving.values()):
        halved(*[name for name, (_, _, step) in moving.items() if step + 1 < levels])
    if "up1" in moving:
        halved("up1")
    rows = WIDTH // size
    own_gain = [
        lax.dynamic_slice_in_dim(gain, mine * rows, rows, 1).astype(F32) for gain in (gain_attn, gain_ffn)
    ]
    targets = dict(
        down0=(0, 0), down1=(0, 3 * eighth), down2=(0, 5 * eighth), up0=(1, 0), up1=(1, 2 * WIDTH), out=(2, 0),
        query=(3, 0), key=(3, WIDTH), value=(3, 2 * WIDTH),
    )
    names = list(targets)
    g_down, g_up, g_out, g_proj, g_b_up, g_b_down, g_gain_attn, g_gain_ffn = gather_up(
        at_dp,
        [targets[name] for name in names],
        [done[name] if name in done else moving[name][1] for name in names],
        [None if name in done else moving[name][0] for name in names],
        names.index("up1"),
        w_proj,
        w_up,
        own_gain,
        size,
        last[0],
    )
    keep_all = (1 - reset_flags).astype(BF)[:, None, None]
    squeezed = jnp.where(is_first, squeezed_first, squeezed_second)
    new_compressed = jnp.concatenate([compressed[:, COMP:] * keep_all, squeezed], axis=1)
    return (
        outputs,
        grad_inputs,
        saved["x"][None],
        new_compressed[None],
        g_gain_attn,
        g_proj[None],
        g_out[None],
        g_gain_ffn,
        g_up[None],
        g_b_up,
        g_down[None],
        g_b_down,
    )


def solution(mesh):
    return jax.shard_map(
        body,
        mesh=mesh,
        in_specs=(
            P("dp", None, "section"),
            P("dp", None, "section"),
            P("section", "dp", None, None),
            P("section", "dp", None, None),
            P("dp"),
            P("dp"),
            P("section", None),
            P("section", None, None),
            P("section", None, None),
            P("section", None),
            P("section", None, None),
            P("section", None),
            P("section", None, None),
            P("section", None),
            P("section", None, None, None),
            P("section", None),
        ),
        out_specs=(
            P("dp", None, "section"),
            P("dp", None, "section"),
            P("section", "dp", None, None),
            P("section", "dp", None, None),
            P("section", "dp"),
            P("section", "dp", None),
            P("section", "dp", None),
            P("section", "dp"),
            P("section", "dp", None),
            P("section", "dp"),
            P("section", "dp", None),
            P("section", "dp"),
        ),
        check_vma=False,
    )
```
